32 devices in a mesh: seq: 8 (over z, y), hx: 4 (over x, core).
Axes of the slice: x: 2, y: 2, z: 4, core: 2. Of those that a mesh axis runs over, the one named last changes fastest.
Arguments:
- queries: bfloat16 [1024, 4096], P('seq', 'hx'), may hold values from -6 to 6
- keys: bfloat16 [1024, 4096], P('seq', 'hx'), may hold values from -6 to 6
- values: bfloat16 [1024, 4096], P('seq', 'hx'), may hold values from -6 to 6
- log_decay: float32 [1024, 32], P('seq', 'hx'), may hold values from -1 to 0
- doc_ids: int32 [1024], P('seq'), may hold values from 0 to 3, as said below
- residual: bfloat16 [1024, 6144], P('seq'), may hold values from -6 to 6
- out_weight: bfloat16 [4096, 6144], P('hx'), may hold values from -0.09375 to 0.09375
- norm_gain: float32 [6144], replicated, may hold values from 0.1 to 1.9
- expert_ids: int32 [1024, 2], P('seq'), may hold values from 0 to 3, all different within a row; in each aligned block of 128 rows (0 to 127, 128 to 255, ...) at most 80 rows name the same one
- route_weight: float32 [1024, 2], P('seq'), may hold values from 0.2 to 1
- w_gate: bfloat16 [4, 6144, 4608], P('hx', None, 'seq'), may hold values from -0.078125 to 0.078125
- w_up: bfloat16 [4, 6144, 4608], P('hx', None, 'seq'), may hold values from -0.078125 to 0.078125
- w_down: bfloat16 [4, 4608, 6144], P('hx', 'seq'), may hold values from -0.09375 to 0.09375
Outputs:
- layer_out: bfloat16 [1024, 6144], P('seq', 'hx')
The draws below stay inside these ranges and needn't reach their ends.
Inputs may be any that keep to these rules, and one draw needn't show every extreme that they name: `expert_ids`: the two experts of a token differ; among the tokens of one sequence shard no expert is named more than 80 times, and some expert reaches 80. `doc_ids`: document numbers start at 0, never fall along the sequence, and rise by one at each of three positions.
All inputs are finite; a program needn't handle non-finite values.
Results may differ from the reference program's by a relative error of at most 0.022.
Values may be sent and summed in bfloat16 or wider, within the bound.
No kernel may reach another device: no remote copies, remote signals or barrier semaphores. Data moves between devices by JAX's collectives and lax.ppermute only.
A program may use at most 128 MiB of HBM per device.

```python
import math
import jax
import jax.numpy as jnp
import numpy as np
from jax import lax

D = 6144
ATTN_GROUPS = 32
HS = 128
FF = 4608
TOK_DEV = 128
SPAN_LENGTH = 1024
EXPERTS = 4
CAP = 80
N_SEQ = 8


def draw_log_decay(key, part):
    key = jax.random.fold_in(key, 7)
    complete_lookup_vectors = jax.random.split(key, 6)
    fast_share = 0.5
    fast_heads = jax.random.uniform(complete_lookup_vectors[0], (ATTN_GROUPS,)) < fast_share
    fast_rate = jnp.exp(jax.random.uniform(complete_lookup_vectors[1], (ATTN_GROUPS,), minval=jnp.log(1.0 / 50.0), maxval=jnp.log(1.0 / 30.0)))
    slow_rate = jnp.exp(jax.random.uniform(complete_lookup_vectors[2], (ATTN_GROUPS,), minval=jnp.log(0.05), maxval=jnp.log(0.25))) * 2.3 / SPAN_LENGTH
    reference_forget_factor = jnp.where(fast_heads, fast_rate, slow_rate)
    noise_perturbation = jnp.exp(jax.random.uniform(complete_lookup_vectors[3], (SPAN_LENGTH, ATTN_GROUPS), minval=jnp.log(0.5), maxval=jnp.log(2.0)))
    segment_spans = jax.random.uniform(complete_lookup_vectors[4], (SPAN_LENGTH, ATTN_GROUPS)) < 2.0 / SPAN_LENGTH
    stack_level = jax.random.uniform(complete_lookup_vectors[5], (SPAN_LENGTH, ATTN_GROUPS), minval=0.22, maxval=0.69)
    closing_result_matrix = -(reference_forget_factor[None, :] * noise_perturbation + jnp.where(segment_spans, stack_level, 0.0))
    return closing_result_matrix.astype(jnp.float32)


def draw_doc_ids(key, part):
    key = jax.random.fold_in(key, 11)
    shuffled = jax.random.permutation(key, SPAN_LENGTH - 1)
    cut_points = shuffled[:3].astype(jnp.int32) + 1
    positions = jnp.arange(SPAN_LENGTH, dtype=jnp.int32)
    return jnp.sum((positions[:, None] >= cut_points[None, :]).astype(jnp.int32), axis=1).astype(jnp.int32)


def block_scale(own_key, shape, pieces, low, high):
    gain, own = 1.0, jax.random.fold_in(own_key, 6)
    for dim, shards_of in pieces:
        steps = jnp.exp(jax.random.uniform(jax.random.fold_in(own, dim), (shards_of,), jnp.float32, low / len(pieces), high / len(pieces)))
        gain = gain * jnp.repeat(steps, shape[dim] // shards_of).reshape([-1 if axis == dim else 1 for axis in range(len(shape))])
    return gain


def deal_out(rng, own, number, rows, number_of, top, reach, skew):
    order = jax.random.permutation(rng, number_of)
    packed, ordinary = portions_of(number_of, rows * top, reach, skew, True), portions_of(number_of, rows * top, reach, skew, False)
    places = jnp.arange(number_of)

    def named(sizes, rotation):
        used = int((sizes > 0).sum())
        fixed = max(1, used // 4)
        passed = fixed + (places - fixed + rotation * (used - fixed)) % max(1, number_of - fixed)
        return jnp.zeros((number_of,), jnp.int32).at[order[jnp.where(places < fixed, places, passed)]].set(jnp.asarray(sizes, jnp.int32))

    sizes = jnp.where(number % 4 == 0, named(packed, number // 4), named(ordinary, number - number // 4 - 1))
    mixed = jax.random.permutation(jax.random.fold_in(own, 3), number_of)
    giver, sink = mixed[0:number_of // 2 * 2:2], mixed[1:number_of // 2 * 2:2]
    slack = jnp.minimum(sizes[giver] - 1, reach - sizes[sink]) // 2
    slack = jnp.where((giver == order[0]) | (sink == order[0]) | (sizes[sink] == 0), 0, jnp.maximum(slack, 0))
    passed = jax.random.randint(jax.random.fold_in(own, 4), (number_of // 2,), 0, 1 << 20) % (slack + 1)
    sizes = sizes.at[giver].add(-passed).at[sink].add(passed)
    members = jnp.searchsorted(jnp.cumsum(sizes), jnp.arange(rows * top), side="right").astype(jnp.int32)
    listing = members.reshape(top, rows).T
    listing = listing[jax.random.permutation(jax.random.fold_in(own, 1), rows)]
    rotation = jax.random.randint(jax.random.fold_in(own, 2), (rows, 1), 0, top)
    return jnp.take_along_axis(listing, (jnp.arange(top)[None, :] + rotation) % top, axis=1)


def portions_of(count, total, bound, lean, full):
    weights = [(1 << 20) // math.isqrt(grade ** lean) + 1 for grade in range(1, count + 1)]
    largest = bound if full else min(bound, max(-(-total // count), total * weights[0] // sum(weights)))
    least = 1 if total - largest >= count - 1 else 0
    counts, rest = [largest] + [least] * (count - 1), total - largest - least * (count - 1)
    while rest > 0:
        candidates = [i for i in range(1, count) if counts[i] < largest] or [i for i in range(1, count) if counts[i] < bound]
        pool, budget = sum([weights[i] for i in candidates]), rest
        for i in candidates:
            more = min(bound - counts[i], max(1, budget * weights[i] // pool), rest)
            counts[i] = counts[i] + more
            rest = rest - more
    return np.array(counts)


def normal_values(own_key, dims, spread, most, pieces=(), kind=jnp.bfloat16):
    factor_of = block_scale(own_key, dims, pieces, -0.22, 0.18) if pieces else 1.0
    drawn = jax.random.normal(own_key, dims, jnp.float32) * spread * factor_of
    return jnp.minimum(jnp.maximum(drawn, -most), most).astype(kind)


def setup_inputs(seed: int = 0) -> dict:
    streams_of = jax.random.split(jax.random.key(seed), 14)
    queries = normal_values(streams_of[0], (SPAN_LENGTH, ATTN_GROUPS * HS), 1.0, 6.0, ((0, 8), (1, 4)))
    keys = normal_values(streams_of[1], (SPAN_LENGTH, ATTN_GROUPS * HS), 1.0, 6.0, ((0, 8), (1, 4)))
    values = normal_values(streams_of[2], (SPAN_LENGTH, ATTN_GROUPS * HS), 1.0, 6.0, ((0, 8), (1, 4)))
    log_decay = draw_log_decay(jax.random.fold_in(streams_of[13], 71), 0)
    doc_ids = draw_doc_ids(jax.random.fold_in(streams_of[13], 71), 0)
    residual = normal_values(streams_of[5], (SPAN_LENGTH, D), 1.0, 6.0, ((0, 8),))
    out_weight = normal_values(streams_of[6], (ATTN_GROUPS * HS, D), (ATTN_GROUPS * HS) ** -0.5, 0.09375, ((0, 4),))
    norm_gain = jnp.clip(1.0 + 0.18 * jax.random.normal(streams_of[7], (D,), jnp.float32), 0.1, 1.9)
    expert_ids_keys = jax.random.split(jax.random.fold_in(streams_of[8], 1), SPAN_LENGTH // TOK_DEV)
    expert_ids_turns = jax.random.permutation(jax.random.fold_in(streams_of[8], 3), SPAN_LENGTH // TOK_DEV)
    expert_ids = jax.vmap(lambda own, number: deal_out(jax.random.fold_in(streams_of[8], 2), own, number, TOK_DEV, EXPERTS, 2, CAP, 2))(expert_ids_keys, expert_ids_turns).reshape((SPAN_LENGTH, 2))
    route_weight = jnp.clip(0.2 + 0.8 * jax.random.uniform(streams_of[9], (SPAN_LENGTH, 2), jnp.float32) ** block_scale(streams_of[9], (SPAN_LENGTH, 2), ((0, 8),), -0.2, 0.2), 0.2, 1.0)
    w_gate = normal_values(streams_of[10], (EXPERTS, D, FF), D ** -0.5, 0.078125, ((0, 4), (2, 8)))
    w_up = normal_values(streams_of[11], (EXPERTS, D, FF), D ** -0.5, 0.078125, ((0, 4), (2, 8)))
    w_down = normal_values(streams_of[12], (EXPERTS, FF, D), FF ** -0.5, 0.09375, ((0, 4), (1, 8)))
    return {"queries": queries, "keys": keys, "values": values, "log_decay": log_decay, "doc_ids": doc_ids, "residual": residual, "out_weight": out_weight, "norm_gain": norm_gain, "expert_ids": expert_ids, "route_weight": route_weight, "w_gate": w_gate, "w_up": w_up, "w_down": w_down}


def reference(queries, keys, values, log_decay, doc_ids, residual, out_weight, norm_gain, expert_ids, route_weight, w_gate, w_up, w_down):
    query_f = queries.astype(jnp.float32).reshape(SPAN_LENGTH, ATTN_GROUPS, HS)
    key_f = keys.astype(jnp.float32).reshape(SPAN_LENGTH, ATTN_GROUPS, HS)
    value_f = values.astype(jnp.float32).reshape(SPAN_LENGTH, ATTN_GROUPS, HS)
    previous = jnp.concatenate([jnp.full((1,), -1, jnp.int32), doc_ids[:-1].astype(jnp.int32)])
    keep_factor = jnp.exp(log_decay) * (doc_ids == previous).astype(log_decay.dtype)[:, None]

    def advance(head_state, inputs):
        query_row, key_row, value_row, keep_row = inputs
        head_state = keep_row[:, None, None] * head_state + key_row[:, :, None] * value_row[:, None, :]
        return (head_state, jnp.einsum('hi,hij->hj', query_row, head_state, precision=lax.Precision.HIGHEST))
    initial = jnp.zeros((ATTN_GROUPS, HS, HS), query_f.dtype)
    _, head_out = lax.scan(advance, initial, (query_f, key_f, value_f, keep_factor))
    normed_heads = head_out * lax.rsqrt(lax.optimization_barrier(jnp.mean(head_out * head_out, axis=-1, keepdims=True)) + 1e-05)
    attn_in = normed_heads.reshape(SPAN_LENGTH, ATTN_GROUPS * HS).astype(jnp.bfloat16)
    hidden = residual.astype(jnp.float32) + jnp.dot(attn_in, out_weight, preferred_element_type=jnp.float32)
    normed = (hidden * lax.rsqrt(lax.optimization_barrier(jnp.mean(hidden * hidden, axis=-1, keepdims=True)) + 1e-06) * norm_gain).astype(jnp.bfloat16)
    moe_sum = jnp.zeros((SPAN_LENGTH, D), hidden.dtype)
    for expert in range(EXPERTS):
        chosen = expert_ids == expert
        used = jnp.any(chosen, axis=1)
        token_weight = lax.optimization_barrier(jnp.sum(jnp.where(chosen, route_weight, 0.0), axis=1))
        order = jnp.argsort(jnp.where(used, 0, 1).astype(jnp.int32), stable=True)[:N_SEQ * CAP]
        row_block = normed[order]
        gate_part = jnp.dot(row_block, w_gate[expert], preferred_element_type=jnp.float32)
        up_part = jnp.dot(row_block, w_up[expert], preferred_element_type=jnp.float32)
        act = (jax.nn.silu(gate_part) * up_part).astype(jnp.bfloat16)
        expert_out = jnp.dot(act, w_down[expert], preferred_element_type=jnp.float32)
        moe_sum = moe_sum.at[order].add(token_weight[order][:, None] * expert_out)
    return (hidden + moe_sum).astype(jnp.bfloat16)
```

```python
import functools

import jax
import jax.numpy as jnp
from jax import lax
from jax.experimental import pallas as pl
from jax.experimental.pallas import tpu as pltpu
from jax.sharding import PartitionSpec as P

HS = 128
AXES = ("seq", "hx")
HALVES = 2
EXTRA = 16
VMEM_LIMIT = 48 * 1024 * 1024
F32, BF16 = jnp.float32, jnp.bfloat16


def bits(low, high):
    out = []
    bit = high // 2
    while bit >= low:
        out.append(bit)
        bit //= 2
    return out


def exchange(x, mask, count):
    even, odd = mask
    pairs = [(d, d ^ (odd if d & 1 else even)) for d in range(count)]
    return lax.ppermute(x, AXES, pairs)


def total(parts):
    return functools.reduce(lambda a, b: a + b, [p.astype(F32) for p in parts])


def add(a, b):
    return total([a, b]).astype(BF16)


def gather_rows(x, masks, count):
    for mask in masks:
        x = jnp.concatenate([x, exchange(x, mask, count)], axis=0)
    return x


def reduce_rows(x, masks, count):
    for mask in reversed(masks):
        half = x.shape[0] // 2
        x = add(x[:half], exchange(x[half:], mask, count))
    return x


def offsets(masks):
    out = [0]
    for mask in masks:
        out = out + [o ^ mask for o in out]
    return out


def split3(x):
    high = x.astype(BF16)
    rest = x - high.astype(F32)
    mid = rest.astype(BF16)
    low = (rest - mid.astype(F32)).astype(BF16)
    return [high, mid, low]


def whole():
    return pl.BlockSpec(memory_space=pltpu.VMEM)


def column_cumsum(decay):
    tok = decay.shape[0]
    row = lax.broadcasted_iota(jnp.int32, (tok, tok), 0)
    col = lax.broadcasted_iota(jnp.int32, (tok, tok), 1)
    lower = (row >= col).astype(F32)
    return jnp.dot(lower, decay, precision=lax.Precision.HIGHEST, preferred_element_type=F32)


def state_kernel(k_ref, v_ref, decay_ref, doc_col_ref, doc_row_ref, weight_ref, out_ref):
    tok, heads = decay_ref.shape
    chunks = out_ref.shape[0]
    chunk = out_ref.shape[1] - EXTRA
    decay = decay_ref[...]
    log_cum = column_cumsum(decay)
    total = log_cum[tok - 1 : tok, :]
    last = doc_col_ref[tok - 1 : tok, :]
    end_weight = jnp.exp(total - log_cum) * (doc_col_ref[...] == last).astype(F32)
    through = jnp.exp(total)
    doc_row = doc_row_ref[...]
    row = lax.broadcasted_iota(jnp.int32, (EXTRA, HS), 0)
    routing = split3(weight_ref[...])
    fixed = [
        jnp.broadcast_to(doc_row[:, :1].astype(F32), (EXTRA, HS)),
        jnp.broadcast_to(doc_row[:, tok - 1 :].astype(F32), (EXTRA, HS)),
    ] + [jnp.broadcast_to(w.astype(F32), (EXTRA, HS)) for w in routing]
    per_head = chunks // heads
    for h in range(heads):
        lanes = slice(h * HS, (h + 1) * HS)
        weighted = (k_ref[:, lanes].astype(F32) * end_weight[:, h : h + 1]).astype(BF16)
        state = lax.dot_general(
            weighted, v_ref[:, lanes], (((0,), (0,)), ((), ())), preferred_element_type=F32
        ).astype(BF16)
        parts = [
            jnp.broadcast_to(p.astype(F32), (EXTRA, HS)) for p in split3(through[:, h : h + 1])
        ] + fixed
        extra = jnp.zeros((EXTRA, HS), F32)
        for i, part in enumerate(parts):
            extra = jnp.where(row == i, part, extra)
        for j in range(per_head):
            at = h * per_head + j
            out_ref[at, :chunk, :] = state[j * chunk : (j + 1) * chunk, :]
            out_ref[at, chunk:, :] = extra.astype(BF16)


def prefix_kernel(in_ref, out_ref):
    shards_n = in_ref.shape[0]
    chunk = out_ref.shape[1]
    carry = jnp.zeros((chunk, HS), F32)
    before = None
    for s in range(shards_n):
        extra = in_ref[s, chunk:, :].astype(F32)
        decay = extra[0:1] + extra[1:2] + extra[2:3]
        first, last = extra[3:4], extra[4:5]
        if s:
            out_ref[s] = (carry * (before == first).astype(F32)).astype(BF16)
            decay = decay * (before == last).astype(F32)
        else:
            out_ref[s] = carry.astype(BF16)
        carry = decay * carry + in_ref[s, :chunk, :].astype(F32)
        before = last


def intra_kernel(q_ref, k_ref, v_ref, decay_ref, decay_t_ref, doc_col_ref, doc_row_ref, out_ref, qw_ref):
    tok, heads = decay_ref.shape
    log_cum = column_cumsum(decay_ref[...])
    row = lax.broadcasted_iota(jnp.int32, (tok, tok), 0)
    col = lax.broadcasted_iota(jnp.int32, (tok, tok), 1)
    upper = (row <= col).astype(F32)
    log_cum_t = jnp.dot(
        decay_t_ref[...], upper, precision=lax.Precision.HIGHEST, preferred_element_type=F32
    )
    doc_col, doc_row = doc_col_ref[...], doc_row_ref[...]
    allowed = (row >= col) & (doc_col == doc_row)
    carry = jnp.exp(log_cum) * (doc_col == doc_row[:, :1]).astype(F32)
    for h in range(heads):
        lanes = slice(h * HS, (h + 1) * HS)
        scores = lax.dot_general(
            q_ref[:, lanes], k_ref[:, lanes], (((1,), (1,)), ((), ())), preferred_element_type=F32
        )
        exponent = jnp.where(allowed, log_cum[:, h : h + 1] - log_cum_t[h : h + 1, :], -jnp.inf)
        weighted = (scores * jnp.exp(exponent)).astype(BF16)
        out_ref[:, lanes] = jnp.dot(weighted, v_ref[:, lanes], preferred_element_type=F32)
        qw_ref[:, lanes] = (q_ref[:, lanes].astype(F32) * carry[:, h : h + 1]).astype(BF16)


def attend_kernel(intra_ref, qw_ref, state_ref, out_ref):
    heads = state_ref.shape[0]
    for h in range(heads):
        lanes = slice(h * HS, (h + 1) * HS)
        head_out = intra_ref[:, lanes] + jnp.dot(
            qw_ref[:, lanes], state_ref[h], preferred_element_type=F32
        )
        scale = lax.rsqrt(jnp.mean(head_out * head_out, axis=-1, keepdims=True) + 1e-05)
        out_ref[:, lanes] = (head_out * scale).astype(BF16)


def expert_kernel(
    steps, xa_ref, xb_ref, gate_ref, up_ref, down_ref, scale_ref, after_ref, oa_ref, ob_ref, done_ref, gate, up, act
):
    step = pl.program_id(0)
    rows = xa_ref.shape[0]
    over_width = (((1,), (1,)), ((), ()))

    @pl.when(step < steps)
    def _():
        x = jnp.concatenate([xa_ref[...], xb_ref[...]], axis=0)
        gate_part = lax.dot_general(gate_ref[...], x, over_width, preferred_element_type=F32)
        up_part = lax.dot_general(up_ref[...], x, over_width, preferred_element_type=F32)

        @pl.when(step == 0)
        def _():
            gate[...] = gate_part
            up[...] = up_part
            done_ref[...] = after_ref[...]

        @pl.when(step > 0)
        def _():
            gate[...] += gate_part
            up[...] += up_part

        @pl.when(step == steps - 1)
        def _():
            g = gate[...]
            acted = g / (1.0 + jnp.exp(-g)) * up[...] * scale_ref[...]
            act[...] = acted.T.astype(BF16)

    @pl.when(step >= steps)
    def _():
        out = jnp.dot(act[...], down_ref[...], preferred_element_type=F32).astype(BF16)
        oa_ref[...] = out[:rows]
        ob_ref[...] = out[rows:]


def expert(xa, xb, w_gate, w_up, w_down, scale, after):
    rows, width = xa.shape
    hidden = w_gate.shape[1]
    block = min(1024, width)
    steps = width // block
    into = lambda i: jnp.minimum(i, steps - 1)
    out_of = lambda i: jnp.maximum(i - steps, 0)
    return pl.pallas_call(
        functools.partial(expert_kernel, steps),
        grid=(2 * steps,),
        in_specs=[
            pl.BlockSpec((rows, block), lambda i: (0, into(i))),
            pl.BlockSpec((rows, block), lambda i: (0, into(i))),
            pl.BlockSpec((None, hidden, block), lambda i: (0, 0, into(i))),
            pl.BlockSpec((None, hidden, block), lambda i: (0, 0, into(i))),
            pl.BlockSpec((None, hidden, block), lambda i: (0, 0, out_of(i))),
            pl.BlockSpec((1, 2 * rows), lambda i: (0, 0)),
            pl.BlockSpec((8, 128), lambda i: (0, 0)),
        ],
        out_specs=[pl.BlockSpec((rows, block), lambda i: (0, out_of(i)))] * 2
        + [pl.BlockSpec((8, 128), lambda i: (0, 0))],
        out_shape=[jax.ShapeDtypeStruct((rows, width), BF16)] * 2 + [jax.ShapeDtypeStruct((8, 128), F32)],
        scratch_shapes=[
            pltpu.VMEM((hidden, 2 * rows), F32),
            pltpu.VMEM((hidden, 2 * rows), F32),
            pltpu.VMEM((2 * rows, hidden), BF16),
        ],
        compiler_params=pltpu.CompilerParams(vmem_limit_bytes=VMEM_LIMIT),
        cost_estimate=pl.CostEstimate(
            flops=12 * rows * width * hidden,
            bytes_accessed=6 * width * hidden + 8 * rows * width,
            transcendentals=2 * rows * hidden,
        ),
    )(xa, xb, w_gate, w_up, w_down, scale, after)


def call(kernel, out_shapes, *operands):
    return pl.pallas_call(
        kernel,
        in_specs=[whole()] * len(operands),
        out_specs=[whole()] * len(out_shapes),
        out_shape=out_shapes,
        compiler_params=pltpu.CompilerParams(vmem_limit_bytes=VMEM_LIMIT),
    )(*operands)


def shards(
    queries,
    keys,
    values,
    log_decay,
    doc_ids,
    residual,
    out_weight,
    norm_gain,
    expert_ids,
    route_weight,
    w_gate,
    w_up,
    w_down,
):
    n_seq, n_hx = lax.axis_size("seq"), lax.axis_size("hx")
    count = n_seq * n_hx
    inner = max(1, n_seq // 4)
    z_masks = bits(n_hx * inner, count)
    y_masks = bits(n_hx, n_hx * inner)
    x_masks = bits(2, n_hx)
    order_even = z_masks + y_masks + x_masks
    order_odd = z_masks + (x_masks + y_masks if len(x_masks) == len(y_masks) else y_masks + x_masks)
    masks = list(zip(order_even, order_odd))
    core = (1, 1)
    hx_masks = [(m, m) for m in x_masks] + [core]
    hx_index = lax.axis_index("hx")
    device = lax.axis_index("seq") * n_hx + hx_index

    tok_count = queries.shape[0]
    own_count = tok_count // n_hx
    half_count = own_count // HALVES
    heads = log_decay.shape[1]
    chunk = heads * HS // n_seq

    doc_col, doc_row = doc_ids.reshape(tok_count, 1), doc_ids.reshape(1, tok_count)
    own_weight = jnp.sum(jnp.where(expert_ids == hx_index, route_weight, 0.0), axis=1).reshape(1, tok_count)
    shape = jax.ShapeDtypeStruct
    (payload,) = call(
        state_kernel,
        [shape((n_seq, chunk + EXTRA, HS), BF16)],
        keys, values, log_decay, doc_col, doc_row, own_weight,
    )
    arrived = lax.all_to_all(payload, "seq", split_axis=0, concat_axis=0, tiled=True)
    intra, query_weighted = call(
        intra_kernel,
        [shape((tok_count, heads * HS), F32), shape((tok_count, heads * HS), BF16)],
        queries, keys, values, log_decay, log_decay.T, doc_col, doc_row,
    )
    (incoming,) = call(prefix_kernel, [shape((n_seq, chunk, HS), BF16)], arrived)
    incoming = lax.all_to_all(incoming, "seq", split_axis=0, concat_axis=0, tiled=True)

    order = offsets([even for even, _ in hx_masks])

    def by_neighbour(x):
        blocks = [
            lax.dynamic_slice_in_dim(x, (hx_index ^ o) * own_count + i * half_count, half_count)
            for i in range(HALVES)
            for o in order
        ]
        return jnp.concatenate(blocks, axis=0)

    (attn_in,) = call(
        attend_kernel,
        [shape((tok_count, heads * HS), BF16)],
        by_neighbour(intra), by_neighbour(query_weighted), incoming.reshape(heads, HS, HS),
    )
    projected = jnp.dot(attn_in, out_weight, preferred_element_type=F32).astype(BF16)
    own_residual = lax.dynamic_slice_in_dim(residual, hx_index * own_count, own_count)

    extra = arrived[:, chunk + 5 : chunk + 8, :].astype(F32)
    weights = jnp.sum(extra, axis=1).reshape(count, own_count)
    even_off, odd_off = offsets(order_even), offsets(order_odd)
    even_off, odd_off = (
        even_off + [o ^ 1 for o in odd_off],
        odd_off + [o ^ 1 for o in even_off],
    )
    sources = device ^ jnp.where(device & 1 == 1, jnp.array(odd_off), jnp.array(even_off))
    weights = weights[sources].reshape(2, 2, count // 4, HALVES, half_count)

    halves = []
    for i in range(HALVES):
        rows = projected[i * n_hx * half_count : (i + 1) * n_hx * half_count]
        rows = reduce_rows(rows, hx_masks, count)
        hidden = own_residual[i * half_count : (i + 1) * half_count].astype(F32) + rows.astype(F32)
        normed = (
            hidden
            * lax.rsqrt(jnp.mean(hidden * hidden, axis=-1, keepdims=True) + 1e-06)
            * norm_gain
        ).astype(BF16)
        halves.append((hidden, normed))

    gate_t, up_t = jnp.swapaxes(w_gate, 1, 2), jnp.swapaxes(w_up, 1, 2)
    done = jnp.zeros((8, 128), F32)
    outs = []
    for i, (hidden, normed) in enumerate(halves):
        near = gather_rows(normed, masks[:-1], count)
        far = exchange(near, masks[-1], count)
        near_other = exchange(near, core, count)
        scale = [weights[:, step, :, i].reshape(1, -1) for step in range(2)]
        near_out, near_back, done = expert(near, near_other, gate_t, up_t, w_down, scale[0], done)
        far, done = lax.optimization_barrier((far, done))
        far_other = exchange(far, core, count)
        far_out, far_back, done = expert(far, far_other, gate_t, up_t, w_down, scale[1], done)
        far_sum = add(far_out, exchange(far_back, core, count))
        parts = [near_out, exchange(near_back, core, count), exchange(far_sum, masks[-1], count)]
        for mask in reversed(masks[:-1]):
            half = parts[0].shape[0] // 2
            sent = total([p[half:] for p in parts]).astype(BF16)
            parts = [total([p[:half] for p in parts]), exchange(sent, mask, count)]
        outs.append(total([hidden] + parts).astype(BF16))
    return lax.all_to_all(jnp.concatenate(outs, axis=0), "hx", split_axis=1, concat_axis=0, tiled=True)


def solution(mesh):
    return jax.shard_map(
        shards,
        mesh=mesh,
        in_specs=(
            P("seq", "hx"),
            P("seq", "hx"),
            P("seq", "hx"),
            P("seq", "hx"),
            P("seq"),
            P("seq", None),
            P("hx", None),
            P(),
            P("seq", None),
            P("seq", None),
            P("hx", None, "seq"),
            P("hx", None, "seq"),
            P("hx", "seq", None),
        ),
        out_specs=P("seq", "hx"),
        check_vma=False,
    )
```

```python
import functools

import jax
import jax.numpy as jnp
from jax import lax
from jax.experimental import pallas as pl
from jax.experimental.pallas import tpu as pltpu
from jax.sharding import PartitionSpec as P

HS = 128
AXES = ("seq", "hx")
HALVES = 2
EXTRA = 16
VMEM_LIMIT = 16 * 1024 * 1024
F32, BF16 = jnp.float32, jnp.bfloat16


def bits(low, high):
    out = []
    bit = high // 2
    while bit >= low:
        out.append(bit)
        bit //= 2
    return out


def exchange(x, mask, count):
    even, odd = mask
    pairs = [(d, d ^ (odd if d & 1 else even)) for d in range(count)]
    return lax.ppermute(x, AXES, pairs)


def total(parts):
    return functools.reduce(lambda a, b: a + b, [p.astype(F32) for p in parts])


def add(a, b):
    return total([a, b]).astype(BF16)


def gather_rows(x, masks, count):
    for mask in masks:
        x = jnp.concatenate([x, exchange(x, mask, count)], axis=0)
    return x


def reduce_rows(x, masks, count):
    for mask in reversed(masks):
        half = x.shape[0] // 2
        x = add(x[:half], exchange(x[half:], mask, count))
    return x


def offsets(masks):
    out = [0]
    for mask in masks:
        out = out + [o ^ mask for o in out]
    return out


def split3(x):
    high = x.astype(BF16)
    rest = x - high.astype(F32)
    mid = rest.astype(BF16)
    low = (rest - mid.astype(F32)).astype(BF16)
    return [high, mid, low]


def whole():
    return pl.BlockSpec(memory_space=pltpu.VMEM)


def over_last(a, b):
    return lax.dot_general(
        a, b, (((1,), (1,)), ((), ())), precision=lax.Precision.HIGHEST, preferred_element_type=F32
    )


def by_column(decay_t, doc_row):
    tok = doc_row.shape[1]
    row = lax.broadcasted_iota(jnp.int32, (tok, tok), 0)
    col = lax.broadcasted_iota(jnp.int32, (tok, tok), 1)
    doc_rows = jnp.broadcast_to(doc_row.astype(F32), (8, tok))
    log_cum = over_last((row >= col).astype(F32), decay_t)
    return log_cum, over_last((row == col).astype(F32), doc_rows)[:, :1]


def state_kernel(me_ref, k_hbm, v_hbm, decay_ref, doc_ref, ids_ref, route_ref, out_ref, k_ref, v_ref, sems):
    copies = [
        pltpu.make_async_copy(k_hbm, k_ref, sems.at[0]),
        pltpu.make_async_copy(v_hbm, v_ref, sems.at[1]),
    ]
    for copy in copies:
        copy.start()
    heads, tok = decay_ref.shape
    chunks = out_ref.shape[0]
    chunk = out_ref.shape[1] - EXTRA
    doc_row = doc_ref[...].astype(F32)
    log_cum, doc_col = by_column(decay_ref[...], doc_row)
    total = log_cum[tok - 1 : tok, :]
    first, last = doc_row[:, :1], doc_row[:, tok - 1 :]
    end_weight = jnp.exp(total - log_cum) * (doc_col == last).astype(F32)
    through = jnp.exp(total)
    weight = jnp.sum(jnp.where(ids_ref[...] == me_ref[0], route_ref[...], 0.0), axis=0, keepdims=True)
    row = lax.broadcasted_iota(jnp.int32, (EXTRA, HS), 0)
    fixed = [jnp.broadcast_to(w.astype(F32), (EXTRA, HS)) for w in [first, last] + split3(weight)]
    per_head = chunks // heads
    for copy in copies:
        copy.wait()
    for h in range(heads):
        lanes = slice(h * HS, (h + 1) * HS)
        weighted = (k_ref[:, lanes].astype(F32) * end_weight[:, h : h + 1]).astype(BF16)
        state = lax.dot_general(
            weighted, v_ref[:, lanes], (((0,), (0,)), ((), ())), preferred_element_type=F32
        ).astype(BF16)
        parts = [
            jnp.broadcast_to(p.astype(F32), (EXTRA, HS)) for p in split3(through[:, h : h + 1])
        ] + fixed
        extra = jnp.zeros((EXTRA, HS), F32)
        for i, part in enumerate(parts):
            extra = jnp.where(row == i, part, extra)
        for j in range(per_head):
            at = h * per_head + j
            out_ref[at, :chunk, :] = state[j * chunk : (j + 1) * chunk, :]
            out_ref[at, chunk:, :] = extra.astype(BF16)


def prefix_kernel(in_ref, out_ref):
    shards_n = in_ref.shape[0]
    chunk = out_ref.shape[1]
    carry = jnp.zeros((chunk, HS), F32)
    before = None
    for s in range(shards_n):
        extra = in_ref[s, chunk:, :].astype(F32)
        decay = extra[0:1] + extra[1:2] + extra[2:3]
        first, last = extra[3:4], extra[4:5]
        if s:
            out_ref[s] = (carry * (before == first).astype(F32)).astype(BF16)
            decay = decay * (before == last).astype(F32)
        else:
            out_ref[s] = carry.astype(BF16)
        carry = decay * carry + in_ref[s, :chunk, :].astype(F32)
        before = last


def intra_kernel(q_hbm, k_hbm, v_hbm, decay_ref, doc_ref, out_ref, qw_ref, q_ref, k_ref, v_ref, sems):
    copies = [
        pltpu.make_async_copy(q_hbm, q_ref, sems.at[0]),
        pltpu.make_async_copy(k_hbm, k_ref, sems.at[1]),
        pltpu.make_async_copy(v_hbm, v_ref, sems.at[2]),
    ]
    for copy in copies:
        copy.start()
    heads, tok = decay_ref.shape
    doc_row = doc_ref[...].astype(F32)
    log_cum, doc_col = by_column(decay_ref[...], doc_row)
    row = lax.broadcasted_iota(jnp.int32, (tok, tok), 0)
    col = lax.broadcasted_iota(jnp.int32, (tok, tok), 1)
    log_cum_t = jnp.dot(
        decay_ref[...], (row <= col).astype(F32), precision=lax.Precision.HIGHEST, preferred_element_type=F32
    )
    allowed = (row >= col) & (doc_col == doc_row)
    carry = jnp.exp(log_cum) * (doc_col == doc_row[:, :1]).astype(F32)
    for copy in copies:
        copy.wait()
    for h in range(heads):
        lanes = slice(h * HS, (h + 1) * HS)
        scores = lax.dot_general(
            q_ref[:, lanes], k_ref[:, lanes], (((1,), (1,)), ((), ())), preferred_element_type=F32
        )
        exponent = jnp.where(allowed, log_cum[:, h : h + 1] - log_cum_t[h : h + 1, :], -jnp.inf)
        weighted = (scores * jnp.exp(exponent)).astype(BF16)
        out_ref[:, lanes] = jnp.dot(weighted, v_ref[:, lanes], preferred_element_type=F32)
        qw_ref[:, lanes] = (q_ref[:, lanes].astype(F32) * carry[:, h : h + 1]).astype(BF16)


def attend_kernel(intra_ref, qw_ref, state_ref, out_ref):
    heads = state_ref.shape[0]
    for h in range(heads):
        lanes = slice(h * HS, (h + 1) * HS)
        head_out = intra_ref[:, lanes] + jnp.dot(
            qw_ref[:, lanes], state_ref[h], preferred_element_type=F32
        )
        scale = lax.rsqrt(jnp.mean(head_out * head_out, axis=-1, keepdims=True) + 1e-05)
        out_ref[:, lanes] = (head_out * scale).astype(BF16)


def load_kernel(*refs):
    count = (len(refs) - 2) // 2
    sems = refs[-1]
    copies = [
        pltpu.make_async_copy(refs[i].at[0], refs[count + i], sems.at[i]) for i in range(count)
    ]
    for copy in copies:
        copy.start()
    for copy in copies:
        copy.wait()
    refs[2 * count][...] = jnp.zeros_like(refs[2 * count])


def load(*weights):
    shapes = [w.shape[1:] for w in weights]
    weights = [pltpu.with_memory_space_constraint(w, pltpu.HBM) for w in weights]
    *loaded, done = pl.pallas_call(
        load_kernel,
        in_specs=[pl.BlockSpec(memory_space=pltpu.HBM)] * len(weights),
        out_specs=[whole()] * (len(weights) + 1),
        out_shape=[pltpu.VMEM(s, BF16) for s in shapes] + [jax.ShapeDtypeStruct((8, 128), F32)],
        scratch_shapes=[pltpu.SemaphoreType.DMA((len(weights),))],
        compiler_params=pltpu.CompilerParams(vmem_limit_bytes=VMEM_LIMIT),
    )(*weights)
    return loaded, done


def expert_kernel(blocks, *refs):
    x_refs, (gate_ref, up_ref, down_ref, scale_ref) = refs[:blocks], refs[blocks : blocks + 4]
    out_refs, (x, act) = refs[blocks + 5 : 2 * blocks + 5], refs[2 * blocks + 5 :]
    rows, width = x_refs[0].shape
    for i, ref in enumerate(x_refs):
        x[i * rows : (i + 1) * rows, :] = ref[...]
    over_width = (((1,), (1,)), ((), ()))
    g = lax.dot_general(gate_ref[...], x[...], over_width, preferred_element_type=F32)
    u = lax.dot_general(up_ref[...], x[...], over_width, preferred_element_type=F32)
    act[...] = (g / (1.0 + jnp.exp(-g)) * u * scale_ref[...]).T.astype(BF16)
    block = min(1024, width)
    for start in range(0, width, block):
        lanes = slice(start, start + block)
        out = jnp.dot(act[...], down_ref[:, lanes], preferred_element_type=F32).astype(BF16)
        for i, ref in enumerate(out_refs):
            ref[:, lanes] = out[i * rows : (i + 1) * rows]


def expert(xs, w_gate, w_up, w_down, loaded, scale):
    rows, width = xs[0].shape
    hidden = w_gate.shape[0]
    blocks = len(xs)
    return pl.pallas_call(
        functools.partial(expert_kernel, blocks),
        in_specs=[whole()] * (blocks + 5),
        out_specs=[whole()] * blocks,
        out_shape=[jax.ShapeDtypeStruct((rows, width), BF16)] * blocks,
        scratch_shapes=[pltpu.VMEM((blocks * rows, width), BF16), pltpu.VMEM((blocks * rows, hidden), BF16)],
        compiler_params=pltpu.CompilerParams(vmem_limit_bytes=VMEM_LIMIT),
        cost_estimate=pl.CostEstimate(
            flops=6 * blocks * rows * width * hidden,
            bytes_accessed=6 * width * hidden + 4 * blocks * rows * width,
            transcendentals=blocks * rows * hidden,
        ),
    )(*xs, w_gate, w_up, w_down, scale, loaded)


def call(kernel, out_shapes, *operands, scalars=0, far=0):
    fetched = operands[scalars : scalars + far]
    specs = [pl.BlockSpec(memory_space=pltpu.SMEM)] * scalars + [pl.BlockSpec(memory_space=pltpu.HBM)] * far
    operands = (
        operands[:scalars]
        + tuple(pltpu.with_memory_space_constraint(f, pltpu.HBM) for f in fetched)
        + operands[scalars + far :]
    )
    scratch = [pltpu.VMEM(f.shape, f.dtype) for f in fetched]
    return pl.pallas_call(
        kernel,
        in_specs=specs + [whole()] * (len(operands) - len(specs)),
        out_specs=[whole()] * len(out_shapes),
        out_shape=out_shapes,
        scratch_shapes=scratch + [pltpu.SemaphoreType.DMA((far,))] * (far > 0),
        compiler_params=pltpu.CompilerParams(vmem_limit_bytes=VMEM_LIMIT),
    )(*operands)


def shards(
    queries,
    keys,
    values,
    log_decay,
    doc_ids,
    residual,
    out_weight,
    norm_gain,
    expert_ids,
    route_weight,
    w_gate,
    w_up,
    w_down,
):
    n_seq, n_hx = lax.axis_size("seq"), lax.axis_size("hx")
    count = n_seq * n_hx
    inner = max(1, n_seq // 4)
    z_masks = bits(n_hx * inner, count)
    y_masks = bits(n_hx, n_hx * inner)
    x_masks = bits(2, n_hx)
    order_even = y_masks + x_masks
    order_odd = x_masks + y_masks if len(x_masks) == len(y_masks) else order_even
    net = list(zip(order_even, order_odd))
    core = (1, 1)
    hx_masks = [(m, m) for m in x_masks] + [core]
    hx_index = lax.axis_index("hx")
    device = lax.axis_index("seq") * n_hx + hx_index

    tok_count = queries.shape[0]
    own_count = tok_count // n_hx
    half_count = own_count // HALVES
    heads = log_decay.shape[1]
    chunk = heads * HS // n_seq

    decay_t, doc_row = log_decay.T, doc_ids.reshape(1, tok_count)
    shape = jax.ShapeDtypeStruct
    (payload,) = call(
        state_kernel,
        [shape((n_seq, chunk + EXTRA, HS), BF16)],
        hx_index.reshape(1), keys, values, decay_t, doc_row, expert_ids.T, route_weight.T,
        scalars=1, far=2,
    )
    arrived = lax.all_to_all(payload, "seq", split_axis=0, concat_axis=0, tiled=True)
    intra, query_weighted = call(
        intra_kernel,
        [shape((tok_count, heads * HS), F32), shape((tok_count, heads * HS), BF16)],
        queries, keys, values, decay_t, doc_row,
        far=3,
    )
    (incoming,) = call(prefix_kernel, [shape((n_seq, chunk, HS), BF16)], arrived)
    incoming = lax.all_to_all(incoming, "seq", split_axis=0, concat_axis=0, tiled=True)

    order = offsets([even for even, _ in hx_masks])

    def by_neighbour(x):
        blocks = [
            lax.dynamic_slice_in_dim(x, (hx_index ^ o) * own_count + i * half_count, half_count)
            for i in range(HALVES)
            for o in order
        ]
        return jnp.concatenate(blocks, axis=0)

    extra = arrived[:, chunk + 5 : chunk + 8, :].astype(F32)
    weights = jnp.sum(extra, axis=1).reshape(count, HALVES, half_count)
    units = {}
    for name, group in (("near", [0]), ("far", [z_masks[1]])):
        even = [o ^ g for g in group for o in offsets([z_masks[0]] + [m for m, _ in net])]
        odd = [o ^ g for g in group for o in offsets([z_masks[0]] + [m for _, m in net])]
        even, odd = even + [o ^ 1 for o in odd], odd + [o ^ 1 for o in even]
        units[name] = device ^ jnp.where(device & 1 == 1, jnp.array(odd), jnp.array(even))
    scale = {
        name + str(i): weights[rows, i].reshape(1, -1) for name, rows in units.items() for i in range(HALVES)
    }
    own_residual = lax.dynamic_slice_in_dim(residual, hx_index * own_count, own_count)
    wait = lax.optimization_barrier
    intra, query_weighted, scale, own_residual = wait(
        (by_neighbour(intra), by_neighbour(query_weighted), scale, own_residual)
    )

    (attn_in,) = call(
        attend_kernel,
        [shape((tok_count, heads * HS), BF16)],
        intra, query_weighted, incoming.reshape(heads, HS, HS),
    )
    projected = jnp.dot(attn_in, out_weight, preferred_element_type=F32).astype(BF16)

    def hx_send(i):
        rows = projected[i * n_hx * half_count : (i + 1) * n_hx * half_count]
        half = rows.shape[0] // 2
        return rows[:half], exchange(rows[half:], core, count)

    def hx_rest(rows, got):
        return reduce_rows(add(rows, got), hx_masks[:-1], count)

    def norm(i, rows, own_residual):
        hidden = own_residual[i * half_count : (i + 1) * half_count].astype(F32) + rows.astype(F32)
        normed = (
            hidden
            * lax.rsqrt(jnp.mean(hidden * hidden, axis=-1, keepdims=True) + 1e-06)
            * norm_gain
        ).astype(BF16)
        return hidden, normed

    def z_step(rows, mask):
        return exchange(rows, (mask, mask), count)

    def spread(unit):
        return gather_rows(unit, net[:-1], count)

    def to_core(rows):
        return exchange(rows, core, count)

    def back(outs):
        mine, mine_last, other, other_last = outs
        return add(mine_last, to_core(other_last)), [mine, to_core(other)]

    def fold(terms, got):
        terms = terms + [got]
        for mask in reversed(net[:-1]):
            half = terms[0].shape[0] // 2
            sent = total([t[half:] for t in terms]).astype(BF16)
            terms = [total([t[:half] for t in terms]), exchange(sent, mask, count)]
        return total(terms)

    last = net[-1]
    rows_a, got_a = hx_send(0)
    rows_b, got_b = hx_send(1)
    a = hx_rest(rows_a, got_a)
    a, rows_b, got_b, weights_in, scale, own_residual = wait(
        (a, rows_b, got_b, (w_gate, w_up, w_down), scale, own_residual)
    )
    hidden_a, a = norm(0, a, own_residual)
    w_gate, w_up, w_down = weights_in
    weights_in, loaded = load(jnp.swapaxes(w_gate, 1, 2), jnp.swapaxes(w_up, 1, 2), w_down)
    a1 = jnp.concatenate([a, z_step(a, z_masks[0])], axis=0)
    a1, rows_b, got_b, loaded = wait((a1, rows_b, got_b, loaded))
    a2 = z_step(a1, z_masks[1])
    a1 = spread(a1)
    b = hx_rest(rows_b, got_b)
    a1, a2, b, own_residual = wait((a1, a2, b, own_residual))
    a1_last, a1_other = exchange(a1, last, count), to_core(a1)
    a2 = spread(a2)
    hidden_b, b = norm(1, b, own_residual)
    b1 = jnp.concatenate([b, z_step(b, z_masks[0])], axis=0)
    a1, a1_last, a1_other, a2, b1 = wait((a1, a1_last, a1_other, a2, b1))
    a2_last, a2_other = exchange(a2, last, count), to_core(a2)
    a1_out = expert([a1, a1_last, a1_other, to_core(a1_last)], *weights_in, loaded, scale["near0"])
    b2 = z_step(b1, z_masks[1])
    b1 = spread(b1)
    a2, a2_last, a2_other, b1, b2, a1_out = wait((a2, a2_last, a2_other, b1, b2, a1_out))
    b1_last, b1_other = exchange(b1, last, count), to_core(b1)
    a2_out = expert([a2, a2_last, a2_other, to_core(a2_last)], *weights_in, loaded, scale["far0"])
    b2 = spread(b2)
    a1_send, a1_rest = back(a1_out)
    a2_send, a2_rest = back(a2_out)
    b1, b1_last, b1_other, b2, a1_send, a1_rest, a2_send, a2_rest = wait(
        (b1, b1_last, b1_other, b2, a1_send, a1_rest, a2_send, a2_rest)
    )
    b2_last, b2_other = exchange(b2, last, count), to_core(b2)
    a2_got = exchange(a2_send, last, count)
    b1_out = expert([b1, b1_last, b1_other, to_core(b1_last)], *weights_in, loaded, scale["near1"])
    b1_send, b1_rest = back(b1_out)
    b2, b2_last, b2_other, a2_got, b1_send, b1_rest, a1_send = wait(
        (b2, b2_last, b2_other, a2_got, b1_send, b1_rest, a1_send)
    )
    a1_got = exchange(a1_send, last, count)
    a2_sum = fold(a2_rest, a2_got)
    b2_out = expert([b2, b2_last, b2_other, to_core(b2_last)], *weights_in, loaded, scale["far1"])
    b2_send, b2_rest = back(b2_out)
    a2_sum, a1_got, b2_send, b2_rest, b1_send, b1_rest = wait(
        (a2_sum, a1_got, b2_send, b2_rest, b1_send, b1_rest)
    )
    a_z = z_step(a2_sum.astype(BF16), z_masks[1])
    a1_sum = fold(a1_rest, a1_got)
    b2_got = exchange(b2_send, last, count)
    a_sum = a1_sum + a_z.astype(F32)
    a_sum, b2_got, b1_send = wait((a_sum, b2_got, b1_send))
    a_z = z_step(a_sum[half_count:].astype(BF16), z_masks[0])
    b2_sum = fold(b2_rest, b2_got)
    b1_got = exchange(b1_send, last, count)
    a_out = total([hidden_a, a_sum[:half_count], a_z]).astype(BF16)
    a_out, b2_sum, b1_got = wait((a_out, b2_sum, b1_got))
    b_z = z_step(b2_sum.astype(BF16), z_masks[1])
    b1_sum = fold(b1_rest, b1_got)
    a_out = lax.all_to_all(a_out, "hx", split_axis=1, concat_axis=0, tiled=True)
    b_sum = b1_sum + b_z.astype(F32)
    b_sum, a_out = wait((b_sum, a_out))
    b_z = z_step(b_sum[half_count:].astype(BF16), z_masks[0])
    b_out = total([hidden_b, b_sum[:half_count], b_z]).astype(BF16)
    b_out = lax.all_to_all(b_out, "hx", split_axis=1, concat_axis=0, tiled=True)
    outs = [o.reshape(n_hx, half_count, -1) for o in (a_out, b_out)]
    return jnp.concatenate(outs, axis=1).reshape(tok_count, -1)


def solution(mesh):
    return jax.shard_map(
        shards,
        mesh=mesh,
        in_specs=(
            P("seq", "hx"),
            P("seq", "hx"),
            P("seq", "hx"),
            P("seq", "hx"),
            P("seq"),
            P("seq", None),
            P("hx", None),
            P(),
            P("seq", None),
            P("seq", None),
            P("hx", None, "seq"),
            P("hx", None, "seq"),
            P("hx", "seq", None),
        ),
        out_specs=P("seq", "hx"),
        check_vma=False,
    )
```

```python
import functools

import jax
import jax.numpy as jnp
from jax import lax
from jax.experimental import pallas as pl
from jax.experimental.pallas import tpu as pltpu
from jax.sharding import PartitionSpec as P

HS = 128
AXES = ("seq", "hx")
HALVES = 2
EXTRA = 16
VMEM_LIMIT = 16 * 1024 * 1024
F32, BF16 = jnp.float32, jnp.bfloat16


def bits(low, high):
    out = []
    bit = high // 2
    while bit >= low:
        out.append(bit)
        bit //= 2
    return out


def exchange(x, mask, count):
    even, odd = mask
    pairs = [(d, d ^ (odd if d & 1 else even)) for d in range(count)]
    return lax.ppermute(x, AXES, pairs)


def total(parts):
    return functools.reduce(lambda a, b: a + b, [p.astype(F32) for p in parts])


def add(a, b):
    return total([a, b]).astype(BF16)


def gather_rows(x, masks, count):
    for mask in masks:
        x = jnp.concatenate([x, exchange(x, mask, count)], axis=0)
    return x


def reduce_rows(x, masks, count):
    for mask in reversed(masks):
        half = x.shape[0] // 2
        x = add(x[:half], exchange(x[half:], mask, count))
    return x


def offsets(masks):
    out = [0]
    for mask in masks:
        out = out + [o ^ mask for o in out]
    return out


def split3(x):
    high = x.astype(BF16)
    rest = x - high.astype(F32)
    mid = rest.astype(BF16)
    low = (rest - mid.astype(F32)).astype(BF16)
    return [high, mid, low]


def whole():
    return pl.BlockSpec(memory_space=pltpu.VMEM)


def over_last(a, b):
    return lax.dot_general(
        a, b, (((1,), (1,)), ((), ())), precision=lax.Precision.HIGHEST, preferred_element_type=F32
    )


def by_column(decay_t, doc_row):
    tok = doc_row.shape[1]
    row = lax.broadcasted_iota(jnp.int32, (tok, tok), 0)
    col = lax.broadcasted_iota(jnp.int32, (tok, tok), 1)
    doc_rows = jnp.broadcast_to(doc_row.astype(F32), (8, tok))
    log_cum = over_last((row >= col).astype(F32), decay_t)
    return log_cum, over_last((row == col).astype(F32), doc_rows)[:, :1]


def fetch(sources, targets, sems):
    copies = [pltpu.make_async_copy(s, t, sems.at[i]) for i, (s, t) in enumerate(zip(sources, targets))]
    for copy in copies:
        copy.start()
    return copies


def state_kernel(me_ref, *refs):
    sources, out_ref, targets, sems = refs[:6], refs[6], refs[7:13], refs[13]
    decay_ref, doc_ref, ids_ref, route_ref, k_ref, v_ref = targets
    copies = fetch(sources, targets, sems)
    for copy in copies[:4]:
        copy.wait()
    heads, tok = decay_ref.shape
    chunks = out_ref.shape[0]
    chunk = out_ref.shape[1] - EXTRA
    doc_row = doc_ref[...].astype(F32)
    log_cum, doc_col = by_column(decay_ref[...], doc_row)
    total = log_cum[tok - 1 : tok, :]
    first, last = doc_row[:, :1], doc_row[:, tok - 1 :]
    end_weight = jnp.exp(total - log_cum) * (doc_col == last).astype(F32)
    through = jnp.exp(total)
    weight = jnp.sum(jnp.where(ids_ref[...] == me_ref[0], route_ref[...], 0.0), axis=0, keepdims=True)
    row = lax.broadcasted_iota(jnp.int32, (EXTRA, HS), 0)
    fixed = [jnp.broadcast_to(w.astype(F32), (EXTRA, HS)) for w in [first, last] + split3(weight)]
    per_head = chunks // heads
    for copy in copies[4:]:
        copy.wait()
    for h in range(heads):
        lanes = slice(h * HS, (h + 1) * HS)
        weighted = (k_ref[:, lanes].astype(F32) * end_weight[:, h : h + 1]).astype(BF16)
        state = lax.dot_general(
            weighted, v_ref[:, lanes], (((0,), (0,)), ((), ())), preferred_element_type=F32
        ).astype(BF16)
        parts = [
            jnp.broadcast_to(p.astype(F32), (EXTRA, HS)) for p in split3(through[:, h : h + 1])
        ] + fixed
        extra = jnp.zeros((EXTRA, HS), F32)
        for i, part in enumerate(parts):
            extra = jnp.where(row == i, part, extra)
        for j in range(per_head):
            at = h * per_head + j
            out_ref[at, :chunk, :] = state[j * chunk : (j + 1) * chunk, :]
            out_ref[at, chunk:, :] = extra.astype(BF16)


def prefix_kernel(in_ref, out_ref):
    shards_n = in_ref.shape[0]
    chunk = out_ref.shape[1]
    carry = jnp.zeros((chunk, HS), F32)
    before = None
    for s in range(shards_n):
        extra = in_ref[s, chunk:, :].astype(F32)
        decay = extra[0:1] + extra[1:2] + extra[2:3]
        first, last = extra[3:4], extra[4:5]
        if s:
            out_ref[s] = (carry * (before == first).astype(F32)).astype(BF16)
            decay = decay * (before == last).astype(F32)
        else:
            out_ref[s] = carry.astype(BF16)
        carry = decay * carry + in_ref[s, :chunk, :].astype(F32)
        before = last


def intra_kernel(*refs):
    sources, (out_ref, qw_ref), targets, sems = refs[:5], refs[5:7], refs[7:12], refs[12]
    decay_ref, doc_ref, q_ref, k_ref, v_ref = targets
    copies = fetch(sources, targets, sems)
    for copy in copies[:2]:
        copy.wait()
    heads, tok = decay_ref.shape
    doc_row = doc_ref[...].astype(F32)
    log_cum, doc_col = by_column(decay_ref[...], doc_row)
    row = lax.broadcasted_iota(jnp.int32, (tok, tok), 0)
    col = lax.broadcasted_iota(jnp.int32, (tok, tok), 1)
    log_cum_t = jnp.dot(
        decay_ref[...], (row <= col).astype(F32), precision=lax.Precision.HIGHEST, preferred_element_type=F32
    )
    allowed = (row >= col) & (doc_col == doc_row)
    carry = jnp.exp(log_cum) * (doc_col == doc_row[:, :1]).astype(F32)
    for copy in copies[2:]:
        copy.wait()
    for h in range(heads):
        lanes = slice(h * HS, (h + 1) * HS)
        scores = lax.dot_general(
            q_ref[:, lanes], k_ref[:, lanes], (((1,), (1,)), ((), ())), preferred_element_type=F32
        )
        exponent = jnp.where(allowed, log_cum[:, h : h + 1] - log_cum_t[h : h + 1, :], -jnp.inf)
        weighted = (scores * jnp.exp(exponent)).astype(BF16)
        out_ref[:, lanes] = jnp.dot(weighted, v_ref[:, lanes], preferred_element_type=F32)
        qw_ref[:, lanes] = (q_ref[:, lanes].astype(F32) * carry[:, h : h + 1]).astype(BF16)


def attend_kernel(intra_ref, qw_ref, state_ref, out_ref):
    heads = state_ref.shape[0]
    for h in range(heads):
        lanes = slice(h * HS, (h + 1) * HS)
        head_out = intra_ref[:, lanes] + jnp.dot(
            qw_ref[:, lanes], state_ref[h], preferred_element_type=F32
        )
        scale = lax.rsqrt(jnp.mean(head_out * head_out, axis=-1, keepdims=True) + 1e-05)
        out_ref[:, lanes] = (head_out * scale).astype(BF16)


def load_kernel(*refs):
    count = (len(refs) - 2) // 2
    sems = refs[-1]
    copies = [
        pltpu.make_async_copy(refs[i].at[0], refs[count + i], sems.at[i]) for i in range(count)
    ]
    for copy in copies:
        copy.start()
    for copy in copies:
        copy.wait()
    refs[2 * count][...] = jnp.zeros_like(refs[2 * count])


def load(*weights):
    shapes = [w.shape[1:] for w in weights]
    weights = [pltpu.with_memory_space_constraint(w, pltpu.HBM) for w in weights]
    *loaded, done = pl.pallas_call(
        load_kernel,
        in_specs=[pl.BlockSpec(memory_space=pltpu.HBM)] * len(weights),
        out_specs=[whole()] * (len(weights) + 1),
        out_shape=[pltpu.VMEM(s, BF16) for s in shapes] + [jax.ShapeDtypeStruct((8, 128), F32)],
        scratch_shapes=[pltpu.SemaphoreType.DMA((len(weights),))],
        compiler_params=pltpu.CompilerParams(vmem_limit_bytes=VMEM_LIMIT),
    )(*weights)
    return loaded, done


def expert_kernel(blocks, *refs):
    x_refs, (gate_ref, up_ref, down_ref, scale_ref) = refs[:blocks], refs[blocks : blocks + 4]
    out_refs, (x, act) = refs[blocks + 5 : -2], refs[-2:]
    rows, width = x_refs[0].shape
    for i, ref in enumerate(x_refs):
        x[i * rows : (i + 1) * rows, :] = ref[...]
    over_width = (((1,), (1,)), ((), ()))
    g = lax.dot_general(gate_ref[...], x[...], over_width, preferred_element_type=F32)
    u = lax.dot_general(up_ref[...], x[...], over_width, preferred_element_type=F32)
    act[...] = (g / (1.0 + jnp.exp(-g)) * u * scale_ref[...]).T.astype(BF16)
    block = min(1024, width)
    for start in range(0, width, block):
        lanes = slice(start, start + block)
        out = jnp.dot(act[...], down_ref[:, lanes], preferred_element_type=F32).astype(BF16)
        at = 0
        for ref in out_refs:
            ref[:, lanes] = out[at : at + ref.shape[0]]
            at += ref.shape[0]


def expert(xs, w_gate, w_up, w_down, loaded, scale):
    rows, width = xs[0].shape
    hidden = w_gate.shape[0]
    blocks = len(xs)
    out_rows = [rows] * blocks
    return pl.pallas_call(
        functools.partial(expert_kernel, blocks),
        in_specs=[whole()] * (blocks + 5),
        out_specs=[whole()] * len(out_rows),
        out_shape=[jax.ShapeDtypeStruct((r, width), BF16) for r in out_rows],
        scratch_shapes=[pltpu.VMEM((blocks * rows, width), BF16), pltpu.VMEM((blocks * rows, hidden), BF16)],
        compiler_params=pltpu.CompilerParams(vmem_limit_bytes=VMEM_LIMIT),
        cost_estimate=pl.CostEstimate(flops=1000, bytes_accessed=1000, transcendentals=0),
    )(*xs, w_gate, w_up, w_down, scale, loaded)


def call(kernel, out_shapes, *operands, scalars=0, far=0):
    fetched = operands[scalars : scalars + far]
    specs = [pl.BlockSpec(memory_space=pltpu.SMEM)] * scalars + [pl.BlockSpec(memory_space=pltpu.HBM)] * far
    operands = (
        operands[:scalars]
        + tuple(pltpu.with_memory_space_constraint(f, pltpu.HBM) for f in fetched)
        + operands[scalars + far :]
    )
    scratch = [pltpu.VMEM(f.shape, f.dtype) for f in fetched]
    return pl.pallas_call(
        kernel,
        in_specs=specs + [whole()] * (len(operands) - len(specs)),
        out_specs=[whole()] * len(out_shapes),
        out_shape=out_shapes,
        scratch_shapes=scratch + [pltpu.SemaphoreType.DMA((far,))] * (far > 0),
        compiler_params=pltpu.CompilerParams(vmem_limit_bytes=VMEM_LIMIT),
    )(*operands)


def shards(
    queries,
    keys,
    values,
    log_decay,
    doc_ids,
    residual,
    out_weight,
    norm_gain,
    expert_ids,
    route_weight,
    w_gate,
    w_up,
    w_down,
):
    n_seq, n_hx = lax.axis_size("seq"), lax.axis_size("hx")
    count = n_seq * n_hx
    inner = max(1, n_seq // 4)
    z_masks = bits(n_hx * inner, count)
    y_masks = bits(n_hx, n_hx * inner)
    x_masks = bits(2, n_hx)
    order_even = y_masks + x_masks
    order_odd = x_masks + y_masks if len(x_masks) == len(y_masks) else order_even
    net = list(zip(order_even, order_odd))
    core = (1, 1)
    hx_masks = [(m, m) for m in x_masks] + [core]
    hx_index = lax.axis_index("hx")
    device = lax.axis_index("seq") * n_hx + hx_index

    tok_count = queries.shape[0]
    own_count = tok_count // n_hx
    half_count = own_count // HALVES
    heads = log_decay.shape[1]
    chunk = heads * HS // n_seq

    decay_t, doc_row = log_decay.T, doc_ids.reshape(1, tok_count)
    shape = jax.ShapeDtypeStruct
    (payload,) = call(
        state_kernel,
        [shape((n_seq, chunk + EXTRA, HS), BF16)],
        hx_index.reshape(1), decay_t, doc_row, expert_ids.T, route_weight.T, keys, values,
        scalars=1, far=6,
    )
    arrived = lax.all_to_all(payload, "seq", split_axis=0, concat_axis=0, tiled=True)
    intra, query_weighted = call(
        intra_kernel,
        [shape((tok_count, heads * HS), F32), shape((tok_count, heads * HS), BF16)],
        decay_t, doc_row, queries, keys, values,
        far=5,
    )
    (incoming,) = call(prefix_kernel, [shape((n_seq, chunk, HS), BF16)], arrived)
    incoming = lax.all_to_all(incoming, "seq", split_axis=0, concat_axis=0, tiled=True)

    order = offsets([even for even, _ in hx_masks])

    def by_neighbour(x):
        blocks = [
            lax.dynamic_slice_in_dim(x, (hx_index ^ o) * own_count + i * half_count, half_count)
            for i in range(HALVES)
            for o in order
        ]
        return jnp.concatenate(blocks, axis=0)

    extra = arrived[:, chunk + 5 : chunk + 8, :].astype(F32)
    weights = jnp.sum(extra, axis=1).reshape(count, HALVES, half_count)
    units = {}
    for name, group in (("near", [0]), ("far", [z_masks[1]])):
        even = [o ^ g for g in group for o in offsets([z_masks[0]] + [m for m, _ in net])]
        odd = [o ^ g for g in group for o in offsets([z_masks[0]] + [m for _, m in net])]
        even, odd = even + [o ^ 1 for o in odd], odd + [o ^ 1 for o in even]
        units[name] = device ^ jnp.where(device & 1 == 1, jnp.array(odd), jnp.array(even))
    scale = {
        name + str(i): weights[rows, i].reshape(1, -1) for name, rows in units.items() for i in range(HALVES)
    }
    own_residual = lax.dynamic_slice_in_dim(residual, hx_index * own_count, own_count)
    wait = lax.optimization_barrier
    intra, query_weighted, scale, own_residual = wait(
        (by_neighbour(intra), by_neighbour(query_weighted), scale, own_residual)
    )

    (attn_in,) = call(
        attend_kernel,
        [shape((tok_count, heads * HS), BF16)],
        intra, query_weighted, incoming.reshape(heads, HS, HS),
    )
    projected = jnp.dot(attn_in, out_weight, preferred_element_type=F32).astype(BF16)

    def hx_send(i):
        rows = projected[i * n_hx * half_count : (i + 1) * n_hx * half_count]
        half = rows.shape[0] // 2
        return rows[:half], exchange(rows[half:], core, count)

    def hx_rest(rows, got):
        return reduce_rows(add(rows, got), hx_masks[:-1], count)

    def norm(i, rows, own_residual):
        hidden = own_residual[i * half_count : (i + 1) * half_count].astype(F32) + rows.astype(F32)
        normed = (
            hidden
            * lax.rsqrt(jnp.mean(hidden * hidden, axis=-1, keepdims=True) + 1e-06)
            * norm_gain
        ).astype(BF16)
        return hidden, normed

    def z_step(rows, mask):
        return exchange(rows, (mask, mask), count)

    def spread(unit):
        unit = gather_rows(unit, net[:-2], count)
        return [unit, exchange(unit, net[-2], count)]

    def joined(parts):
        return jnp.concatenate(parts, axis=0)

    def to_core(rows):
        return exchange(rows, core, count)

    def back(outs):
        mine, mine_last, other, other_last = outs
        return add(mine_last, to_core(other_last)), [mine, to_core(other)]

    def fold(terms, got):
        terms = terms + [got]
        for mask in reversed(net[:-1]):
            half = terms[0].shape[0] // 2
            sent = total([t[half:] for t in terms]).astype(BF16)
            terms = [total([t[:half] for t in terms]), exchange(sent, mask, count)]
        return total(terms)

    def deliver(hidden, rows):
        own = total([hidden, rows[:half_count]]).astype(BF16)
        across = rows[half_count:].astype(BF16)
        width = own.shape[1] // n_hx
        sums = {}
        for o in offsets([z_masks[0]] + x_masks + [1]):
            to = o % n_hx
            piece = across if o >= n_hx else own
            piece = lax.dynamic_slice_in_dim(piece, (hx_index ^ to) * width, width, axis=1)
            sums.setdefault(to, []).append(exchange(piece, (o, o), count) if o else piece)
        out = jnp.zeros((n_hx, half_count, width), BF16)
        for to, parts in sums.items():
            out = lax.dynamic_update_slice_in_dim(out, add(*parts)[None], hx_index ^ to, axis=0)
        return out

    last = net[-1]
    rows_a, got_a = hx_send(0)
    rows_b, got_b = hx_send(1)
    a = hx_rest(rows_a, got_a)
    a, rows_b, got_b, weights_in, scale, own_residual = wait(
        (a, rows_b, got_b, (w_gate, w_up, w_down), scale, own_residual)
    )
    hidden_a, a = norm(0, a, own_residual)
    w_gate, w_up, w_down = weights_in
    weights_in, loaded = load(jnp.swapaxes(w_gate, 1, 2), jnp.swapaxes(w_up, 1, 2), w_down)
    a1 = jnp.concatenate([a, z_step(a, z_masks[0])], axis=0)
    a1, rows_b, got_b, loaded = wait((a1, rows_b, got_b, loaded))
    a2 = z_step(a1, z_masks[1])
    a1 = spread(a1)
    b = hx_rest(rows_b, got_b)
    a1, a2, b, own_residual = wait((a1, a2, b, own_residual))
    a1 = joined(a1)
    a1_last, a1_other = exchange(a1, last, count), to_core(a1)
    a2 = spread(a2)
    hidden_b, b = norm(1, b, own_residual)
    b1 = jnp.concatenate([b, z_step(b, z_masks[0])], axis=0)
    a1, a1_last, a1_other, a2, b1 = wait((a1, a1_last, a1_other, a2, b1))
    a2 = joined(a2)
    a2_last, a2_other = exchange(a2, last, count), to_core(a2)
    a1_out = expert([a1, a1_last, a1_other, to_core(a1_last)], *weights_in, loaded, scale["near0"])
    b2 = z_step(b1, z_masks[1])
    b1 = spread(b1)
    a2, a2_last, a2_other, b1, b2, a1_out = wait((a2, a2_last, a2_other, b1, b2, a1_out))
    b1 = joined(b1)
    b1_last, b1_other = exchange(b1, last, count), to_core(b1)
    a2_out = expert([a2, a2_last, a2_other, to_core(a2_last)], *weights_in, loaded, scale["far0"])
    b2 = spread(b2)
    a1_send, a1_rest = back(a1_out)
    a2_send, a2_rest = back(a2_out)
    b1, b1_last, b1_other, b2, a1_send, a1_rest, a2_send, a2_rest = wait(
        (b1, b1_last, b1_other, b2, a1_send, a1_rest, a2_send, a2_rest)
    )
    b2 = joined(b2)
    b2_last, b2_other = exchange(b2, last, count), to_core(b2)
    a2_got = exchange(a2_send, last, count)
    b1_out = expert([b1, b1_last, b1_other, to_core(b1_last)], *weights_in, loaded, scale["near1"])
    b2, b2_last, b2_other, a2_got, b1_out, a1_send = wait((b2, b2_last, b2_other, a2_got, b1_out, a1_send))
    a1_got = exchange(a1_send, last, count)
    a2_sum = fold(a2_rest, a2_got)
    b2_out = expert([b2, b2_last, b2_other, to_core(b2_last)], *weights_in, loaded, scale["far1"])
    b1_send, b1_rest = back(b1_out)
    b2_send, b2_rest = back(b2_out)
    a2_sum, a1_got, b2_send, b2_rest, b1_send, b1_rest = wait(
        (a2_sum, a1_got, b2_send, b2_rest, b1_send, b1_rest)
    )
    a_z = z_step(a2_sum.astype(BF16), z_masks[1])
    a1_sum = fold(a1_rest, a1_got)
    b2_got = exchange(b2_send, last, count)
    a_sum = a1_sum + a_z.astype(F32)
    a_sum, b2_got, b1_send = wait((a_sum, b2_got, b1_send))
    a_z = z_step(a_sum[half_count:].astype(BF16), z_masks[0])
    b2_sum = fold(b2_rest, b2_got)
    b1_got = exchange(b1_send, last, count)
    a_out = total([hidden_a, a_sum[:half_count], a_z]).astype(BF16)
    a_out, b2_sum, b1_got = wait((a_out, b2_sum, b1_got))
    b_z = z_step(b2_sum.astype(BF16), z_masks[1])
    b1_sum = fold(b1_rest, b1_got)
    a_out = lax.all_to_all(a_out, "hx", split_axis=1, concat_axis=0, tiled=True)
    b_sum = b1_sum + b_z.astype(F32)
    b_sum, a_out = wait((b_sum, a_out))
    b_out = deliver(hidden_b, b_sum)
    outs = [o.reshape(n_hx, half_count, -1) for o in (a_out, b_out)]
    return jnp.concatenate(outs, axis=1).reshape(tok_count, -1)


def solution(mesh):
    return jax.shard_map(
        shards,
        mesh=mesh,
        in_specs=(
            P("seq", "hx"),
            P("seq", "hx"),
            P("seq", "hx"),
            P("seq", "hx"),
            P("seq"),
            P("seq", None),
            P("hx", None),
            P(),
            P("seq", None),
            P("seq", None),
            P("hx", None, "seq"),
            P("hx", None, "seq"),
            P("hx", "seq", None),
        ),
        out_specs=P("seq", "hx"),
        check_vma=False,
    )
```

```python
import functools

import jax
import jax.numpy as jnp
from jax import lax
from jax.experimental import pallas as pl
from jax.experimental.pallas import tpu as pltpu
from jax.sharding import PartitionSpec as P

HS = 128
AXES = ("seq", "hx")
HALVES = 2
EXTRA = 16
VMEM_LIMIT = 16 * 1024 * 1024
F32, BF16 = jnp.float32, jnp.bfloat16


def bits(low, high):
    out = []
    bit = high // 2
    while bit >= low:
        out.append(bit)
        bit //= 2
    return out


def exchange(x, mask, count):
    even, odd = mask
    pairs = [(d, d ^ (odd if d & 1 else even)) for d in range(count)]
    return lax.ppermute(x, AXES, pairs)


def total(parts):
    return functools.reduce(lambda a, b: a + b, [p.astype(F32) for p in parts])


def add(a, b):
    return total([a, b]).astype(BF16)


def gather_rows(x, masks, count):
    for mask in masks:
        x = jnp.concatenate([x, exchange(x, mask, count)], axis=0)
    return x


def reduce_rows(x, masks, count):
    for mask in reversed(masks):
        half = x.shape[0] // 2
        x = add(x[:half], exchange(x[half:], mask, count))
    return x


def offsets(masks):
    out = [0]
    for mask in masks:
        out = out + [o ^ mask for o in out]
    return out


def split3(x):
    high = x.astype(BF16)
    rest = x - high.astype(F32)
    mid = rest.astype(BF16)
    low = (rest - mid.astype(F32)).astype(BF16)
    return [high, mid, low]


def whole():
    return pl.BlockSpec(memory_space=pltpu.VMEM)


def over_last(a, b):
    return lax.dot_general(
        a, b, (((1,), (1,)), ((), ())), precision=lax.Precision.HIGHEST, preferred_element_type=F32
    )


def by_column(decay_t, doc_row):
    tok = doc_row.shape[1]
    row = lax.broadcasted_iota(jnp.int32, (tok, tok), 0)
    col = lax.broadcasted_iota(jnp.int32, (tok, tok), 1)
    doc_rows = jnp.broadcast_to(doc_row.astype(F32), (8, tok))
    log_cum = over_last((row >= col).astype(F32), decay_t)
    return log_cum, over_last((row == col).astype(F32), doc_rows)[:, :1]


def fetch(sources, targets, sems):
    copies = [pltpu.make_async_copy(s, t, sems.at[i]) for i, (s, t) in enumerate(zip(sources, targets))]
    for copy in copies:
        copy.start()
    return copies


def state_kernel(me_ref, *refs):
    sources, out_ref, targets, sems = refs[:6], refs[6], refs[7:13], refs[13]
    decay_ref, doc_ref, ids_ref, route_ref, k_ref, v_ref = targets
    copies = fetch(sources, targets, sems)
    for copy in copies[:4]:
        copy.wait()
    heads, tok = decay_ref.shape
    chunks = out_ref.shape[0]
    chunk = out_ref.shape[1] - EXTRA
    doc_row = doc_ref[...].astype(F32)
    log_cum, doc_col = by_column(decay_ref[...], doc_row)
    total = log_cum[tok - 1 : tok, :]
    first, last = doc_row[:, :1], doc_row[:, tok - 1 :]
    end_weight = jnp.exp(total - log_cum) * (doc_col == last).astype(F32)
    through = jnp.exp(total)
    weight = jnp.sum(jnp.where(ids_ref[...] == me_ref[0], route_ref[...], 0.0), axis=0, keepdims=True)
    row = lax.broadcasted_iota(jnp.int32, (EXTRA, HS), 0)
    fixed = [jnp.broadcast_to(w.astype(F32), (EXTRA, HS)) for w in [first, last] + split3(weight)]
    per_head = chunks // heads
    for copy in copies[4:]:
        copy.wait()
    for h in range(heads):
        lanes = slice(h * HS, (h + 1) * HS)
        weighted = (k_ref[:, lanes].astype(F32) * end_weight[:, h : h + 1]).astype(BF16)
        state = lax.dot_general(
            weighted, v_ref[:, lanes], (((0,), (0,)), ((), ())), preferred_element_type=F32
        ).astype(BF16)
        parts = [
            jnp.broadcast_to(p.astype(F32), (EXTRA, HS)) for p in split3(through[:, h : h + 1])
        ] + fixed
        extra = jnp.zeros((EXTRA, HS), F32)
        for i, part in enumerate(parts):
            extra = jnp.where(row == i, part, extra)
        for j in range(per_head):
            at = h * per_head + j
            out_ref[at, :chunk, :] = state[j * chunk : (j + 1) * chunk, :]
            out_ref[at, chunk:, :] = extra.astype(BF16)


def prefix_kernel(in_ref, out_ref):
    shards_n = in_ref.shape[0]
    chunk = out_ref.shape[1]
    carry = jnp.zeros((chunk, HS), F32)
    before = None
    for s in range(shards_n):
        extra = in_ref[s, chunk:, :].astype(F32)
        decay = extra[0:1] + extra[1:2] + extra[2:3]
        first, last = extra[3:4], extra[4:5]
        if s:
            out_ref[s] = (carry * (before == first).astype(F32)).astype(BF16)
            decay = decay * (before == last).astype(F32)
        else:
            out_ref[s] = carry.astype(BF16)
        carry = decay * carry + in_ref[s, :chunk, :].astype(F32)
        before = last


def intra_kernel(*refs):
    sources, (out_ref, qw_ref), targets, sems = refs[:5], refs[5:7], refs[7:12], refs[12]
    decay_ref, doc_ref, q_ref, k_ref, v_ref = targets
    copies = fetch(sources, targets, sems)
    for copy in copies[:2]:
        copy.wait()
    heads, tok = decay_ref.shape
    doc_row = doc_ref[...].astype(F32)
    log_cum, doc_col = by_column(decay_ref[...], doc_row)
    row = lax.broadcasted_iota(jnp.int32, (tok, tok), 0)
    col = lax.broadcasted_iota(jnp.int32, (tok, tok), 1)
    log_cum_t = jnp.dot(
        decay_ref[...], (row <= col).astype(F32), precision=lax.Precision.HIGHEST, preferred_element_type=F32
    )
    allowed = (row >= col) & (doc_col == doc_row)
    carry = jnp.exp(log_cum) * (doc_col == doc_row[:, :1]).astype(F32)
    for copy in copies[2:]:
        copy.wait()
    for h in range(heads):
        lanes = slice(h * HS, (h + 1) * HS)
        scores = lax.dot_general(
            q_ref[:, lanes], k_ref[:, lanes], (((1,), (1,)), ((), ())), preferred_element_type=F32
        )
        exponent = jnp.where(allowed, log_cum[:, h : h + 1] - log_cum_t[h : h + 1, :], -jnp.inf)
        weighted = (scores * jnp.exp(exponent)).astype(BF16)
        out_ref[:, lanes] = jnp.dot(weighted, v_ref[:, lanes], preferred_element_type=F32)
        qw_ref[:, lanes] = (q_ref[:, lanes].astype(F32) * carry[:, h : h + 1]).astype(BF16)


def attend_kernel(intra_ref, qw_ref, state_ref, out_ref):
    heads = state_ref.shape[0]
    for h in range(heads):
        lanes = slice(h * HS, (h + 1) * HS)
        head_out = intra_ref[:, lanes] + jnp.dot(
            qw_ref[:, lanes], state_ref[h], preferred_element_type=F32
        )
        scale = lax.rsqrt(jnp.mean(head_out * head_out, axis=-1, keepdims=True) + 1e-05)
        out_ref[:, lanes] = (head_out * scale).astype(BF16)


def load_kernel(*refs):
    count = (len(refs) - 2) // 2
    sems = refs[-1]
    copies = [
        pltpu.make_async_copy(refs[i].at[0], refs[count + i], sems.at[i]) for i in range(count)
    ]
    for copy in copies:
        copy.start()
    for copy in copies:
        copy.wait()
    refs[2 * count][...] = jnp.zeros_like(refs[2 * count])


def load(*weights):
    shapes = [w.shape[1:] for w in weights]
    weights = [pltpu.with_memory_space_constraint(w, pltpu.HBM) for w in weights]
    *loaded, done = pl.pallas_call(
        load_kernel,
        in_specs=[pl.BlockSpec(memory_space=pltpu.HBM)] * len(weights),
        out_specs=[whole()] * (len(weights) + 1),
        out_shape=[pltpu.VMEM(s, BF16) for s in shapes] + [jax.ShapeDtypeStruct((8, 128), F32)],
        scratch_shapes=[pltpu.SemaphoreType.DMA((len(weights),))],
        compiler_params=pltpu.CompilerParams(vmem_limit_bytes=VMEM_LIMIT),
    )(*weights)
    return loaded, done


def expert_kernel(blocks, *refs):
    x_refs, (gate_ref, up_ref, down_ref, scale_ref) = refs[:blocks], refs[blocks : blocks + 4]
    out_refs, (x, act) = refs[blocks + 5 : -2], refs[-2:]
    rows, width = x_refs[0].shape
    for i, ref in enumerate(x_refs):
        x[i * rows : (i + 1) * rows, :] = ref[...]
    over_width = (((1,), (1,)), ((), ()))
    g = lax.dot_general(gate_ref[...], x[...], over_width, preferred_element_type=F32)
    u = lax.dot_general(up_ref[...], x[...], over_width, preferred_element_type=F32)
    act[...] = (g / (1.0 + jnp.exp(-g)) * u * scale_ref[...]).T.astype(BF16)
    block = min(1024, width)
    for start in range(0, width, block):
        lanes = slice(start, start + block)
        out = jnp.dot(act[...], down_ref[:, lanes], preferred_element_type=F32).astype(BF16)
        at = 0
        for ref in out_refs:
            ref[:, lanes] = out[at : at + ref.shape[0]]
            at += ref.shape[0]


def expert(xs, w_gate, w_up, w_down, loaded, scale):
    rows, width = xs[0].shape
    hidden = w_gate.shape[0]
    blocks = len(xs)
    out_rows = [rows] * blocks
    return pl.pallas_call(
        functools.partial(expert_kernel, blocks),
        in_specs=[whole()] * (blocks + 5),
        out_specs=[whole()] * len(out_rows),
        out_shape=[jax.ShapeDtypeStruct((r, width), BF16) for r in out_rows],
        scratch_shapes=[pltpu.VMEM((blocks * rows, width), BF16), pltpu.VMEM((blocks * rows, hidden), BF16)],
        compiler_params=pltpu.CompilerParams(vmem_limit_bytes=VMEM_LIMIT),
        cost_estimate=pl.CostEstimate(flops=1000, bytes_accessed=1000, transcendentals=0),
    )(*xs, w_gate, w_up, w_down, scale, loaded)


def call(kernel, out_shapes, *operands, scalars=0, far=0):
    fetched = operands[scalars : scalars + far]
    specs = [pl.BlockSpec(memory_space=pltpu.SMEM)] * scalars + [pl.BlockSpec(memory_space=pltpu.HBM)] * far
    operands = (
        operands[:scalars]
        + tuple(pltpu.with_memory_space_constraint(f, pltpu.HBM) for f in fetched)
        + operands[scalars + far :]
    )
    scratch = [pltpu.VMEM(f.shape, f.dtype) for f in fetched]
    return pl.pallas_call(
        kernel,
        in_specs=specs + [whole()] * (len(operands) - len(specs)),
        out_specs=[whole()] * len(out_shapes),
        out_shape=out_shapes,
        scratch_shapes=scratch + [pltpu.SemaphoreType.DMA((far,))] * (far > 0),
        compiler_params=pltpu.CompilerParams(vmem_limit_bytes=VMEM_LIMIT),
    )(*operands)


def shards(
    queries,
    keys,
    values,
    log_decay,
    doc_ids,
    residual,
    out_weight,
    norm_gain,
    expert_ids,
    route_weight,
    w_gate,
    w_up,
    w_down,
):
    n_seq, n_hx = lax.axis_size("seq"), lax.axis_size("hx")
    count = n_seq * n_hx
    inner = max(1, n_seq // 4)
    z_masks = bits(n_hx * inner, count)
    y_masks = bits(n_hx, n_hx * inner)
    x_masks = bits(2, n_hx)
    order_even = y_masks + x_masks
    order_odd = x_masks + y_masks if len(x_masks) == len(y_masks) else order_even
    net = list(zip(order_even, order_odd))
    core = (1, 1)
    hx_masks = [(m, m) for m in x_masks] + [core]
    hx_index = lax.axis_index("hx")
    device = lax.axis_index("seq") * n_hx + hx_index

    tok_count = queries.shape[0]
    own_count = tok_count // n_hx
    half_count = own_count // HALVES
    heads = log_decay.shape[1]
    chunk = heads * HS // n_seq

    decay_t, doc_row = log_decay.T, doc_ids.reshape(1, tok_count)
    shape = jax.ShapeDtypeStruct
    (payload,) = call(
        state_kernel,
        [shape((n_seq, chunk + EXTRA, HS), BF16)],
        hx_index.reshape(1), decay_t, doc_row, expert_ids.T, route_weight.T, keys, values,
        scalars=1, far=6,
    )
    arrived = lax.all_to_all(payload, "seq", split_axis=0, concat_axis=0, tiled=True)
    intra, query_weighted = call(
        intra_kernel,
        [shape((tok_count, heads * HS), F32), shape((tok_count, heads * HS), BF16)],
        decay_t, doc_row, queries, keys, values,
        far=5,
    )
    (incoming,) = call(prefix_kernel, [shape((n_seq, chunk, HS), BF16)], arrived)
    incoming = lax.all_to_all(incoming, "seq", split_axis=0, concat_axis=0, tiled=True)

    order = offsets([even for even, _ in hx_masks])

    def by_neighbour(x):
        blocks = [
            lax.dynamic_slice_in_dim(x, (hx_index ^ o) * own_count + i * half_count, half_count)
            for i in range(HALVES)
            for o in order
        ]
        return jnp.concatenate(blocks, axis=0)

    extra = arrived[:, chunk + 5 : chunk + 8, :].astype(F32)
    weights = jnp.sum(extra, axis=1).reshape(count, HALVES, half_count)
    units = {}
    for name, group in (("near", [0]), ("far", [z_masks[1]])):
        even = [o ^ g for g in group for o in offsets([z_masks[0]] + [m for m, _ in net])]
        odd = [o ^ g for g in group for o in offsets([z_masks[0]] + [m for _, m in net])]
        even, odd = even + [o ^ 1 for o in odd], odd + [o ^ 1 for o in even]
        units[name] = device ^ jnp.where(device & 1 == 1, jnp.array(odd), jnp.array(even))
    scale = {
        name + str(i): weights[rows, i].reshape(1, -1) for name, rows in units.items() for i in range(HALVES)
    }
    own_residual = lax.dynamic_slice_in_dim(residual, hx_index * own_count, own_count)
    wait = lax.optimization_barrier
    intra, query_weighted, scale, own_residual = wait(
        (by_neighbour(intra), by_neighbour(query_weighted), scale, own_residual)
    )

    (attn_in,) = call(
        attend_kernel,
        [shape((tok_count, heads * HS), BF16)],
        intra, query_weighted, incoming.reshape(heads, HS, HS),
    )
    projected = jnp.dot(attn_in, out_weight, preferred_element_type=F32).astype(BF16)

    def hx_send(i):
        rows = projected[i * n_hx * half_count : (i + 1) * n_hx * half_count]
        half = rows.shape[0] // 2
        return rows[:half], exchange(rows[half:], core, count)

    def hx_rest(rows, got):
        return reduce_rows(add(rows, got), hx_masks[:-1], count)

    def norm(i, rows, own_residual):
        hidden = own_residual[i * half_count : (i + 1) * half_count].astype(F32) + rows.astype(F32)
        normed = (
            hidden
            * lax.rsqrt(jnp.mean(hidden * hidden, axis=-1, keepdims=True) + 1e-06)
            * norm_gain
        ).astype(BF16)
        return hidden, normed

    def z_step(rows, mask):
        return exchange(rows, (mask, mask), count)

    def spread(unit):
        unit = gather_rows(unit, net[:-2], count)
        return [unit, exchange(unit, net[-2], count)]

    def joined(parts):
        return jnp.concatenate(parts, axis=0)

    def to_core(rows):
        return exchange(rows, core, count)

    def back(outs):
        mine, mine_last, other, other_last = outs
        return add(mine_last, to_core(other_last)), [mine, to_core(other)]

    def fold(terms, got):
        terms = terms + [got]
        for mask in reversed(net[:-1]):
            half = terms[0].shape[0] // 2
            sent = total([t[half:] for t in terms]).astype(BF16)
            terms = [total([t[:half] for t in terms]), exchange(sent, mask, count)]
        return terms

    def deliver(own, across):
        width = own.shape[1] // n_hx
        sums = {}
        for o in offsets(([z_masks[0]] if across is not None else []) + x_masks + [1]):
            to = o % n_hx
            piece = across if o >= n_hx else own
            piece = lax.dynamic_slice_in_dim(piece, (hx_index ^ to) * width, width, axis=1)
            sums.setdefault(to, []).append(exchange(piece, (o, o), count) if o else piece)
        return {to: total(parts).astype(BF16) if len(parts) > 1 else parts[0] for to, parts in sums.items()}

    last = net[-1]
    rows_a, got_a = hx_send(0)
    rows_b, got_b = hx_send(1)
    a = hx_rest(rows_a, got_a)
    a, rows_b, got_b, weights_in, scale, own_residual = wait(
        (a, rows_b, got_b, (w_gate, w_up, w_down), scale, own_residual)
    )
    hidden_a, a = norm(0, a, own_residual)
    w_gate, w_up, w_down = weights_in
    weights_in, loaded = load(jnp.swapaxes(w_gate, 1, 2), jnp.swapaxes(w_up, 1, 2), w_down)
    a1 = jnp.concatenate([a, z_step(a, z_masks[0])], axis=0)
    a1, rows_b, got_b, loaded = wait((a1, rows_b, got_b, loaded))
    a2 = z_step(a1, z_masks[1])
    a1 = spread(a1)
    b = hx_rest(rows_b, got_b)
    a1, a2, b, own_residual = wait((a1, a2, b, own_residual))
    a1 = joined(a1)
    a1_last, a1_other = exchange(a1, last, count), to_core(a1)
    a2 = spread(a2)
    hidden_b, b = norm(1, b, own_residual)
    b1 = jnp.concatenate([b, z_step(b, z_masks[0])], axis=0)
    a1, a1_last, a1_other, a2, b1 = wait((a1, a1_last, a1_other, a2, b1))
    a2 = joined(a2)
    a2_last, a2_other = exchange(a2, last, count), to_core(a2)
    a1_out = expert([a1, a1_last, a1_other, to_core(a1_last)], *weights_in, loaded, scale["near0"])
    b2 = z_step(b1, z_masks[1])
    b1 = spread(b1)
    a2, a2_last, a2_other, b1, b2, a1_out = wait((a2, a2_last, a2_other, b1, b2, a1_out))
    b1 = joined(b1)
    b1_last, b1_other = exchange(b1, last, count), to_core(b1)
    a2_out = expert([a2, a2_last, a2_other, to_core(a2_last)], *weights_in, loaded, scale["far0"])
    b2 = spread(b2)
    a1_send, a1_rest = back(a1_out)
    a2_send, a2_rest = back(a2_out)
    b1, b1_last, b1_other, b2, a1_send, a1_rest, a2_send, a2_rest = wait(
        (b1, b1_last, b1_other, b2, a1_send, a1_rest, a2_send, a2_rest)
    )
    b2 = joined(b2)
    b2_last, b2_other = exchange(b2, last, count), to_core(b2)
    a2_got = exchange(a2_send, last, count)
    b1_out = expert([b1, b1_last, b1_other, to_core(b1_last)], *weights_in, loaded, scale["near1"])
    b2, b2_last, b2_other, a2_got, b1_out, a1_send = wait((b2, b2_last, b2_other, a2_got, b1_out, a1_send))
    a1_got = exchange(a1_send, last, count)
    a2_sum = fold(a2_rest, a2_got)
    b2_out = expert([b2, b2_last, b2_other, to_core(b2_last)], *weights_in, loaded, scale["far1"])
    b1_send, b1_rest = back(b1_out)
    b2_send, b2_rest = back(b2_out)
    a2_sum, a1_got, b2_send, b2_rest, b1_send, b1_rest = wait(
        (a2_sum, a1_got, b2_send, b2_rest, b1_send, b1_rest)
    )
    a_z = z_step(total(a2_sum).astype(BF16), z_masks[1])
    a1_sum = fold(a1_rest, a1_got)
    b2_got = exchange(b2_send, last, count)
    a_z, a1_sum, b2_got, b1_send = wait((a_z, a1_sum, b2_got, b1_send))
    b1_got = exchange(b1_send, last, count)
    a_sum = total(a1_sum + [a_z])
    a_z = z_step(a_sum[half_count:].astype(BF16), z_masks[0])
    b2_sum = fold(b2_rest, b2_got)
    a_z, a_sum, b2_sum, b1_got = wait((a_z, a_sum, b2_sum, b1_got))
    b_z = z_step(total(b2_sum).astype(BF16), z_masks[1])
    b1_sum = fold(b1_rest, b1_got)
    a_out = deliver(total([hidden_a, a_sum[:half_count], a_z]).astype(BF16), None)
    b_z, b1_sum, a_out = wait((b_z, b1_sum, a_out))
    b_sum = total(b1_sum + [b_z])
    b_out = deliver(total([hidden_b, b_sum[:half_count]]).astype(BF16), b_sum[half_count:].astype(BF16))
    out = jnp.zeros((n_hx, HALVES * half_count, b_sum.shape[1] // n_hx), BF16)
    for to in a_out:
        rows = jnp.concatenate([a_out[to], b_out[to]], axis=0)
        out = lax.dynamic_update_slice_in_dim(out, rows[None], hx_index ^ to, axis=0)
    return out.reshape(tok_count, -1)


def solution(mesh):
    return jax.shard_map(
        shards,
        mesh=mesh,
        in_specs=(
            P("seq", "hx"),
            P("seq", "hx"),
            P("seq", "hx"),
            P("seq", "hx"),
            P("seq"),
            P("seq", None),
            P("hx", None),
            P(),
            P("seq", None),
            P("seq", None),
            P("hx", None, "seq"),
            P("hx", None, "seq"),
            P("hx", "seq", None),
        ),
        out_specs=P("seq", "hx"),
        check_vma=False,
    )
```

```python
import functools

import jax
import jax.numpy as jnp
from jax import lax
from jax.experimental import pallas as pl
from jax.experimental.pallas import tpu as pltpu
from jax.sharding import PartitionSpec as P

HS = 128
AXES = ("seq", "hx")
HALVES = 2
EXTRA = 16
VMEM_LIMIT = 16 * 1024 * 1024
F32, BF16 = jnp.float32, jnp.bfloat16


def bits(low, high):
    out = []
    bit = high // 2
    while bit >= low:
        out.append(bit)
        bit //= 2
    return out


def exchange(x, mask, count):
    even, odd = mask
    pairs = [(d, d ^ (odd if d & 1 else even)) for d in range(count)]
    return lax.ppermute(x, AXES, pairs)


def total(parts):
    return functools.reduce(lambda a, b: a + b, [p.astype(F32) for p in parts])


def add(a, b):
    return total([a, b]).astype(BF16)


def gather_rows(x, masks, count):
    for mask in masks:
        x = jnp.concatenate([x, exchange(x, mask, count)], axis=0)
    return x


def reduce_rows(x, masks, count):
    for mask in reversed(masks):
        half = x.shape[0] // 2
        x = add(x[:half], exchange(x[half:], mask, count))
    return x


def offsets(masks):
    out = [0]
    for mask in masks:
        out = out + [o ^ mask for o in out]
    return out


def split3(x):
    high = x.astype(BF16)
    rest = x - high.astype(F32)
    mid = rest.astype(BF16)
    low = (rest - mid.astype(F32)).astype(BF16)
    return [high, mid, low]


def whole():
    return pl.BlockSpec(memory_space=pltpu.VMEM)


def over_last(a, b):
    return lax.dot_general(
        a, b, (((1,), (1,)), ((), ())), precision=lax.Precision.HIGHEST, preferred_element_type=F32
    )


def by_column(decay_t, doc_row):
    tok = doc_row.shape[1]
    row = lax.broadcasted_iota(jnp.int32, (tok, tok), 0)
    col = lax.broadcasted_iota(jnp.int32, (tok, tok), 1)
    doc_rows = jnp.broadcast_to(doc_row.astype(F32), (8, tok))
    log_cum = over_last((row >= col).astype(F32), decay_t)
    return log_cum, over_last((row == col).astype(F32), doc_rows)[:, :1]


def fetch(sources, targets, sems):
    copies = [pltpu.make_async_copy(s, t, sems.at[i]) for i, (s, t) in enumerate(zip(sources, targets))]
    for copy in copies:
        copy.start()
    return copies


def state_kernel(me_ref, *refs):
    sources, out_ref, targets, sems = refs[:6], refs[6], refs[7:13], refs[13]
    decay_ref, doc_ref, ids_ref, route_ref, k_ref, v_ref = targets
    copies = fetch(sources, targets, sems)
    for copy in copies[:4]:
        copy.wait()
    heads, tok = decay_ref.shape
    chunks = out_ref.shape[0]
    chunk = out_ref.shape[1] - EXTRA
    doc_row = doc_ref[...].astype(F32)
    log_cum, doc_col = by_column(decay_ref[...], doc_row)
    total = log_cum[tok - 1 : tok, :]
    first, last = doc_row[:, :1], doc_row[:, tok - 1 :]
    end_weight = jnp.exp(total - log_cum) * (doc_col == last).astype(F32)
    through = jnp.exp(total)
    weight = jnp.sum(jnp.where(ids_ref[...] == me_ref[0], route_ref[...], 0.0), axis=0, keepdims=True)
    row = lax.broadcasted_iota(jnp.int32, (EXTRA, HS), 0)
    fixed = [jnp.broadcast_to(w.astype(F32), (EXTRA, HS)) for w in [first, last] + split3(weight)]
    per_head = chunks // heads
    for copy in copies[4:]:
        copy.wait()
    for h in range(heads):
        lanes = slice(h * HS, (h + 1) * HS)
        weighted = (k_ref[:, lanes].astype(F32) * end_weight[:, h : h + 1]).astype(BF16)
        state = lax.dot_general(
            weighted, v_ref[:, lanes], (((0,), (0,)), ((), ())), preferred_element_type=F32
        ).astype(BF16)
        parts = [
            jnp.broadcast_to(p.astype(F32), (EXTRA, HS)) for p in split3(through[:, h : h + 1])
        ] + fixed
        extra = jnp.zeros((EXTRA, HS), F32)
        for i, part in enumerate(parts):
            extra = jnp.where(row == i, part, extra)
        for j in range(per_head):
            at = h * per_head + j
            out_ref[at, :chunk, :] = state[j * chunk : (j + 1) * chunk, :]
            out_ref[at, chunk:, :] = extra.astype(BF16)


def prefix_kernel(in_ref, out_ref):
    shards_n = in_ref.shape[0]
    chunk = out_ref.shape[1]
    carry = jnp.zeros((chunk, HS), F32)
    before = None
    for s in range(shards_n):
        extra = in_ref[s, chunk:, :].astype(F32)
        decay = extra[0:1] + extra[1:2] + extra[2:3]
        first, last = extra[3:4], extra[4:5]
        if s:
            out_ref[s] = (carry * (before == first).astype(F32)).astype(BF16)
            decay = decay * (before == last).astype(F32)
        else:
            out_ref[s] = carry.astype(BF16)
        carry = decay * carry + in_ref[s, :chunk, :].astype(F32)
        before = last


def intra_kernel(*refs):
    sources, (out_ref, qw_ref), targets, sems = refs[:5], refs[5:7], refs[7:12], refs[12]
    decay_ref, doc_ref, q_ref, k_ref, v_ref = targets
    copies = fetch(sources, targets, sems)
    for copy in copies[:2]:
        copy.wait()
    heads, tok = decay_ref.shape
    doc_row = doc_ref[...].astype(F32)
    log_cum, doc_col = by_column(decay_ref[...], doc_row)
    row = lax.broadcasted_iota(jnp.int32, (tok, tok), 0)
    col = lax.broadcasted_iota(jnp.int32, (tok, tok), 1)
    log_cum_t = jnp.dot(
        decay_ref[...], (row <= col).astype(F32), precision=lax.Precision.HIGHEST, preferred_element_type=F32
    )
    allowed = (row >= col) & (doc_col == doc_row)
    carry = jnp.exp(log_cum) * (doc_col == doc_row[:, :1]).astype(F32)
    for copy in copies[2:]:
        copy.wait()
    for h in range(heads):
        lanes = slice(h * HS, (h + 1) * HS)
        scores = lax.dot_general(
            q_ref[:, lanes], k_ref[:, lanes], (((1,), (1,)), ((), ())), preferred_element_type=F32
        )
        exponent = jnp.where(allowed, log_cum[:, h : h + 1] - log_cum_t[h : h + 1, :], -jnp.inf)
        weighted = (scores * jnp.exp(exponent)).astype(BF16)
        out_ref[:, lanes] = jnp.dot(weighted, v_ref[:, lanes], preferred_element_type=F32)
        qw_ref[:, lanes] = (q_ref[:, lanes].astype(F32) * carry[:, h : h + 1]).astype(BF16)


def attend_kernel(intra_ref, qw_ref, state_ref, out_ref):
    heads = state_ref.shape[0]
    for h in range(heads):
        lanes = slice(h * HS, (h + 1) * HS)
        head_out = intra_ref[:, lanes] + jnp.dot(
            qw_ref[:, lanes], state_ref[h], preferred_element_type=F32
        )
        scale = lax.rsqrt(jnp.mean(head_out * head_out, axis=-1, keepdims=True) + 1e-05)
        out_ref[:, lanes] = (head_out * scale).astype(BF16)


def load_kernel(*refs):
    count = (len(refs) - 2) // 2
    sems = refs[-1]
    copies = [
        pltpu.make_async_copy(refs[i].at[0], refs[count + i], sems.at[i]) for i in range(count)
    ]
    for copy in copies:
        copy.start()
    for copy in copies:
        copy.wait()
    refs[2 * count][...] = jnp.zeros_like(refs[2 * count])


def load(*weights):
    shapes = [w.shape[1:] for w in weights]
    weights = [pltpu.with_memory_space_constraint(w, pltpu.HBM) for w in weights]
    *loaded, done = pl.pallas_call(
        load_kernel,
        in_specs=[pl.BlockSpec(memory_space=pltpu.HBM)] * len(weights),
        out_specs=[whole()] * (len(weights) + 1),
        out_shape=[pltpu.VMEM(s, BF16) for s in shapes] + [jax.ShapeDtypeStruct((8, 128), F32)],
        scratch_shapes=[pltpu.SemaphoreType.DMA((len(weights),))],
        compiler_params=pltpu.CompilerParams(vmem_limit_bytes=VMEM_LIMIT),
    )(*weights)
    return loaded, done


def expert_kernel(blocks, *refs):
    x_refs, (gate_ref, up_ref, down_ref, scale_ref) = refs[:blocks], refs[blocks : blocks + 4]
    out_refs, (x, act) = refs[blocks + 5 : -2], refs[-2:]
    rows, width = x_refs[0].shape
    for i, ref in enumerate(x_refs):
        x[i * rows : (i + 1) * rows, :] = ref[...]
    over_width = (((1,), (1,)), ((), ()))
    g = lax.dot_general(gate_ref[...], x[...], over_width, preferred_element_type=F32)
    u = lax.dot_general(up_ref[...], x[...], over_width, preferred_element_type=F32)
    act[...] = (g / (1.0 + jnp.exp(-g)) * u * scale_ref[...]).T.astype(BF16)
    block = min(1024, width)
    for start in range(0, width, block):
        lanes = slice(start, start + block)
        out = jnp.dot(act[...], down_ref[:, lanes], preferred_element_type=F32).astype(BF16)
        at = 0
        for ref in out_refs:
            ref[:, lanes] = out[at : at + ref.shape[0]]
            at += ref.shape[0]


def expert(xs, w_gate, w_up, w_down, loaded, scale):
    rows, width = xs[0].shape
    hidden = w_gate.shape[0]
    blocks = len(xs)
    out_rows = [rows] * blocks
    return pl.pallas_call(
        functools.partial(expert_kernel, blocks),
        in_specs=[whole()] * (blocks + 5),
        out_specs=[whole()] * len(out_rows),
        out_shape=[jax.ShapeDtypeStruct((r, width), BF16) for r in out_rows],
        scratch_shapes=[pltpu.VMEM((blocks * rows, width), BF16), pltpu.VMEM((blocks * rows, hidden), BF16)],
        compiler_params=pltpu.CompilerParams(vmem_limit_bytes=VMEM_LIMIT),
        cost_estimate=pl.CostEstimate(flops=1000, bytes_accessed=1000, transcendentals=0),
    )(*xs, w_gate, w_up, w_down, scale, loaded)


def call(kernel, out_shapes, *operands, scalars=0, far=0):
    fetched = operands[scalars : scalars + far]
    specs = [pl.BlockSpec(memory_space=pltpu.SMEM)] * scalars + [pl.BlockSpec(memory_space=pltpu.HBM)] * far
    operands = (
        operands[:scalars]
        + tuple(pltpu.with_memory_space_constraint(f, pltpu.HBM) for f in fetched)
        + operands[scalars + far :]
    )
    scratch = [pltpu.VMEM(f.shape, f.dtype) for f in fetched]
    return pl.pallas_call(
        kernel,
        in_specs=specs + [whole()] * (len(operands) - len(specs)),
        out_specs=[whole()] * len(out_shapes),
        out_shape=out_shapes,
        scratch_shapes=scratch + [pltpu.SemaphoreType.DMA((far,))] * (far > 0),
        compiler_params=pltpu.CompilerParams(vmem_limit_bytes=VMEM_LIMIT),
    )(*operands)


def shards(
    queries,
    keys,
    values,
    log_decay,
    doc_ids,
    residual,
    out_weight,
    norm_gain,
    expert_ids,
    route_weight,
    w_gate,
    w_up,
    w_down,
):
    n_seq, n_hx = lax.axis_size("seq"), lax.axis_size("hx")
    count = n_seq * n_hx
    inner = max(1, n_seq // 4)
    z_masks = bits(n_hx * inner, count)
    y_masks = bits(n_hx, n_hx * inner)
    x_masks = bits(2, n_hx)
    order_even = y_masks + x_masks
    order_odd = x_masks + y_masks if len(x_masks) == len(y_masks) else order_even
    net = list(zip(order_even, order_odd))
    core = (1, 1)
    hx_masks = [(m, m) for m in x_masks] + [core]
    hx_index = lax.axis_index("hx")
    device = lax.axis_index("seq") * n_hx + hx_index

    tok_count = queries.shape[0]
    own_count = tok_count // n_hx
    half_count = own_count // HALVES
    heads = log_decay.shape[1]
    chunk = heads * HS // n_seq

    decay_t, doc_row = log_decay.T, doc_ids.reshape(1, tok_count)
    shape = jax.ShapeDtypeStruct
    (payload,) = call(
        state_kernel,
        [shape((n_seq, chunk + EXTRA, HS), BF16)],
        hx_index.reshape(1), decay_t, doc_row, expert_ids.T, route_weight.T, keys, values,
        scalars=1, far=6,
    )
    arrived = lax.all_to_all(payload, "seq", split_axis=0, concat_axis=0, tiled=True)
    intra, query_weighted = call(
        intra_kernel,
        [shape((tok_count, heads * HS), F32), shape((tok_count, heads * HS), BF16)],
        decay_t, doc_row, queries, keys, values,
        far=5,
    )
    (incoming,) = call(prefix_kernel, [shape((n_seq, chunk, HS), BF16)], arrived)
    incoming = lax.all_to_all(incoming, "seq", split_axis=0, concat_axis=0, tiled=True)

    order = offsets([even for even, _ in hx_masks])

    def by_neighbour(x):
        blocks = [
            lax.dynamic_slice_in_dim(x, (hx_index ^ o) * own_count + i * half_count, half_count)
            for i in range(HALVES)
            for o in order
        ]
        return jnp.concatenate(blocks, axis=0)

    extra = arrived[:, chunk + 5 : chunk + 8, :].astype(F32)
    weights = jnp.sum(extra, axis=1).reshape(count, HALVES, half_count)
    units = {}
    for name, group in (("near", [0]), ("far", [z_masks[1]])):
        even = [o ^ g for g in group for o in offsets([z_masks[0]] + [m for m, _ in net])]
        odd = [o ^ g for g in group for o in offsets([z_masks[0]] + [m for _, m in net])]
        even, odd = even + [o ^ 1 for o in odd], odd + [o ^ 1 for o in even]
        units[name] = device ^ jnp.where(device & 1 == 1, jnp.array(odd), jnp.array(even))
    scale = {
        name + str(i): weights[rows, i].reshape(1, -1) for name, rows in units.items() for i in range(HALVES)
    }
    own_residual = lax.dynamic_slice_in_dim(residual, hx_index * own_count, own_count)
    wait = lax.optimization_barrier
    intra, query_weighted, scale, own_residual = wait(
        (by_neighbour(intra), by_neighbour(query_weighted), scale, own_residual)
    )

    (attn_in,) = call(
        attend_kernel,
        [shape((tok_count, heads * HS), BF16)],
        intra, query_weighted, incoming.reshape(heads, HS, HS),
    )
    projected = jnp.dot(attn_in, out_weight, preferred_element_type=F32).astype(BF16)

    def hx_send(i):
        rows = projected[i * n_hx * half_count : (i + 1) * n_hx * half_count]
        half = rows.shape[0] // 2
        return rows[:half], exchange(rows[half:], core, count)

    def hx_rest(rows, got):
        return reduce_rows(add(rows, got), hx_masks[:-1], count)

    def norm(i, rows, own_residual):
        hidden = own_residual[i * half_count : (i + 1) * half_count].astype(F32) + rows.astype(F32)
        normed = (
            hidden
            * lax.rsqrt(jnp.mean(hidden * hidden, axis=-1, keepdims=True) + 1e-06)
            * norm_gain
        ).astype(BF16)
        return hidden, normed

    def z_step(rows, mask):
        return exchange(rows, (mask, mask), count)

    def spread(unit):
        unit = gather_rows(unit, net[:-2], count)
        return [unit, exchange(unit, net[-2], count)]

    def alternate(a, b):
        blocks = [x.reshape(-1, 1, half_count, x.shape[1]) for x in (a, b)]
        return jnp.concatenate(blocks, axis=1).reshape(-1, a.shape[1])

    def joined(parts):
        return jnp.concatenate(parts, axis=0)

    def to_core(rows):
        return exchange(rows, core, count)

    def back(outs):
        mine, mine_last, other, other_last = outs
        return add(mine_last, to_core(other_last)), [mine, to_core(other)]

    def fold(terms, got):
        terms = terms + [got]
        for mask in reversed(net[:-1]):
            half = terms[0].shape[0] // 2
            sent = total([t[half:] for t in terms]).astype(BF16)
            terms = [total([t[:half] for t in terms]), exchange(sent, mask, count)]
        return terms

    def deliver(own, across):
        width = own.shape[1] // n_hx

        def piece(rows, to):
            return lax.dynamic_slice_in_dim(rows, (hx_index ^ to) * width, width, axis=1)

        group = offsets(x_masks + [1])
        sums = {to: [] for to in group}
        if across is not None:
            for to in group:
                sums[to].append(exchange(piece(across, to), (z_masks[0] ^ to,) * 2, count))
        sums[0].append(piece(own, 0))
        sums[1].append(to_core(piece(own, 1)))
        others = {to: piece(own, to) for to in group if to > 1}
        if across is not None:
            others, sums[1] = wait((others, sums[1]))
        for to, rows in others.items():
            sums[to].append(exchange(rows, (to, to), count))
        return {to: total(parts).astype(BF16) if len(parts) > 1 else parts[0] for to, parts in sums.items()}

    last = net[-1]
    rows_a, got_a = hx_send(0)
    rows_b, got_b = hx_send(1)
    a = hx_rest(rows_a, got_a)
    a, rows_b, got_b, weights_in, scale, own_residual = wait(
        (a, rows_b, got_b, (w_gate, w_up, w_down), scale, own_residual)
    )
    hidden_a, a = norm(0, a, own_residual)
    w_gate, w_up, w_down = weights_in
    weights_in, loaded = load(jnp.swapaxes(w_gate, 1, 2), jnp.swapaxes(w_up, 1, 2), w_down)
    a_z, a_own = z_step(a, z_masks[0]), spread(a)
    a, a_z, a_own, rows_b, got_b, loaded = wait((a, a_z, a_own, rows_b, got_b, loaded))
    a2 = z_step(joined([a, a_z]), z_masks[1])
    a_own = joined(a_own)
    a_own_last, a_z = exchange(a_own, last, count), spread(a_z)
    b = hx_rest(rows_b, got_b)
    a_own, a_own_last, a_z, a2, b, own_residual = wait((a_own, a_own_last, a_z, a2, b, own_residual))
    a_z = joined(a_z)
    a_z_last = exchange(a_z, last, count)
    a1 = alternate(a_own, a_z)
    a1_other = to_core(a1)
    a2 = spread(a2)
    hidden_b, b = norm(1, b, own_residual)
    b1 = jnp.concatenate([b, z_step(b, z_masks[0])], axis=0)
    a1, a_own_last, a_z_last, a1_other, a2, b1 = wait((a1, a_own_last, a_z_last, a1_other, a2, b1))
    a1_last = alternate(a_own_last, a_z_last)
    a2 = joined(a2)
    a2_last, a2_other = exchange(a2, last, count), to_core(a2)
    a1_out = expert([a1, a1_last, a1_other, to_core(a1_last)], *weights_in, loaded, scale["near0"])
    b2 = z_step(b1, z_masks[1])
    b1 = spread(b1)
    a2, a2_last, a2_other, b1, b2, a1_out = wait((a2, a2_last, a2_other, b1, b2, a1_out))
    b1 = joined(b1)
    b1_last, b1_other = exchange(b1, last, count), to_core(b1)
    a2_out = expert([a2, a2_last, a2_other, to_core(a2_last)], *weights_in, loaded, scale["far0"])
    b2 = spread(b2)
    a1_send, a1_rest = back(a1_out)
    a2_send, a2_rest = back(a2_out)
    b1, b1_last, b1_other, b2, a1_send, a1_rest, a2_send, a2_rest = wait(
        (b1, b1_last, b1_other, b2, a1_send, a1_rest, a2_send, a2_rest)
    )
    b2 = joined(b2)
    b2_last, b2_other = exchange(b2, last, count), to_core(b2)
    a2_got = exchange(a2_send, last, count)
    b1_out = expert([b1, b1_last, b1_other, to_core(b1_last)], *weights_in, loaded, scale["near1"])
    b2, b2_last, b2_other, a2_got, b1_out, a1_send = wait((b2, b2_last, b2_other, a2_got, b1_out, a1_send))
    a1_got = exchange(a1_send, last, count)
    a2_sum = fold(a2_rest, a2_got)
    b2_out = expert([b2, b2_last, b2_other, to_core(b2_last)], *weights_in, loaded, scale["far1"])
    b1_send, b1_rest = back(b1_out)
    b2_send, b2_rest = back(b2_out)
    a2_sum, a1_got, b2_send, b2_rest, b1_send, b1_rest = wait(
        (a2_sum, a1_got, b2_send, b2_rest, b1_send, b1_rest)
    )
    a_z = z_step(total(a2_sum).astype(BF16), z_masks[1])
    a1_sum = fold(a1_rest, a1_got)
    b2_got = exchange(b2_send, last, count)
    a_z, a1_sum, b2_got, b1_send = wait((a_z, a1_sum, b2_got, b1_send))
    b1_got = exchange(b1_send, last, count)
    a_sum = a1_sum + [a_z]
    a_z = z_step(total([t[half_count:] for t in a_sum]).astype(BF16), z_masks[0])
    a_sum = total([t[:half_count] for t in a_sum])
    b2_sum = total(fold(b2_rest, b2_got)).astype(BF16)
    a_z, a_sum, b2_sum, b1_got = wait((a_z, a_sum, b2_sum, b1_got))
    b_z = z_step(b2_sum, z_masks[1])
    b1_sum = fold(b1_rest, b1_got)
    a_out = deliver(total([hidden_a, a_sum, a_z]).astype(BF16), None)
    b_z, b1_sum, a_out = wait((b_z, b1_sum, a_out))
    b_sum = b1_sum + [b_z]
    across = total([t[half_count:] for t in b_sum]).astype(BF16)
    b_out = deliver(total([hidden_b] + [t[:half_count] for t in b_sum]).astype(BF16), across)
    out = jnp.zeros((n_hx, HALVES * half_count, across.shape[1] // n_hx), BF16)
    for to in a_out:
        rows = jnp.concatenate([a_out[to], b_out[to]], axis=0)
        out = lax.dynamic_update_slice_in_dim(out, rows[None], hx_index ^ to, axis=0)
    return out.reshape(tok_count, -1)


def solution(mesh):
    return jax.shard_map(
        shards,
        mesh=mesh,
        in_specs=(
            P("seq", "hx"),
            P("seq", "hx"),
            P("seq", "hx"),
            P("seq", "hx"),
            P("seq"),
            P("seq", None),
            P("hx", None),
            P(),
            P("seq", None),
            P("seq", None),
            P("hx", None, "seq"),
            P("hx", None, "seq"),
            P("hx", "seq", None),
        ),
        out_specs=P("seq", "hx"),
        check_vma=False,
    )
```

```python
import functools

import jax
import jax.numpy as jnp
from jax import lax
from jax.experimental import pallas as pl
from jax.experimental.pallas import tpu as pltpu
from jax.sharding import PartitionSpec as P

HS = 128
AXES = ("seq", "hx")
HALVES = 2
EXTRA = 16
VMEM_LIMIT = 16 * 1024 * 1024
F32, BF16 = jnp.float32, jnp.bfloat16


def bits(low, high):
    out = []
    bit = high // 2
    while bit >= low:
        out.append(bit)
        bit //= 2
    return out


def exchange(x, mask, count):
    even, odd = mask
    pairs = [(d, d ^ (odd if d & 1 else even)) for d in range(count)]
    return lax.ppermute(x, AXES, pairs)


def total(parts):
    return functools.reduce(lambda a, b: a + b, [p.astype(F32) for p in parts])


def add(a, b):
    return total([a, b]).astype(BF16)


def gather_rows(x, masks, count):
    for mask in masks:
        x = jnp.concatenate([x, exchange(x, mask, count)], axis=0)
    return x


def reduce_rows(x, masks, count):
    for mask in reversed(masks):
        half = x.shape[0] // 2
        x = add(x[:half], exchange(x[half:], mask, count))
    return x


def offsets(masks):
    out = [0]
    for mask in masks:
        out = out + [o ^ mask for o in out]
    return out


def split3(x):
    high = x.astype(BF16)
    rest = x - high.astype(F32)
    mid = rest.astype(BF16)
    low = (rest - mid.astype(F32)).astype(BF16)
    return [high, mid, low]


def whole():
    return pl.BlockSpec(memory_space=pltpu.VMEM)


def over_last(a, b):
    return lax.dot_general(
        a, b, (((1,), (1,)), ((), ())), precision=lax.Precision.HIGHEST, preferred_element_type=F32
    )


def by_column(decay_t, doc_row):
    tok = doc_row.shape[1]
    row = lax.broadcasted_iota(jnp.int32, (tok, tok), 0)
    col = lax.broadcasted_iota(jnp.int32, (tok, tok), 1)
    doc_rows = jnp.broadcast_to(doc_row.astype(F32), (8, tok))
    log_cum = over_last((row >= col).astype(F32), decay_t)
    return log_cum, over_last((row == col).astype(F32), doc_rows)[:, :1]


def fetch(sources, targets, sems):
    copies = [pltpu.make_async_copy(s, t, sems.at[i]) for i, (s, t) in enumerate(zip(sources, targets))]
    for copy in copies:
        copy.start()
    return copies


def state_kernel(me_ref, *refs):
    sources, out_ref, targets, sems = refs[:6], refs[6], refs[7:13], refs[13]
    decay_ref, doc_ref, ids_ref, route_ref, k_ref, v_ref = targets
    copies = fetch(sources, targets, sems)
    for copy in copies[:4]:
        copy.wait()
    heads, tok = decay_ref.shape
    chunks = out_ref.shape[0]
    chunk = out_ref.shape[1] - EXTRA
    doc_row = doc_ref[...].astype(F32)
    log_cum, doc_col = by_column(decay_ref[...], doc_row)
    total = log_cum[tok - 1 : tok, :]
    first, last = doc_row[:, :1], doc_row[:, tok - 1 :]
    end_weight = jnp.exp(total - log_cum) * (doc_col == last).astype(F32)
    through = jnp.exp(total)
    weight = jnp.sum(jnp.where(ids_ref[...] == me_ref[0], route_ref[...], 0.0), axis=0, keepdims=True)
    row = lax.broadcasted_iota(jnp.int32, (EXTRA, HS), 0)
    fixed = [jnp.broadcast_to(w.astype(F32), (EXTRA, HS)) for w in [first, last] + split3(weight)]
    per_head = chunks // heads
    for copy in copies[4:]:
        copy.wait()
    for h in range(heads):
        lanes = slice(h * HS, (h + 1) * HS)
        weighted = (k_ref[:, lanes].astype(F32) * end_weight[:, h : h + 1]).astype(BF16)
        state = lax.dot_general(
            weighted, v_ref[:, lanes], (((0,), (0,)), ((), ())), preferred_element_type=F32
        ).astype(BF16)
        parts = [
            jnp.broadcast_to(p.astype(F32), (EXTRA, HS)) for p in split3(through[:, h : h + 1])
        ] + fixed
        extra = jnp.zeros((EXTRA, HS), F32)
        for i, part in enumerate(parts):
            extra = jnp.where(row == i, part, extra)
        for j in range(per_head):
            at = h * per_head + j
            out_ref[at, :chunk, :] = state[j * chunk : (j + 1) * chunk, :]
            out_ref[at, chunk:, :] = extra.astype(BF16)


def prefix_kernel(in_ref, out_ref):
    shards_n = in_ref.shape[0]
    chunk = out_ref.shape[1]
    carry = jnp.zeros((chunk, HS), F32)
    before = None
    for s in range(shards_n):
        extra = in_ref[s, chunk:, :].astype(F32)
        decay = extra[0:1] + extra[1:2] + extra[2:3]
        first, last = extra[3:4], extra[4:5]
        if s:
            out_ref[s] = (carry * (before == first).astype(F32)).astype(BF16)
            decay = decay * (before == last).astype(F32)
        else:
            out_ref[s] = carry.astype(BF16)
        carry = decay * carry + in_ref[s, :chunk, :].astype(F32)
        before = last


def intra_kernel(*refs):
    sources, (out_ref, qw_ref), targets, sems = refs[:5], refs[5:7], refs[7:12], refs[12]
    decay_ref, doc_ref, q_ref, k_ref, v_ref = targets
    copies = fetch(sources, targets, sems)
    for copy in copies[:2]:
        copy.wait()
    heads, tok = decay_ref.shape
    doc_row = doc_ref[...].astype(F32)
    log_cum, doc_col = by_column(decay_ref[...], doc_row)
    row = lax.broadcasted_iota(jnp.int32, (tok, tok), 0)
    col = lax.broadcasted_iota(jnp.int32, (tok, tok), 1)
    log_cum_t = jnp.dot(
        decay_ref[...], (row <= col).astype(F32), precision=lax.Precision.HIGHEST, preferred_element_type=F32
    )
    allowed = (row >= col) & (doc_col == doc_row)
    carry = jnp.exp(log_cum) * (doc_col == doc_row[:, :1]).astype(F32)
    for copy in copies[2:]:
        copy.wait()
    for h in range(heads):
        lanes = slice(h * HS, (h + 1) * HS)
        scores = lax.dot_general(
            q_ref[:, lanes], k_ref[:, lanes], (((1,), (1,)), ((), ())), preferred_element_type=F32
        )
        exponent = jnp.where(allowed, log_cum[:, h : h + 1] - log_cum_t[h : h + 1, :], -jnp.inf)
        weighted = (scores * jnp.exp(exponent)).astype(BF16)
        out_ref[:, lanes] = jnp.dot(weighted, v_ref[:, lanes], preferred_element_type=F32)
        qw_ref[:, lanes] = (q_ref[:, lanes].astype(F32) * carry[:, h : h + 1]).astype(BF16)


def attend_kernel(intra_ref, qw_ref, state_ref, out_ref):
    heads = state_ref.shape[0]
    for h in range(heads):
        lanes = slice(h * HS, (h + 1) * HS)
        head_out = intra_ref[:, lanes] + jnp.dot(
            qw_ref[:, lanes], state_ref[h], preferred_element_type=F32
        )
        scale = lax.rsqrt(jnp.mean(head_out * head_out, axis=-1, keepdims=True) + 1e-05)
        out_ref[:, lanes] = (head_out * scale).astype(BF16)


def load_kernel(*refs):
    count = (len(refs) - 2) // 2
    sems = refs[-1]
    copies = [
        pltpu.make_async_copy(refs[i].at[0], refs[count + i], sems.at[i]) for i in range(count)
    ]
    for copy in copies:
        copy.start()
    for copy in copies:
        copy.wait()
    refs[2 * count][...] = jnp.zeros_like(refs[2 * count])


def load(*weights):
    shapes = [w.shape[1:] for w in weights]
    weights = [pltpu.with_memory_space_constraint(w, pltpu.HBM) for w in weights]
    *loaded, done = pl.pallas_call(
        load_kernel,
        in_specs=[pl.BlockSpec(memory_space=pltpu.HBM)] * len(weights),
        out_specs=[whole()] * (len(weights) + 1),
        out_shape=[pltpu.VMEM(s, BF16) for s in shapes] + [jax.ShapeDtypeStruct((8, 128), F32)],
        scratch_shapes=[pltpu.SemaphoreType.DMA((len(weights),))],
        compiler_params=pltpu.CompilerParams(vmem_limit_bytes=VMEM_LIMIT),
    )(*weights)
    return loaded, done


def expert_kernel(blocks, *refs):
    x_refs, (gate_ref, up_ref, down_ref, scale_ref) = refs[:blocks], refs[blocks : blocks + 4]
    out_refs, (x, act) = refs[blocks + 5 : -2], refs[-2:]
    rows, width = x_refs[0].shape
    for i, ref in enumerate(x_refs):
        x[i * rows : (i + 1) * rows, :] = ref[...]
    over_width = (((1,), (1,)), ((), ()))
    g = lax.dot_general(gate_ref[...], x[...], over_width, preferred_element_type=F32)
    u = lax.dot_general(up_ref[...], x[...], over_width, preferred_element_type=F32)
    act[...] = (g / (1.0 + jnp.exp(-g)) * u * scale_ref[...]).T.astype(BF16)
    block = min(1024, width)
    for start in range(0, width, block):
        lanes = slice(start, start + block)
        out = jnp.dot(act[...], down_ref[:, lanes], preferred_element_type=F32).astype(BF16)
        at = 0
        for ref in out_refs:
            ref[:, lanes] = out[at : at + ref.shape[0]]
            at += ref.shape[0]


def expert(xs, w_gate, w_up, w_down, loaded, scale):
    rows, width = xs[0].shape
    hidden = w_gate.shape[0]
    blocks = len(xs)
    out_rows = [rows] * blocks
    return pl.pallas_call(
        functools.partial(expert_kernel, blocks),
        in_specs=[whole()] * (blocks + 5),
        out_specs=[whole()] * len(out_rows),
        out_shape=[jax.ShapeDtypeStruct((r, width), BF16) for r in out_rows],
        scratch_shapes=[pltpu.VMEM((blocks * rows, width), BF16), pltpu.VMEM((blocks * rows, hidden), BF16)],
        compiler_params=pltpu.CompilerParams(vmem_limit_bytes=VMEM_LIMIT),
        cost_estimate=pl.CostEstimate(flops=1000, bytes_accessed=1000, transcendentals=0),
    )(*xs, w_gate, w_up, w_down, scale, loaded)


def call(kernel, out_shapes, *operands, scalars=0, far=0):
    fetched = operands[scalars : scalars + far]
    specs = [pl.BlockSpec(memory_space=pltpu.SMEM)] * scalars + [pl.BlockSpec(memory_space=pltpu.HBM)] * far
    operands = (
        operands[:scalars]
        + tuple(pltpu.with_memory_space_constraint(f, pltpu.HBM) for f in fetched)
        + operands[scalars + far :]
    )
    scratch = [pltpu.VMEM(f.shape, f.dtype) for f in fetched]
    return pl.pallas_call(
        kernel,
        in_specs=specs + [whole()] * (len(operands) - len(specs)),
        out_specs=[whole()] * len(out_shapes),
        out_shape=out_shapes,
        scratch_shapes=scratch + [pltpu.SemaphoreType.DMA((far,))] * (far > 0),
        compiler_params=pltpu.CompilerParams(vmem_limit_bytes=VMEM_LIMIT),
    )(*operands)


def shards(
    queries,
    keys,
    values,
    log_decay,
    doc_ids,
    residual,
    out_weight,
    norm_gain,
    expert_ids,
    route_weight,
    w_gate,
    w_up,
    w_down,
):
    n_seq, n_hx = lax.axis_size("seq"), lax.axis_size("hx")
    count = n_seq * n_hx
    inner = max(1, n_seq // 4)
    z_masks = bits(n_hx * inner, count)
    y_masks = bits(n_hx, n_hx * inner)
    x_masks = bits(2, n_hx)
    order_even = y_masks + x_masks
    order_odd = x_masks + y_masks if len(x_masks) == len(y_masks) else order_even
    net = list(zip(order_even, order_odd))
    core = (1, 1)
    hx_masks = [(m, m) for m in x_masks] + [core]
    hx_index = lax.axis_index("hx")
    device = lax.axis_index("seq") * n_hx + hx_index

    tok_count = queries.shape[0]
    own_count = tok_count // n_hx
    half_count = own_count // HALVES
    heads = log_decay.shape[1]
    chunk = heads * HS // n_seq

    decay_t, doc_row = log_decay.T, doc_ids.reshape(1, tok_count)
    shape = jax.ShapeDtypeStruct
    (payload,) = call(
        state_kernel,
        [shape((n_seq, chunk + EXTRA, HS), BF16)],
        hx_index.reshape(1), decay_t, doc_row, expert_ids.T, route_weight.T, keys, values,
        scalars=1, far=6,
    )
    arrived = lax.all_to_all(payload, "seq", split_axis=0, concat_axis=0, tiled=True)
    intra, query_weighted = call(
        intra_kernel,
        [shape((tok_count, heads * HS), F32), shape((tok_count, heads * HS), BF16)],
        decay_t, doc_row, queries, keys, values,
        far=5,
    )
    (incoming,) = call(prefix_kernel, [shape((n_seq, chunk, HS), BF16)], arrived)
    incoming = lax.all_to_all(incoming, "seq", split_axis=0, concat_axis=0, tiled=True)

    order = offsets([even for even, _ in hx_masks])

    def by_neighbour(x):
        blocks = [
            lax.dynamic_slice_in_dim(x, (hx_index ^ o) * own_count + i * half_count, half_count)
            for i in range(HALVES)
            for o in order
        ]
        return jnp.concatenate(blocks, axis=0)

    extra = arrived[:, chunk + 5 : chunk + 8, :].astype(F32)
    weights = jnp.sum(extra, axis=1).reshape(count, HALVES, half_count)
    units = {}
    for name, group in (("near", [0]), ("far", [z_masks[1]])):
        even = [o ^ g for g in group for o in offsets([z_masks[0]] + [m for m, _ in net])]
        odd = [o ^ g for g in group for o in offsets([z_masks[0]] + [m for _, m in net])]
        even, odd = even + [o ^ 1 for o in odd], odd + [o ^ 1 for o in even]
        units[name] = device ^ jnp.where(device & 1 == 1, jnp.array(odd), jnp.array(even))
    scale = {
        name + str(i): weights[rows, i].reshape(1, -1) for name, rows in units.items() for i in range(HALVES)
    }
    own_residual = lax.dynamic_slice_in_dim(residual, hx_index * own_count, own_count)
    wait = lax.optimization_barrier
    intra, query_weighted, scale, own_residual = wait(
        (by_neighbour(intra), by_neighbour(query_weighted), scale, own_residual)
    )

    (attn_in,) = call(
        attend_kernel,
        [shape((tok_count, heads * HS), BF16)],
        intra, query_weighted, incoming.reshape(heads, HS, HS),
    )
    projected = jnp.dot(attn_in, out_weight, preferred_element_type=F32).astype(BF16)

    def hx_send(i):
        rows = projected[i * n_hx * half_count : (i + 1) * n_hx * half_count]
        half = rows.shape[0] // 2
        return rows[:half], exchange(rows[half:], core, count)

    def hx_rest(rows, got):
        return reduce_rows(add(rows, got), hx_masks[:-1], count)

    def norm(i, rows, own_residual):
        hidden = own_residual[i * half_count : (i + 1) * half_count].astype(F32) + rows.astype(F32)
        normed = (
            hidden
            * lax.rsqrt(jnp.mean(hidden * hidden, axis=-1, keepdims=True) + 1e-06)
            * norm_gain
        ).astype(BF16)
        return hidden, normed

    def z_step(rows, mask):
        return exchange(rows, (mask, mask), count)

    def spread(unit):
        unit = gather_rows(unit, net[:-2], count)
        return [unit, exchange(unit, net[-2], count)]

    def alternate(a, b):
        blocks = [x.reshape(-1, 1, half_count, x.shape[1]) for x in (a, b)]
        return jnp.concatenate(blocks, axis=1).reshape(-1, a.shape[1])

    def joined(parts):
        return jnp.concatenate(parts, axis=0)

    def to_core(rows):
        return exchange(rows, core, count)

    def back(outs):
        mine, mine_last, other, other_last = outs
        return add(mine_last, to_core(other_last)), [mine, to_core(other)]

    def fold(terms, got):
        terms = terms + [got]
        for mask in reversed(net[:-1]):
            half = terms[0].shape[0] // 2
            sent = total([t[half:] for t in terms]).astype(BF16)
            terms = [total([t[:half] for t in terms]), exchange(sent, mask, count)]
        return terms

    def deliver(own, across):
        width = own.shape[1] // n_hx

        def piece(rows, to):
            return lax.dynamic_slice_in_dim(rows, (hx_index ^ to) * width, width, axis=1)

        group = offsets(x_masks + [1])
        sums = {to: [] for to in group}
        if across is not None:
            for to in group:
                sums[to].append(exchange(piece(across, to), (z_masks[0] ^ to,) * 2, count))
        sums[0].append(piece(own, 0))
        sums[1].append(to_core(piece(own, 1)))
        others = {to: piece(own, to) for to in group if to > 1}
        if across is not None:
            others, sums[1] = wait((others, sums[1]))
        for to, rows in others.items():
            sums[to].append(exchange(rows, (to, to), count))
        return {to: total(parts).astype(BF16) if len(parts) > 1 else parts[0] for to, parts in sums.items()}

    last = net[-1]
    rows_a, got_a = hx_send(0)
    rows_b, got_b = hx_send(1)
    a = hx_rest(rows_a, got_a)
    a, rows_b, got_b, weights_in, scale, own_residual = wait(
        (a, rows_b, got_b, (w_gate, w_up, w_down), scale, own_residual)
    )
    hidden_a, a = norm(0, a, own_residual)
    w_gate, w_up, w_down = weights_in
    weights_in, loaded = load(jnp.swapaxes(w_gate, 1, 2), jnp.swapaxes(w_up, 1, 2), w_down)
    a_z, a_own = z_step(a, z_masks[0]), spread(a)
    a, a_z, a_own, rows_b, got_b, loaded = wait((a, a_z, a_own, rows_b, got_b, loaded))
    a2 = z_step(joined([a, a_z]), z_masks[1])
    a_own = joined(a_own)
    a_own_last, a_z = exchange(a_own, last, count), spread(a_z)
    b = hx_rest(rows_b, got_b)
    a_own, a_own_last, a_z, a2, b, own_residual = wait((a_own, a_own_last, a_z, a2, b, own_residual))
    a_z = joined(a_z)
    a_z_last = exchange(a_z, last, count)
    a1 = alternate(a_own, a_z)
    a1_other = to_core(a1)
    a2 = spread(a2)
    hidden_b, b = norm(1, b, own_residual)
    b1 = jnp.concatenate([b, z_step(b, z_masks[0])], axis=0)
    a1, a_own_last, a_z_last, a1_other, a2, b1 = wait((a1, a_own_last, a_z_last, a1_other, a2, b1))
    a1_last = alternate(a_own_last, a_z_last)
    a2 = joined(a2)
    a2_last, a2_other = exchange(a2, last, count), to_core(a2)
    a1_out = expert([a1, a1_last, a1_other, to_core(a1_last)], *weights_in, loaded, scale["near0"])
    b2 = z_step(b1, z_masks[1])
    b1 = spread(b1)
    a2, a2_last, a2_other, b1, b2, a1_out = wait((a2, a2_last, a2_other, b1, b2, a1_out))
    b2 = [gather_rows(b2, net[:-2], count), z_step(b1[1], z_masks[1])]
    b1 = joined(b1)
    b1_last, b1_other = exchange(b1, last, count), to_core(b1)
    a2_out = expert([a2, a2_last, a2_other, to_core(a2_last)], *weights_in, loaded, scale["far0"])
    a1_send, a1_rest = back(a1_out)
    a2_send, a2_rest = back(a2_out)
    b1, b1_last, b1_other, b2, a1_send, a1_rest, a2_send, a2_rest = wait(
        (b1, b1_last, b1_other, b2, a1_send, a1_rest, a2_send, a2_rest)
    )
    b2_last = [exchange(b2[0], last, count), z_step(b1_last[b1_last.shape[0] // 2 :], z_masks[1])]
    b2 = joined(b2)
    b2_other = to_core(b2)
    a2_got = exchange(a2_send, last, count)
    b1_out = expert([b1, b1_last, b1_other, to_core(b1_last)], *weights_in, loaded, scale["near1"])
    b2, b2_last, b2_other, a2_got, b1_out, a1_send = wait((b2, b2_last, b2_other, a2_got, b1_out, a1_send))
    b2_last = joined(b2_last)
    a1_got = exchange(a1_send, last, count)
    a2_sum = fold(a2_rest, a2_got)
    b2_out = expert([b2, b2_last, b2_other, to_core(b2_last)], *weights_in, loaded, scale["far1"])
    b1_send, b1_rest = back(b1_out)
    b2_send, b2_rest = back(b2_out)
    a2_sum, a1_got, b2_send, b2_rest, b1_send, b1_rest = wait(
        (a2_sum, a1_got, b2_send, b2_rest, b1_send, b1_rest)
    )
    a_z = z_step(total(a2_sum).astype(BF16), z_masks[1])
    a1_sum = fold(a1_rest, a1_got)
    b2_got = exchange(b2_send, last, count)
    a_z, a1_sum, b2_got, b1_send = wait((a_z, a1_sum, b2_got, b1_send))
    b1_got = exchange(b1_send, last, count)
    a_sum = a1_sum + [a_z]
    a_z = z_step(total([t[half_count:] for t in a_sum]).astype(BF16), z_masks[0])
    a_sum = total([t[:half_count] for t in a_sum])
    b2_sum = total(fold(b2_rest, b2_got)).astype(BF16)
    a_z, a_sum, b2_sum, b1_got = wait((a_z, a_sum, b2_sum, b1_got))
    b_z = z_step(b2_sum, z_masks[1])
    b1_sum = fold(b1_rest, b1_got)
    a_out = deliver(total([hidden_a, a_sum, a_z]).astype(BF16), None)
    b_z, b1_sum, a_out = wait((b_z, b1_sum, a_out))
    b_sum = b1_sum + [b_z]
    across = total([t[half_count:] for t in b_sum]).astype(BF16)
    b_out = deliver(total([hidden_b] + [t[:half_count] for t in b_sum]).astype(BF16), across)
    out = jnp.zeros((n_hx, HALVES * half_count, across.shape[1] // n_hx), BF16)
    for to in a_out:
        rows = jnp.concatenate([a_out[to], b_out[to]], axis=0)
        out = lax.dynamic_update_slice_in_dim(out, rows[None], hx_index ^ to, axis=0)
    return out.reshape(tok_count, -1)


def solution(mesh):
    return jax.shard_map(
        shards,
        mesh=mesh,
        in_specs=(
            P("seq", "hx"),
            P("seq", "hx"),
            P("seq", "hx"),
            P("seq", "hx"),
            P("seq"),
            P("seq", None),
            P("hx", None),
            P(),
            P("seq", None),
            P("seq", None),
            P("hx", None, "seq"),
            P("hx", None, "seq"),
            P("hx", "seq", None),
        ),
        out_specs=P("seq", "hx"),
        check_vma=False,
    )
```

```python
import functools

import jax
import jax.numpy as jnp
from jax import lax
from jax.experimental import pallas as pl
from jax.experimental.pallas import tpu as pltpu
from jax.sharding import PartitionSpec as P

HS = 128
AXES = ("seq", "hx")
HALVES = 2
EXTRA = 16
VMEM_LIMIT = 16 * 1024 * 1024
F32, BF16 = jnp.float32, jnp.bfloat16


def bits(low, high):
    out = []
    bit = high // 2
    while bit >= low:
        out.append(bit)
        bit //= 2
    return out


def exchange(x, mask, count):
    even, odd = mask
    pairs = [(d, d ^ (odd if d & 1 else even)) for d in range(count)]
    return lax.ppermute(x, AXES, pairs)


def total(parts):
    return functools.reduce(lambda a, b: a + b, [p.astype(F32) for p in parts])


def add(a, b):
    return total([a, b]).astype(BF16)


def gather_rows(x, masks, count):
    for mask in masks:
        x = jnp.concatenate([x, exchange(x, mask, count)], axis=0)
    return x


def reduce_rows(x, masks, count):
    for mask in reversed(masks):
        half = x.shape[0] // 2
        x = add(x[:half], exchange(x[half:], mask, count))
    return x


def offsets(masks):
    out = [0]
    for mask in masks:
        out = out + [o ^ mask for o in out]
    return out


def split3(x):
    high = x.astype(BF16)
    rest = x - high.astype(F32)
    mid = rest.astype(BF16)
    low = (rest - mid.astype(F32)).astype(BF16)
    return [high, mid, low]


def whole():
    return pl.BlockSpec(memory_space=pltpu.VMEM)


def over_last(a, b):
    return lax.dot_general(
        a, b, (((1,), (1,)), ((), ())), precision=lax.Precision.HIGHEST, preferred_element_type=F32
    )


def by_column(decay_t, doc_row):
    tok = doc_row.shape[1]
    row = lax.broadcasted_iota(jnp.int32, (tok, tok), 0)
    col = lax.broadcasted_iota(jnp.int32, (tok, tok), 1)
    doc_rows = jnp.broadcast_to(doc_row.astype(F32), (8, tok))
    log_cum = over_last((row >= col).astype(F32), decay_t)
    return log_cum, over_last((row == col).astype(F32), doc_rows)[:, :1]


def fetch(sources, targets, sems):
    copies = [pltpu.make_async_copy(s, t, sems.at[i]) for i, (s, t) in enumerate(zip(sources, targets))]
    for copy in copies:
        copy.start()
    return copies


def state_kernel(me_ref, *refs):
    sources, out_ref, targets, sems = refs[:6], refs[6], refs[7:13], refs[13]
    decay_ref, doc_ref, ids_ref, route_ref, k_ref, v_ref = targets
    copies = fetch(sources, targets, sems)
    for copy in copies[:4]:
        copy.wait()
    heads, tok = decay_ref.shape
    chunks = out_ref.shape[0]
    chunk = out_ref.shape[1] - EXTRA
    doc_row = doc_ref[...].astype(F32)
    log_cum, doc_col = by_column(decay_ref[...], doc_row)
    total = log_cum[tok - 1 : tok, :]
    first, last = doc_row[:, :1], doc_row[:, tok - 1 :]
    end_weight = jnp.exp(total - log_cum) * (doc_col == last).astype(F32)
    through = jnp.exp(total)
    weight = jnp.sum(jnp.where(ids_ref[...] == me_ref[0], route_ref[...], 0.0), axis=0, keepdims=True)
    row = lax.broadcasted_iota(jnp.int32, (EXTRA, HS), 0)
    fixed = [jnp.broadcast_to(w.astype(F32), (EXTRA, HS)) for w in [first, last] + split3(weight)]
    per_head = chunks // heads
    for copy in copies[4:]:
        copy.wait()
    for h in range(heads):
        lanes = slice(h * HS, (h + 1) * HS)
        weighted = (k_ref[:, lanes].astype(F32) * end_weight[:, h : h + 1]).astype(BF16)
        state = lax.dot_general(
            weighted, v_ref[:, lanes], (((0,), (0,)), ((), ())), preferred_element_type=F32
        ).astype(BF16)
        parts = [
            jnp.broadcast_to(p.astype(F32), (EXTRA, HS)) for p in split3(through[:, h : h + 1])
        ] + fixed
        extra = jnp.zeros((EXTRA, HS), F32)
        for i, part in enumerate(parts):
            extra = jnp.where(row == i, part, extra)
        for j in range(per_head):
            at = h * per_head + j
            out_ref[at, :chunk, :] = state[j * chunk : (j + 1) * chunk, :]
            out_ref[at, chunk:, :] = extra.astype(BF16)


def prefix_kernel(in_ref, out_ref):
    shards_n = in_ref.shape[0]
    chunk = out_ref.shape[1]
    carry = jnp.zeros((chunk, HS), F32)
    before = None
    for s in range(shards_n):
        extra = in_ref[s, chunk:, :].astype(F32)
        decay = extra[0:1] + extra[1:2] + extra[2:3]
        first, last = extra[3:4], extra[4:5]
        if s:
            out_ref[s] = (carry * (before == first).astype(F32)).astype(BF16)
            decay = decay * (before == last).astype(F32)
        else:
            out_ref[s] = carry.astype(BF16)
        carry = decay * carry + in_ref[s, :chunk, :].astype(F32)
        before = last


def intra_kernel(*refs):
    sources, (out_ref, qw_ref), targets, sems = refs[:5], refs[5:7], refs[7:12], refs[12]
    decay_ref, doc_ref, q_ref, k_ref, v_ref = targets
    copies = fetch(sources, targets, sems)
    for copy in copies[:2]:
        copy.wait()
    heads, tok = decay_ref.shape
    doc_row = doc_ref[...].astype(F32)
    log_cum, doc_col = by_column(decay_ref[...], doc_row)
    row = lax.broadcasted_iota(jnp.int32, (tok, tok), 0)
    col = lax.broadcasted_iota(jnp.int32, (tok, tok), 1)
    log_cum_t = jnp.dot(
        decay_ref[...], (row <= col).astype(F32), precision=lax.Precision.HIGHEST, preferred_element_type=F32
    )
    allowed = (row >= col) & (doc_col == doc_row)
    carry = jnp.exp(log_cum) * (doc_col == doc_row[:, :1]).astype(F32)
    for copy in copies[2:]:
        copy.wait()
    for h in range(heads):
        lanes = slice(h * HS, (h + 1) * HS)
        scores = lax.dot_general(
            q_ref[:, lanes], k_ref[:, lanes], (((1,), (1,)), ((), ())), preferred_element_type=F32
        )
        exponent = jnp.where(allowed, log_cum[:, h : h + 1] - log_cum_t[h : h + 1, :], -jnp.inf)
        weighted = (scores * jnp.exp(exponent)).astype(BF16)
        out_ref[:, lanes] = jnp.dot(weighted, v_ref[:, lanes], preferred_element_type=F32)
        qw_ref[:, lanes] = (q_ref[:, lanes].astype(F32) * carry[:, h : h + 1]).astype(BF16)


def attend_kernel(intra_ref, qw_ref, state_ref, out_ref):
    heads = state_ref.shape[0]
    for h in range(heads):
        lanes = slice(h * HS, (h + 1) * HS)
        head_out = intra_ref[:, lanes] + jnp.dot(
            qw_ref[:, lanes], state_ref[h], preferred_element_type=F32
        )
        scale = lax.rsqrt(jnp.mean(head_out * head_out, axis=-1, keepdims=True) + 1e-05)
        out_ref[:, lanes] = (head_out * scale).astype(BF16)


def load_kernel(*refs):
    count = (len(refs) - 2) // 2
    sems = refs[-1]
    copies = [
        pltpu.make_async_copy(refs[i].at[0], refs[count + i], sems.at[i]) for i in range(count)
    ]
    for copy in copies:
        copy.start()
    for copy in copies:
        copy.wait()
    refs[2 * count][...] = jnp.zeros_like(refs[2 * count])


def load(*weights):
    shapes = [w.shape[1:] for w in weights]
    weights = [pltpu.with_memory_space_constraint(w, pltpu.HBM) for w in weights]
    *loaded, done = pl.pallas_call(
        load_kernel,
        in_specs=[pl.BlockSpec(memory_space=pltpu.HBM)] * len(weights),
        out_specs=[whole()] * (len(weights) + 1),
        out_shape=[pltpu.VMEM(s, BF16) for s in shapes] + [jax.ShapeDtypeStruct((8, 128), F32)],
        scratch_shapes=[pltpu.SemaphoreType.DMA((len(weights),))],
        compiler_params=pltpu.CompilerParams(vmem_limit_bytes=VMEM_LIMIT),
    )(*weights)
    return loaded, done


def expert_kernel(blocks, *refs):
    x_refs, (gate_ref, up_ref, down_ref, scale_ref) = refs[:blocks], refs[blocks : blocks + 4]
    out_refs, (x, act) = refs[blocks + 5 : -2], refs[-2:]
    rows, width = x_refs[0].shape
    for i, ref in enumerate(x_refs):
        x[i * rows : (i + 1) * rows, :] = ref[...]
    over_width = (((1,), (1,)), ((), ()))
    g = lax.dot_general(gate_ref[...], x[...], over_width, preferred_element_type=F32)
    u = lax.dot_general(up_ref[...], x[...], over_width, preferred_element_type=F32)
    act[...] = (g / (1.0 + jnp.exp(-g)) * u * scale_ref[...]).T.astype(BF16)
    block = min(1024, width)
    for start in range(0, width, block):
        lanes = slice(start, start + block)
        out = jnp.dot(act[...], down_ref[:, lanes], preferred_element_type=F32).astype(BF16)
        at = 0
        for ref in out_refs:
            ref[:, lanes] = out[at : at + ref.shape[0]]
            at += ref.shape[0]


def expert(xs, w_gate, w_up, w_down, loaded, scale):
    rows, width = xs[0].shape
    hidden = w_gate.shape[0]
    blocks = len(xs)
    out_rows = [rows] * blocks
    return pl.pallas_call(
        functools.partial(expert_kernel, blocks),
        in_specs=[whole()] * (blocks + 5),
        out_specs=[whole()] * len(out_rows),
        out_shape=[jax.ShapeDtypeStruct((r, width), BF16) for r in out_rows],
        scratch_shapes=[pltpu.VMEM((blocks * rows, width), BF16), pltpu.VMEM((blocks * rows, hidden), BF16)],
        compiler_params=pltpu.CompilerParams(vmem_limit_bytes=VMEM_LIMIT),
        cost_estimate=pl.CostEstimate(flops=1000, bytes_accessed=1000, transcendentals=0),
    )(*xs, w_gate, w_up, w_down, scale, loaded)


def call(kernel, out_shapes, *operands, scalars=0, far=0):
    fetched = operands[scalars : scalars + far]
    specs = [pl.BlockSpec(memory_space=pltpu.SMEM)] * scalars + [pl.BlockSpec(memory_space=pltpu.HBM)] * far
    operands = (
        operands[:scalars]
        + tuple(pltpu.with_memory_space_constraint(f, pltpu.HBM) for f in fetched)
        + operands[scalars + far :]
    )
    scratch = [pltpu.VMEM(f.shape, f.dtype) for f in fetched]
    return pl.pallas_call(
        kernel,
        in_specs=specs + [whole()] * (len(operands) - len(specs)),
        out_specs=[whole()] * len(out_shapes),
        out_shape=out_shapes,
        scratch_shapes=scratch + [pltpu.SemaphoreType.DMA((far,))] * (far > 0),
        compiler_params=pltpu.CompilerParams(vmem_limit_bytes=VMEM_LIMIT),
    )(*operands)


def shards(
    queries,
    keys,
    values,
    log_decay,
    doc_ids,
    residual,
    out_weight,
    norm_gain,
    expert_ids,
    route_weight,
    w_gate,
    w_up,
    w_down,
):
    n_seq, n_hx = lax.axis_size("seq"), lax.axis_size("hx")
    count = n_seq * n_hx
    inner = max(1, n_seq // 4)
    z_masks = bits(n_hx * inner, count)
    y_masks = bits(n_hx, n_hx * inner)
    x_masks = bits(2, n_hx)
    order_even = y_masks + x_masks
    order_odd = x_masks + y_masks if len(x_masks) == len(y_masks) else order_even
    net = list(zip(order_even, order_odd))
    core = (1, 1)
    hx_masks = [(m, m) for m in x_masks] + [core]
    hx_index = lax.axis_index("hx")
    device = lax.axis_index("seq") * n_hx + hx_index

    tok_count = queries.shape[0]
    own_count = tok_count // n_hx
    half_count = own_count // HALVES
    heads = log_decay.shape[1]
    chunk = heads * HS // n_seq

    decay_t, doc_row = log_decay.T, doc_ids.reshape(1, tok_count)
    shape = jax.ShapeDtypeStruct
    (payload,) = call(
        state_kernel,
        [shape((n_seq, chunk + EXTRA, HS), BF16)],
        hx_index.reshape(1), decay_t, doc_row, expert_ids.T, route_weight.T, keys, values,
        scalars=1, far=6,
    )
    arrived = lax.all_to_all(payload, "seq", split_axis=0, concat_axis=0, tiled=True)
    intra, query_weighted = call(
        intra_kernel,
        [shape((tok_count, heads * HS), F32), shape((tok_count, heads * HS), BF16)],
        decay_t, doc_row, queries, keys, values,
        far=5,
    )
    (incoming,) = call(prefix_kernel, [shape((n_seq, chunk, HS), BF16)], arrived)
    incoming = lax.all_to_all(incoming, "seq", split_axis=0, concat_axis=0, tiled=True)

    order = offsets([even for even, _ in hx_masks])

    def by_neighbour(x):
        blocks = [
            lax.dynamic_slice_in_dim(x, (hx_index ^ o) * own_count + i * half_count, half_count)
            for i in range(HALVES)
            for o in order
        ]
        return jnp.concatenate(blocks, axis=0)

    extra = arrived[:, chunk + 5 : chunk + 8, :].astype(F32)
    weights = jnp.sum(extra, axis=1).reshape(count, HALVES, half_count)
    units = {}
    for name, group in (("near", [0]), ("far", [z_masks[1]])):
        even = [o ^ g for g in group for o in offsets([z_masks[0]] + [m for m, _ in net])]
        odd = [o ^ g for g in group for o in offsets([z_masks[0]] + [m for _, m in net])]
        even, odd = even + [o ^ 1 for o in odd], odd + [o ^ 1 for o in even]
        units[name] = device ^ jnp.where(device & 1 == 1, jnp.array(odd), jnp.array(even))
    scale = {
        name + str(i): weights[rows, i].reshape(1, -1) for name, rows in units.items() for i in range(HALVES)
    }
    own_residual = lax.dynamic_slice_in_dim(residual, hx_index * own_count, own_count)
    wait = lax.optimization_barrier
    intra, query_weighted, scale, own_residual = wait(
        (by_neighbour(intra), by_neighbour(query_weighted), scale, own_residual)
    )

    (attn_in,) = call(
        attend_kernel,
        [shape((tok_count, heads * HS), BF16)],
        intra, query_weighted, incoming.reshape(heads, HS, HS),
    )
    projected = jnp.dot(attn_in, out_weight, preferred_element_type=F32).astype(BF16)

    def hx_send(i):
        rows = projected[i * n_hx * half_count : (i + 1) * n_hx * half_count]
        half = rows.shape[0] // 2
        return rows[:half], exchange(rows[half:], core, count)

    def hx_rest(rows, got):
        return reduce_rows(add(rows, got), hx_masks[:-1], count)

    def norm(i, rows, own_residual):
        hidden = own_residual[i * half_count : (i + 1) * half_count].astype(F32) + rows.astype(F32)
        normed = (
            hidden
            * lax.rsqrt(jnp.mean(hidden * hidden, axis=-1, keepdims=True) + 1e-06)
            * norm_gain
        ).astype(BF16)
        return hidden, normed

    def z_step(rows, mask):
        return exchange(rows, (mask, mask), count)

    def spread(unit):
        unit = gather_rows(unit, net[:-2], count)
        return [unit, exchange(unit, net[-2], count)]

    def alternate(a, b):
        blocks = [x.reshape(-1, 1, half_count, x.shape[1]) for x in (a, b)]
        return jnp.concatenate(blocks, axis=1).reshape(-1, a.shape[1])

    def joined(parts):
        return jnp.concatenate(parts, axis=0)

    def to_core(rows):
        return exchange(rows, core, count)

    def back(outs):
        mine, mine_last, other, other_last = outs
        return add(mine_last, to_core(other_last)), [mine, to_core(other)]

    def fold_sums(terms):
        half = terms[0].shape[0] // 2
        return total([t[:half] for t in terms]), total([t[half:] for t in terms]).astype(BF16)

    def fold(stays, sent, masks):
        terms = [stays, exchange(sent, masks[-1], count)]
        for mask in reversed(masks[:-1]):
            stays, sent = fold_sums(terms)
            terms = [stays, exchange(sent, mask, count)]
        return terms

    def deliver(own, across):
        width = own.shape[1] // n_hx

        def piece(rows, to):
            return lax.dynamic_slice_in_dim(rows, (hx_index ^ to) * width, width, axis=1)

        group = offsets(x_masks + [1])
        sums = {to: [] for to in group}
        if across is not None:
            for to in group:
                sums[to].append(exchange(piece(across, to), (z_masks[0] ^ to,) * 2, count))
        sums[0].append(piece(own, 0))
        sums[1].append(to_core(piece(own, 1)))
        others = {to: piece(own, to) for to in group if to > 1}
        if across is not None:
            others, sums[1] = wait((others, sums[1]))
        for to, rows in others.items():
            sums[to].append(exchange(rows, (to, to), count))
        return {to: total(parts).astype(BF16) if len(parts) > 1 else parts[0] for to, parts in sums.items()}

    last = net[-1]
    rows_a, got_a = hx_send(0)
    rows_b, got_b = hx_send(1)
    a = hx_rest(rows_a, got_a)
    a, rows_b, got_b, weights_in, scale, own_residual = wait(
        (a, rows_b, got_b, (w_gate, w_up, w_down), scale, own_residual)
    )
    hidden_a, a = norm(0, a, own_residual)
    w_gate, w_up, w_down = weights_in
    weights_in, loaded = load(jnp.swapaxes(w_gate, 1, 2), jnp.swapaxes(w_up, 1, 2), w_down)
    a_z, a_own = z_step(a, z_masks[0]), spread(a)
    a, a_z, a_own, rows_b, got_b, loaded = wait((a, a_z, a_own, rows_b, got_b, loaded))
    a2 = z_step(joined([a, a_z]), z_masks[1])
    a_own = joined(a_own)
    a_own_last, a_z = exchange(a_own, last, count), spread(a_z)
    b = hx_rest(rows_b, got_b)
    a_own, a_own_last, a_z, a2, b, own_residual = wait((a_own, a_own_last, a_z, a2, b, own_residual))
    a_z = joined(a_z)
    a_z_last = exchange(a_z, last, count)
    a1 = alternate(a_own, a_z)
    a1_other = to_core(a1)
    a2 = spread(a2)
    hidden_b, b = norm(1, b, own_residual)
    b1 = jnp.concatenate([b, z_step(b, z_masks[0])], axis=0)
    a1, a_own_last, a_z_last, a1_other, a2, b1 = wait((a1, a_own_last, a_z_last, a1_other, a2, b1))
    a1_last = alternate(a_own_last, a_z_last)
    a2 = joined(a2)
    a2_last, a2_other = exchange(a2, last, count), to_core(a2)
    a1_out = expert([a1, a1_last, a1_other, to_core(a1_last)], *weights_in, loaded, scale["near0"])
    b2 = z_step(b1, z_masks[1])
    b1 = spread(b1)
    a2, a2_last, a2_other, b1, b2, a1_out = wait((a2, a2_last, a2_other, b1, b2, a1_out))
    b2 = [gather_rows(b2, net[:-2], count), z_step(b1[1], z_masks[1])]
    b1 = joined(b1)
    b1_last, b1_other = exchange(b1, last, count), to_core(b1)
    a2_out = expert([a2, a2_last, a2_other, to_core(a2_last)], *weights_in, loaded, scale["far0"])
    a1_send, a1_rest = back(a1_out)
    a2_send, a2_rest = back(a2_out)
    b1, b1_last, b1_other, b2, a1_send, a1_rest, a2_send, a2_rest = wait(
        (b1, b1_last, b1_other, b2, a1_send, a1_rest, a2_send, a2_rest)
    )
    b2_last = [exchange(b2[0], last, count), z_step(b1_last[b1_last.shape[0] // 2 :], z_masks[1])]
    b2 = joined(b2)
    b2_other = to_core(b2)
    a2_got = exchange(a2_send, last, count)
    b1_out = expert([b1, b1_last, b1_other, to_core(b1_last)], *weights_in, loaded, scale["near1"])
    b2, b2_last, b2_other, a2_got, b1_out, a1_send = wait((b2, b2_last, b2_other, a2_got, b1_out, a1_send))
    b2_last = joined(b2_last)
    steps = net[:-1]
    a1_got = exchange(a1_send, last, count)
    a2_stays, a2_sent = fold_sums(a2_rest + [a2_got])
    a2_across = z_step(a2_sent, z_masks[1])
    b2_out = expert([b2, b2_last, b2_other, to_core(b2_last)], *weights_in, loaded, scale["far1"])
    b1_send, b1_rest = back(b1_out)
    b2_send, b2_rest = back(b2_out)
    a2_stays, a2_across, a1_got, b2_send, b2_rest, b1_send, b1_rest = wait(
        (a2_stays, a2_across, a1_got, b2_send, b2_rest, b1_send, b1_rest)
    )
    for mask in reversed(steps[:-1]):
        a2_stays = total(fold(*fold_sums([a2_stays]), [mask]))
    a_z = z_step(a2_stays.astype(BF16), z_masks[1])
    half = a1_got.shape[0] // 2
    a1_sent = total([t[half:] for t in a1_rest + [a1_got]] + [a2_across]).astype(BF16)
    a1_sum = fold(total([t[:half] for t in a1_rest + [a1_got]]), a1_sent, steps)
    b2_got = exchange(b2_send, last, count)
    b2_parts = fold_sums(b2_rest + [b2_got])
    a_z, a1_sum, b2_parts, b1_send = wait((a_z, a1_sum, b2_parts, b1_send))
    b1_got = exchange(b1_send, last, count)
    b1_parts = fold_sums(b1_rest + [b1_got])
    a_sum = a1_sum + [a_z]
    a_z = z_step(total([t[half_count:] for t in a_sum]).astype(BF16), z_masks[0])
    a_sum = total([t[:half_count] for t in a_sum])
    b2_sum = total(fold(*b2_parts, steps)).astype(BF16)
    a_z, a_sum, b2_sum, b1_parts = wait((a_z, a_sum, b2_sum, b1_parts))
    b_z = z_step(b2_sum, z_masks[1])
    b1_sum = fold(*b1_parts, steps)
    a_out = deliver(total([hidden_a, a_sum, a_z]).astype(BF16), None)
    b_z, b1_sum, a_out = wait((b_z, b1_sum, a_out))
    b_sum = b1_sum + [b_z]
    across = total([t[half_count:] for t in b_sum]).astype(BF16)
    b_out = deliver(total([hidden_b] + [t[:half_count] for t in b_sum]).astype(BF16), across)
    out = jnp.zeros((n_hx, HALVES * half_count, across.shape[1] // n_hx), BF16)
    for to in a_out:
        rows = jnp.concatenate([a_out[to], b_out[to]], axis=0)
        out = lax.dynamic_update_slice_in_dim(out, rows[None], hx_index ^ to, axis=0)
    return out.reshape(tok_count, -1)


def solution(mesh):
    return jax.shard_map(
        shards,
        mesh=mesh,
        in_specs=(
            P("seq", "hx"),
            P("seq", "hx"),
            P("seq", "hx"),
            P("seq", "hx"),
            P("seq"),
            P("seq", None),
            P("hx", None),
            P(),
            P("seq", None),
            P("seq", None),
            P("hx", None, "seq"),
            P("hx", None, "seq"),
            P("hx", "seq", None),
        ),
        out_specs=P("seq", "hx"),
        check_vma=False,
    )
```

```python
import functools

import jax
import jax.numpy as jnp
from jax import lax
from jax.experimental import pallas as pl
from jax.experimental.pallas import tpu as pltpu
from jax.sharding import PartitionSpec as P

HS = 128
AXES = ("seq", "hx")
HALVES = 2
EXTRA = 16
VMEM_LIMIT = 16 * 1024 * 1024
F32, BF16 = jnp.float32, jnp.bfloat16


def bits(low, high):
    out = []
    bit = high // 2
    while bit >= low:
        out.append(bit)
        bit //= 2
    return out


def exchange(x, mask, count):
    even, odd = mask
    pairs = [(d, d ^ (odd if d & 1 else even)) for d in range(count)]
    return lax.ppermute(x, AXES, pairs)


def total(parts):
    return functools.reduce(lambda a, b: a + b, [p.astype(F32) for p in parts])


def add(a, b):
    return total([a, b]).astype(BF16)


def gather_rows(x, masks, count):
    for mask in masks:
        x = jnp.concatenate([x, exchange(x, mask, count)], axis=0)
    return x


def reduce_rows(x, masks, count):
    for mask in reversed(masks):
        half = x.shape[0] // 2
        x = add(x[:half], exchange(x[half:], mask, count))
    return x


def offsets(masks):
    out = [0]
    for mask in masks:
        out = out + [o ^ mask for o in out]
    return out


def split3(x):
    high = x.astype(BF16)
    rest = x - high.astype(F32)
    mid = rest.astype(BF16)
    low = (rest - mid.astype(F32)).astype(BF16)
    return [high, mid, low]


def whole():
    return pl.BlockSpec(memory_space=pltpu.VMEM)


def over_last(a, b):
    return lax.dot_general(
        a, b, (((1,), (1,)), ((), ())), precision=lax.Precision.HIGHEST, preferred_element_type=F32
    )


def by_column(decay_t, doc_row):
    tok = doc_row.shape[1]
    row = lax.broadcasted_iota(jnp.int32, (tok, tok), 0)
    col = lax.broadcasted_iota(jnp.int32, (tok, tok), 1)
    doc_rows = jnp.broadcast_to(doc_row.astype(F32), (8, tok))
    log_cum = over_last((row >= col).astype(F32), decay_t)
    return log_cum, over_last((row == col).astype(F32), doc_rows)[:, :1]


def fetch(sources, targets, sems):
    copies = [pltpu.make_async_copy(s, t, sems.at[i]) for i, (s, t) in enumerate(zip(sources, targets))]
    for copy in copies:
        copy.start()
    return copies


def state_kernel(me_ref, *refs):
    sources, out_ref, targets, sems = refs[:6], refs[6], refs[7:13], refs[13]
    decay_ref, doc_ref, ids_ref, route_ref, k_ref, v_ref = targets
    copies = fetch(sources, targets, sems)
    for copy in copies[:4]:
        copy.wait()
    heads, tok = decay_ref.shape
    chunks = out_ref.shape[0]
    chunk = out_ref.shape[1] - EXTRA
    doc_row = doc_ref[...].astype(F32)
    log_cum, doc_col = by_column(decay_ref[...], doc_row)
    total = log_cum[tok - 1 : tok, :]
    first, last = doc_row[:, :1], doc_row[:, tok - 1 :]
    end_weight = jnp.exp(total - log_cum) * (doc_col == last).astype(F32)
    through = jnp.exp(total)
    weight = jnp.sum(jnp.where(ids_ref[...] == me_ref[0], route_ref[...], 0.0), axis=0, keepdims=True)
    row = lax.broadcasted_iota(jnp.int32, (EXTRA, HS), 0)
    fixed = [jnp.broadcast_to(w.astype(F32), (EXTRA, HS)) for w in [first, last] + split3(weight)]
    per_head = chunks // heads
    for copy in copies[4:]:
        copy.wait()
    for h in range(heads):
        lanes = slice(h * HS, (h + 1) * HS)
        weighted = (k_ref[:, lanes].astype(F32) * end_weight[:, h : h + 1]).astype(BF16)
        state = lax.dot_general(
            weighted, v_ref[:, lanes], (((0,), (0,)), ((), ())), preferred_element_type=F32
        ).astype(BF16)
        parts = [
            jnp.broadcast_to(p.astype(F32), (EXTRA, HS)) for p in split3(through[:, h : h + 1])
        ] + fixed
        extra = jnp.zeros((EXTRA, HS), F32)
        for i, part in enumerate(parts):
            extra = jnp.where(row == i, part, extra)
        for j in range(per_head):
            at = h * per_head + j
            out_ref[at, :chunk, :] = state[j * chunk : (j + 1) * chunk, :]
            out_ref[at, chunk:, :] = extra.astype(BF16)


def prefix_kernel(in_ref, out_ref):
    shards_n = in_ref.shape[0]
    chunk = out_ref.shape[1]
    carry = jnp.zeros((chunk, HS), F32)
    before = None
    for s in range(shards_n):
        extra = in_ref[s, chunk:, :].astype(F32)
        decay = extra[0:1] + extra[1:2] + extra[2:3]
        first, last = extra[3:4], extra[4:5]
        if s:
            out_ref[s] = (carry * (before == first).astype(F32)).astype(BF16)
            decay = decay * (before == last).astype(F32)
        else:
            out_ref[s] = carry.astype(BF16)
        carry = decay * carry + in_ref[s, :chunk, :].astype(F32)
        before = last


def intra_kernel(*refs):
    sources, (out_ref, qw_ref), targets, sems = refs[:5], refs[5:7], refs[7:12], refs[12]
    decay_ref, doc_ref, q_ref, k_ref, v_ref = targets
    copies = fetch(sources, targets, sems)
    for copy in copies[:2]:
        copy.wait()
    heads, tok = decay_ref.shape
    doc_row = doc_ref[...].astype(F32)
    log_cum, doc_col = by_column(decay_ref[...], doc_row)
    row = lax.broadcasted_iota(jnp.int32, (tok, tok), 0)
    col = lax.broadcasted_iota(jnp.int32, (tok, tok), 1)
    log_cum_t = jnp.dot(
        decay_ref[...], (row <= col).astype(F32), precision=lax.Precision.HIGHEST, preferred_element_type=F32
    )
    allowed = (row >= col) & (doc_col == doc_row)
    carry = jnp.exp(log_cum) * (doc_col == doc_row[:, :1]).astype(F32)
    for copy in copies[2:]:
        copy.wait()
    for h in range(heads):
        lanes = slice(h * HS, (h + 1) * HS)
        scores = lax.dot_general(
            q_ref[:, lanes], k_ref[:, lanes], (((1,), (1,)), ((), ())), preferred_element_type=F32
        )
        exponent = jnp.where(allowed, log_cum[:, h : h + 1] - log_cum_t[h : h + 1, :], -jnp.inf)
        weighted = (scores * jnp.exp(exponent)).astype(BF16)
        out_ref[:, lanes] = jnp.dot(weighted, v_ref[:, lanes], preferred_element_type=F32)
        qw_ref[:, lanes] = (q_ref[:, lanes].astype(F32) * carry[:, h : h + 1]).astype(BF16)


def attend_kernel(intra_ref, qw_ref, state_ref, out_ref):
    heads = state_ref.shape[0]
    for h in range(heads):
        lanes = slice(h * HS, (h + 1) * HS)
        head_out = intra_ref[:, lanes] + jnp.dot(
            qw_ref[:, lanes], state_ref[h], preferred_element_type=F32
        )
        scale = lax.rsqrt(jnp.mean(head_out * head_out, axis=-1, keepdims=True) + 1e-05)
        out_ref[:, lanes] = (head_out * scale).astype(BF16)


def load_kernel(*refs):
    count = (len(refs) - 2) // 2
    sems = refs[-1]
    copies = [
        pltpu.make_async_copy(refs[i].at[0], refs[count + i], sems.at[i]) for i in range(count)
    ]
    for copy in copies:
        copy.start()
    for copy in copies:
        copy.wait()
    refs[2 * count][...] = jnp.zeros_like(refs[2 * count])


def load(*weights):
    shapes = [w.shape[1:] for w in weights]
    weights = [pltpu.with_memory_space_constraint(w, pltpu.HBM) for w in weights]
    *loaded, done = pl.pallas_call(
        load_kernel,
        in_specs=[pl.BlockSpec(memory_space=pltpu.HBM)] * len(weights),
        out_specs=[whole()] * (len(weights) + 1),
        out_shape=[pltpu.VMEM(s, BF16) for s in shapes] + [jax.ShapeDtypeStruct((8, 128), F32)],
        scratch_shapes=[pltpu.SemaphoreType.DMA((len(weights),))],
        compiler_params=pltpu.CompilerParams(vmem_limit_bytes=VMEM_LIMIT),
    )(*weights)
    return loaded, done


def expert_kernel(blocks, *refs):
    x_refs, (gate_ref, up_ref, down_ref, scale_ref) = refs[:blocks], refs[blocks : blocks + 4]
    out_refs, (x, act) = refs[blocks + 5 : -2], refs[-2:]
    rows, width = x_refs[0].shape
    for i, ref in enumerate(x_refs):
        x[i * rows : (i + 1) * rows, :] = ref[...]
    over_width = (((1,), (1,)), ((), ()))
    g = lax.dot_general(gate_ref[...], x[...], over_width, preferred_element_type=F32)
    u = lax.dot_general(up_ref[...], x[...], over_width, preferred_element_type=F32)
    act[...] = (g / (1.0 + jnp.exp(-g)) * u * scale_ref[...]).T.astype(BF16)
    block = min(1024, width)
    for start in range(0, width, block):
        lanes = slice(start, start + block)
        out = jnp.dot(act[...], down_ref[:, lanes], preferred_element_type=F32).astype(BF16)
        at = 0
        for ref in out_refs:
            ref[:, lanes] = out[at : at + ref.shape[0]]
            at += ref.shape[0]


def expert(xs, w_gate, w_up, w_down, loaded, scale):
    rows, width = xs[0].shape
    hidden = w_gate.shape[0]
    blocks = len(xs)
    out_rows = [rows] * blocks
    return pl.pallas_call(
        functools.partial(expert_kernel, blocks),
        in_specs=[whole()] * (blocks + 5),
        out_specs=[whole()] * len(out_rows),
        out_shape=[jax.ShapeDtypeStruct((r, width), BF16) for r in out_rows],
        scratch_shapes=[pltpu.VMEM((blocks * rows, width), BF16), pltpu.VMEM((blocks * rows, hidden), BF16)],
        compiler_params=pltpu.CompilerParams(vmem_limit_bytes=VMEM_LIMIT),
        cost_estimate=pl.CostEstimate(flops=1000, bytes_accessed=1000, transcendentals=0),
    )(*xs, w_gate, w_up, w_down, scale, loaded)


def call(kernel, out_shapes, *operands, scalars=0, far=0):
    fetched = operands[scalars : scalars + far]
    specs = [pl.BlockSpec(memory_space=pltpu.SMEM)] * scalars + [pl.BlockSpec(memory_space=pltpu.HBM)] * far
    operands = (
        operands[:scalars]
        + tuple(pltpu.with_memory_space_constraint(f, pltpu.HBM) for f in fetched)
        + operands[scalars + far :]
    )
    scratch = [pltpu.VMEM(f.shape, f.dtype) for f in fetched]
    return pl.pallas_call(
        kernel,
        in_specs=specs + [whole()] * (len(operands) - len(specs)),
        out_specs=[whole()] * len(out_shapes),
        out_shape=out_shapes,
        scratch_shapes=scratch + [pltpu.SemaphoreType.DMA((far,))] * (far > 0),
        compiler_params=pltpu.CompilerParams(vmem_limit_bytes=VMEM_LIMIT),
    )(*operands)


def shards(
    queries,
    keys,
    values,
    log_decay,
    doc_ids,
    residual,
    out_weight,
    norm_gain,
    expert_ids,
    route_weight,
    w_gate,
    w_up,
    w_down,
):
    n_seq, n_hx = lax.axis_size("seq"), lax.axis_size("hx")
    count = n_seq * n_hx
    inner = max(1, n_seq // 4)
    z_masks = bits(n_hx * inner, count)
    y_masks = bits(n_hx, n_hx * inner)
    x_masks = bits(2, n_hx)
    order_even = y_masks + x_masks
    order_odd = x_masks + y_masks if len(x_masks) == len(y_masks) else order_even
    net = list(zip(order_even, order_odd))
    core = (1, 1)
    hx_masks = [(m, m) for m in x_masks] + [core]
    hx_index = lax.axis_index("hx")
    device = lax.axis_index("seq") * n_hx + hx_index

    tok_count = queries.shape[0]
    own_count = tok_count // n_hx
    half_count = own_count // HALVES
    heads = log_decay.shape[1]
    chunk = heads * HS // n_seq

    decay_t, doc_row = log_decay.T, doc_ids.reshape(1, tok_count)
    shape = jax.ShapeDtypeStruct
    (payload,) = call(
        state_kernel,
        [shape((n_seq, chunk + EXTRA, HS), BF16)],
        hx_index.reshape(1), decay_t, doc_row, expert_ids.T, route_weight.T, keys, values,
        scalars=1, far=6,
    )
    arrived = lax.all_to_all(payload, "seq", split_axis=0, concat_axis=0, tiled=True)
    intra, query_weighted = call(
        intra_kernel,
        [shape((tok_count, heads * HS), F32), shape((tok_count, heads * HS), BF16)],
        decay_t, doc_row, queries, keys, values,
        far=5,
    )
    (incoming,) = call(prefix_kernel, [shape((n_seq, chunk, HS), BF16)], arrived)
    incoming = lax.all_to_all(incoming, "seq", split_axis=0, concat_axis=0, tiled=True)

    order = offsets([even for even, _ in hx_masks])

    def by_neighbour(x):
        blocks = [
            lax.dynamic_slice_in_dim(x, (hx_index ^ o) * own_count + i * half_count, half_count)
            for i in range(HALVES)
            for o in order
        ]
        return jnp.concatenate(blocks, axis=0)

    extra = arrived[:, chunk + 5 : chunk + 8, :].astype(F32)
    weights = jnp.sum(extra, axis=1).reshape(count, HALVES, half_count)
    units = {}
    for name, group in (("near", [0]), ("far", [z_masks[1]])):
        even = [o ^ g for g in group for o in offsets([z_masks[0]] + [m for m, _ in net])]
        odd = [o ^ g for g in group for o in offsets([z_masks[0]] + [m for _, m in net])]
        even, odd = even + [o ^ 1 for o in odd], odd + [o ^ 1 for o in even]
        units[name] = device ^ jnp.where(device & 1 == 1, jnp.array(odd), jnp.array(even))
    scale = {
        name + str(i): weights[rows, i].reshape(1, -1) for name, rows in units.items() for i in range(HALVES)
    }
    own_residual = lax.dynamic_slice_in_dim(residual, hx_index * own_count, own_count)
    wait = lax.optimization_barrier
    intra, query_weighted, scale, own_residual = wait(
        (by_neighbour(intra), by_neighbour(query_weighted), scale, own_residual)
    )

    (attn_in,) = call(
        attend_kernel,
        [shape((tok_count, heads * HS), BF16)],
        intra, query_weighted, incoming.reshape(heads, HS, HS),
    )
    projected = jnp.dot(attn_in, out_weight, preferred_element_type=F32).astype(BF16)

    def hx_send(i):
        rows = projected[i * n_hx * half_count : (i + 1) * n_hx * half_count]
        half = rows.shape[0] // 2
        return rows[:half], exchange(rows[half:], core, count)

    def hx_rest(rows, got):
        return reduce_rows(add(rows, got), hx_masks[:-1], count)

    def norm(i, rows, own_residual):
        hidden = own_residual[i * half_count : (i + 1) * half_count].astype(F32) + rows.astype(F32)
        normed = (
            hidden
            * lax.rsqrt(jnp.mean(hidden * hidden, axis=-1, keepdims=True) + 1e-06)
            * norm_gain
        ).astype(BF16)
        return hidden, normed

    def z_step(rows, mask):
        return exchange(rows, (mask, mask), count)

    def spread(unit):
        unit = gather_rows(unit, net[:-2], count)
        return [unit, exchange(unit, net[-2], count)]

    def alternate(a, b):
        blocks = [x.reshape(-1, 1, half_count, x.shape[1]) for x in (a, b)]
        return jnp.concatenate(blocks, axis=1).reshape(-1, a.shape[1])

    def joined(parts):
        return jnp.concatenate(parts, axis=0)

    def to_core(rows):
        return exchange(rows, core, count)

    def back(outs):
        mine, mine_last, other, other_last = outs
        return add(mine_last, to_core(other_last)), [mine, to_core(other)]

    def fold_sums(terms):
        half = terms[0].shape[0] // 2
        return total([t[:half] for t in terms]), total([t[half:] for t in terms]).astype(BF16)

    def fold(stays, sent, masks):
        terms = [stays, exchange(sent, masks[-1], count)]
        for mask in reversed(masks[:-1]):
            stays, sent = fold_sums(terms)
            terms = [stays, exchange(sent, mask, count)]
        return terms

    def deliver(own, across, place):
        width = own.shape[1] // n_hx

        def piece(rows, to):
            return lax.dynamic_slice_in_dim(rows, (place ^ to) * width, width, axis=1)

        group = offsets(x_masks + [1])
        sums = {to: [] for to in group}
        if across is not None:
            for to in group:
                sums[to].append(exchange(piece(across, to), (z_masks[0] ^ to,) * 2, count))
        sums[0].append(piece(own, 0))
        sums[1].append(to_core(piece(own, 1)))
        others = {to: piece(own, to) for to in group if to > 1}
        if across is not None:
            others, sums[1] = wait((others, sums[1]))
        for to, rows in others.items():
            sums[to].append(exchange(rows, (to, to), count))
        return {to: total(parts).astype(BF16) if len(parts) > 1 else parts[0] for to, parts in sums.items()}

    last = net[-1]
    rows_a, got_a = hx_send(0)
    rows_b, got_b = hx_send(1)
    a = hx_rest(rows_a, got_a)
    a, rows_b, got_b, weights_in, scale, own_residual = wait(
        (a, rows_b, got_b, (w_gate, w_up, w_down), scale, own_residual)
    )
    hidden_a, a = norm(0, a, own_residual)
    w_gate, w_up, w_down = weights_in
    weights_in, loaded = load(jnp.swapaxes(w_gate, 1, 2), jnp.swapaxes(w_up, 1, 2), w_down)
    a_z, a_own = z_step(a, z_masks[0]), spread(a)
    a, a_z, a_own, rows_b, got_b, loaded = wait((a, a_z, a_own, rows_b, got_b, loaded))
    a2 = z_step(joined([a, a_z]), z_masks[1])
    a_own = joined(a_own)
    a_own_last, a_z = exchange(a_own, last, count), spread(a_z)
    b = hx_rest(rows_b, got_b)
    a_own, a_own_last, a_z, a2, b, own_residual = wait((a_own, a_own_last, a_z, a2, b, own_residual))
    a_z = joined(a_z)
    a_z_last = exchange(a_z, last, count)
    a1 = alternate(a_own, a_z)
    a1_other = to_core(a1)
    a2 = spread(a2)
    hidden_b, b = norm(1, b, own_residual)
    b1 = jnp.concatenate([b, z_step(b, z_masks[0])], axis=0)
    a1, a_own_last, a_z_last, a1_other, a2, b1 = wait((a1, a_own_last, a_z_last, a1_other, a2, b1))
    a1_last = alternate(a_own_last, a_z_last)
    a2 = joined(a2)
    a2_last, a2_other = exchange(a2, last, count), to_core(a2)
    a1_out = expert([a1, a1_last, a1_other, to_core(a1_last)], *weights_in, loaded, scale["near0"])
    b2 = z_step(b1, z_masks[1])
    b1 = spread(b1)
    a2, a2_last, a2_other, b1, b2, a1_out = wait((a2, a2_last, a2_other, b1, b2, a1_out))
    b2 = [gather_rows(b2, net[:-2], count), z_step(b1[1], z_masks[1])]
    b1 = joined(b1)
    b1_last, b1_other = exchange(b1, last, count), to_core(b1)
    a2_out = expert([a2, a2_last, a2_other, to_core(a2_last)], *weights_in, loaded, scale["far0"])
    a1_send, a1_rest = back(a1_out)
    a2_send, a2_rest = back(a2_out)
    b1, b1_last, b1_other, b2, a1_send, a1_rest, a2_send, a2_rest = wait(
        (b1, b1_last, b1_other, b2, a1_send, a1_rest, a2_send, a2_rest)
    )
    b2_last = [exchange(b2[0], last, count), z_step(b1_last[b1_last.shape[0] // 2 :], z_masks[1])]
    b2 = joined(b2)
    b2_other = to_core(b2)
    a2_got = exchange(a2_send, last, count)
    b1_out = expert([b1, b1_last, b1_other, to_core(b1_last)], *weights_in, loaded, scale["near1"])
    b2, b2_last, b2_other, a2_got, b1_out, a1_send = wait((b2, b2_last, b2_other, a2_got, b1_out, a1_send))
    b2_last = joined(b2_last)
    steps = net[:-1]
    a1_got = exchange(a1_send, last, count)
    a2_stays, a2_sent = fold_sums(a2_rest + [a2_got])
    a2_across = z_step(a2_sent, z_masks[1])
    b2_out = expert([b2, b2_last, b2_other, to_core(b2_last)], *weights_in, loaded, scale["far1"])
    b1_send, b1_rest = back(b1_out)
    b2_send, b2_rest = back(b2_out)
    a2_stays, a2_across, a1_got, b2_send, b2_rest, b1_send, b1_rest = wait(
        (a2_stays, a2_across, a1_got, b2_send, b2_rest, b1_send, b1_rest)
    )
    for mask in reversed(steps[:-1]):
        a2_stays = total(fold(*fold_sums([a2_stays]), [mask]))
    a_z = z_step(a2_stays.astype(BF16), z_masks[1])
    half = a1_got.shape[0] // 2
    a1_sent = total([t[half:] for t in a1_rest + [a1_got]] + [a2_across]).astype(BF16)
    a1_sum = fold(total([t[:half] for t in a1_rest + [a1_got]]), a1_sent, steps)
    b2_got = exchange(b2_send, last, count)
    b2_parts = fold_sums(b2_rest + [b2_got])
    a_z, a1_sum, b2_parts, b1_send = wait((a_z, a1_sum, b2_parts, b1_send))
    b1_got = exchange(b1_send, last, count)
    b1_parts = fold_sums(b1_rest + [b1_got])
    a_sum = a1_sum + [a_z]
    a_z = z_step(total([t[half_count:] for t in a_sum]).astype(BF16), z_masks[0])
    a_sum = total([t[:half_count] for t in a_sum])
    b2_sum = total(fold(*b2_parts, steps)).astype(BF16)
    a_z, a_sum, b2_sum, b1_parts, place = wait((a_z, a_sum, b2_sum, b1_parts, hx_index))
    b_z = z_step(b2_sum, z_masks[1])
    b1_sum = fold(*b1_parts, steps)
    a_out = deliver(total([hidden_a, a_sum, a_z]).astype(BF16), None, place)
    b_z, b1_sum, a_out = wait((b_z, b1_sum, a_out))
    b_sum = b1_sum + [b_z]
    across = total([t[half_count:] for t in b_sum]).astype(BF16)
    b_out = deliver(total([hidden_b] + [t[:half_count] for t in b_sum]).astype(BF16), across, place)
    out = jnp.zeros((n_hx, HALVES * half_count, across.shape[1] // n_hx), BF16)
    for to in a_out:
        rows = jnp.concatenate([a_out[to], b_out[to]], axis=0)
        out = lax.dynamic_update_slice_in_dim(out, rows[None], place ^ to, axis=0)
    return out.reshape(tok_count, -1)


def solution(mesh):
    return jax.shard_map(
        shards,
        mesh=mesh,
        in_specs=(
            P("seq", "hx"),
            P("seq", "hx"),
            P("seq", "hx"),
            P("seq", "hx"),
            P("seq"),
            P("seq", None),
            P("hx", None),
            P(),
            P("seq", None),
            P("seq", None),
            P("hx", None, "seq"),
            P("hx", None, "seq"),
            P("hx", "seq", None),
        ),
        out_specs=P("seq", "hx"),
        check_vma=False,
    )
```

```python
import functools

import jax
import jax.numpy as jnp
from jax import lax
from jax.experimental import pallas as pl
from jax.experimental.pallas import tpu as pltpu
from jax.sharding import PartitionSpec as P

HS = 128
AXES = ("seq", "hx")
HALVES = 2
EXTRA = 16
VMEM_LIMIT = 16 * 1024 * 1024
F32, BF16 = jnp.float32, jnp.bfloat16


def bits(low, high):
    out = []
    bit = high // 2
    while bit >= low:
        out.append(bit)
        bit //= 2
    return out


def exchange(x, mask, count):
    even, odd = mask
    pairs = [(d, d ^ (odd if d & 1 else even)) for d in range(count)]
    return lax.ppermute(x, AXES, pairs)


def total(parts):
    return functools.reduce(lambda a, b: a + b, [p.astype(F32) for p in parts])


def add(a, b):
    return total([a, b]).astype(BF16)


def gather_rows(x, masks, count):
    for mask in masks:
        x = jnp.concatenate([x, exchange(x, mask, count)], axis=0)
    return x


def reduce_rows(x, masks, count):
    for mask in reversed(masks):
        half = x.shape[0] // 2
        x = add(x[:half], exchange(x[half:], mask, count))
    return x


def offsets(masks):
    out = [0]
    for mask in masks:
        out = out + [o ^ mask for o in out]
    return out


def split3(x):
    high = x.astype(BF16)
    rest = x - high.astype(F32)
    mid = rest.astype(BF16)
    low = (rest - mid.astype(F32)).astype(BF16)
    return [high, mid, low]


def whole():
    return pl.BlockSpec(memory_space=pltpu.VMEM)


def over_last(a, b):
    return lax.dot_general(
        a, b, (((1,), (1,)), ((), ())), precision=lax.Precision.HIGHEST, preferred_element_type=F32
    )


def by_column(decay_t, doc_row):
    tok = doc_row.shape[1]
    row = lax.broadcasted_iota(jnp.int32, (tok, tok), 0)
    col = lax.broadcasted_iota(jnp.int32, (tok, tok), 1)
    doc_rows = jnp.broadcast_to(doc_row.astype(F32), (8, tok))
    log_cum = over_last((row >= col).astype(F32), decay_t)
    return log_cum, over_last((row == col).astype(F32), doc_rows)[:, :1]


def fetch(sources, targets, sems):
    copies = [pltpu.make_async_copy(s, t, sems.at[i]) for i, (s, t) in enumerate(zip(sources, targets))]
    for copy in copies:
        copy.start()
    return copies


def state_kernel(me_ref, *refs):
    sources, out_ref, targets, sems = refs[:6], refs[6], refs[7:13], refs[13]
    decay_ref, doc_ref, ids_ref, route_ref, k_ref, v_ref = targets
    copies = fetch(sources, targets, sems)
    for copy in copies[:4]:
        copy.wait()
    heads, tok = decay_ref.shape
    chunks = out_ref.shape[0]
    chunk = out_ref.shape[1] - EXTRA
    doc_row = doc_ref[...].astype(F32)
    log_cum, doc_col = by_column(decay_ref[...], doc_row)
    total = log_cum[tok - 1 : tok, :]
    first, last = doc_row[:, :1], doc_row[:, tok - 1 :]
    end_weight = jnp.exp(total - log_cum) * (doc_col == last).astype(F32)
    through = jnp.exp(total)
    weight = jnp.sum(jnp.where(ids_ref[...] == me_ref[0], route_ref[...], 0.0), axis=0, keepdims=True)
    row = lax.broadcasted_iota(jnp.int32, (EXTRA, HS), 0)
    fixed = [jnp.broadcast_to(w.astype(F32), (EXTRA, HS)) for w in [first, last] + split3(weight)]
    per_head = chunks // heads
    for copy in copies[4:]:
        copy.wait()
    for h in range(heads):
        lanes = slice(h * HS, (h + 1) * HS)
        weighted = (k_ref[:, lanes].astype(F32) * end_weight[:, h : h + 1]).astype(BF16)
        state = lax.dot_general(
            weighted, v_ref[:, lanes], (((0,), (0,)), ((), ())), preferred_element_type=F32
        ).astype(BF16)
        parts = [
            jnp.broadcast_to(p.astype(F32), (EXTRA, HS)) for p in split3(through[:, h : h + 1])
        ] + fixed
        extra = jnp.zeros((EXTRA, HS), F32)
        for i, part in enumerate(parts):
            extra = jnp.where(row == i, part, extra)
        for j in range(per_head):
            at = h * per_head + j
            out_ref[at, :chunk, :] = state[j * chunk : (j + 1) * chunk, :]
            out_ref[at, chunk:, :] = extra.astype(BF16)


def prefix_kernel(in_ref, out_ref):
    shards_n = in_ref.shape[0]
    chunk = out_ref.shape[1]
    carry = jnp.zeros((chunk, HS), F32)
    before = None
    for s in range(shards_n):
        extra = in_ref[s, chunk:, :].astype(F32)
        decay = extra[0:1] + extra[1:2] + extra[2:3]
        first, last = extra[3:4], extra[4:5]
        if s:
            out_ref[s] = (carry * (before == first).astype(F32)).astype(BF16)
            decay = decay * (before == last).astype(F32)
        else:
            out_ref[s] = carry.astype(BF16)
        carry = decay * carry + in_ref[s, :chunk, :].astype(F32)
        before = last


def intra_kernel(*refs):
    sources, (out_ref, qw_ref), targets, sems = refs[:5], refs[5:7], refs[7:12], refs[12]
    decay_ref, doc_ref, q_ref, k_ref, v_ref = targets
    copies = fetch(sources, targets, sems)
    for copy in copies[:2]:
        copy.wait()
    heads, tok = decay_ref.shape
    doc_row = doc_ref[...].astype(F32)
    log_cum, doc_col = by_column(decay_ref[...], doc_row)
    row = lax.broadcasted_iota(jnp.int32, (tok, tok), 0)
    col = lax.broadcasted_iota(jnp.int32, (tok, tok), 1)
    log_cum_t = jnp.dot(
        decay_ref[...], (row <= col).astype(F32), precision=lax.Precision.HIGHEST, preferred_element_type=F32
    )
    allowed = (row >= col) & (doc_col == doc_row)
    carry = jnp.exp(log_cum) * (doc_col == doc_row[:, :1]).astype(F32)
    for copy in copies[2:]:
        copy.wait()
    for h in range(heads):
        lanes = slice(h * HS, (h + 1) * HS)
        scores = lax.dot_general(
            q_ref[:, lanes], k_ref[:, lanes], (((1,), (1,)), ((), ())), preferred_element_type=F32
        )
        exponent = jnp.where(allowed, log_cum[:, h : h + 1] - log_cum_t[h : h + 1, :], -jnp.inf)
        weighted = (scores * jnp.exp(exponent)).astype(BF16)
        out_ref[:, lanes] = jnp.dot(weighted, v_ref[:, lanes], preferred_element_type=F32)
        qw_ref[:, lanes] = (q_ref[:, lanes].astype(F32) * carry[:, h : h + 1]).astype(BF16)


def attend_kernel(intra_ref, qw_ref, state_ref, out_ref):
    heads = state_ref.shape[0]
    for h in range(heads):
        lanes = slice(h * HS, (h + 1) * HS)
        head_out = intra_ref[:, lanes] + jnp.dot(
            qw_ref[:, lanes], state_ref[h], preferred_element_type=F32
        )
        scale = lax.rsqrt(jnp.mean(head_out * head_out, axis=-1, keepdims=True) + 1e-05)
        out_ref[:, lanes] = (head_out * scale).astype(BF16)


def load_kernel(*refs):
    count = (len(refs) - 2) // 2
    sems = refs[-1]
    copies = [
        pltpu.make_async_copy(refs[i].at[0], refs[count + i], sems.at[i]) for i in range(count)
    ]
    for copy in copies:
        copy.start()
    for copy in copies:
        copy.wait()
    refs[2 * count][...] = jnp.zeros_like(refs[2 * count])


def load(*weights):
    shapes = [w.shape[1:] for w in weights]
    weights = [pltpu.with_memory_space_constraint(w, pltpu.HBM) for w in weights]
    *loaded, done = pl.pallas_call(
        load_kernel,
        in_specs=[pl.BlockSpec(memory_space=pltpu.HBM)] * len(weights),
        out_specs=[whole()] * (len(weights) + 1),
        out_shape=[pltpu.VMEM(s, BF16) for s in shapes] + [jax.ShapeDtypeStruct((8, 128), F32)],
        scratch_shapes=[pltpu.SemaphoreType.DMA((len(weights),))],
        compiler_params=pltpu.CompilerParams(vmem_limit_bytes=VMEM_LIMIT),
    )(*weights)
    return loaded, done


def expert_kernel(blocks, *refs):
    x_refs, (gate_ref, up_ref, down_ref, scale_ref) = refs[:blocks], refs[blocks : blocks + 4]
    out_refs, (x, act) = refs[blocks + 5 : -2], refs[-2:]
    rows, width = x_refs[0].shape
    for i, ref in enumerate(x_refs):
        x[i * rows : (i + 1) * rows, :] = ref[...]
    over_width = (((1,), (1,)), ((), ()))
    g = lax.dot_general(gate_ref[...], x[...], over_width, preferred_element_type=F32)
    u = lax.dot_general(up_ref[...], x[...], over_width, preferred_element_type=F32)
    act[...] = (g / (1.0 + jnp.exp(-g)) * u * scale_ref[...]).T.astype(BF16)
    block = min(1024, width)
    for start in range(0, width, block):
        lanes = slice(start, start + block)
        out = jnp.dot(act[...], down_ref[:, lanes], preferred_element_type=F32).astype(BF16)
        at = 0
        for ref in out_refs:
            ref[:, lanes] = out[at : at + ref.shape[0]]
            at += ref.shape[0]


def expert(xs, w_gate, w_up, w_down, loaded, scale):
    rows, width = xs[0].shape
    hidden = w_gate.shape[0]
    blocks = len(xs)
    out_rows = [rows] * blocks
    return pl.pallas_call(
        functools.partial(expert_kernel, blocks),
        in_specs=[whole()] * (blocks + 5),
        out_specs=[whole()] * len(out_rows),
        out_shape=[jax.ShapeDtypeStruct((r, width), BF16) for r in out_rows],
        scratch_shapes=[pltpu.VMEM((blocks * rows, width), BF16), pltpu.VMEM((blocks * rows, hidden), BF16)],
        compiler_params=pltpu.CompilerParams(vmem_limit_bytes=VMEM_LIMIT),
        cost_estimate=pl.CostEstimate(flops=1000, bytes_accessed=1000, transcendentals=0),
    )(*xs, w_gate, w_up, w_down, scale, loaded)


def call(kernel, out_shapes, *operands, scalars=0, far=0):
    fetched = operands[scalars : scalars + far]
    specs = [pl.BlockSpec(memory_space=pltpu.SMEM)] * scalars + [pl.BlockSpec(memory_space=pltpu.HBM)] * far
    operands = (
        operands[:scalars]
        + tuple(pltpu.with_memory_space_constraint(f, pltpu.HBM) for f in fetched)
        + operands[scalars + far :]
    )
    scratch = [pltpu.VMEM(f.shape, f.dtype) for f in fetched]
    return pl.pallas_call(
        kernel,
        in_specs=specs + [whole()] * (len(operands) - len(specs)),
        out_specs=[whole()] * len(out_shapes),
        out_shape=out_shapes,
        scratch_shapes=scratch + [pltpu.SemaphoreType.DMA((far,))] * (far > 0),
        compiler_params=pltpu.CompilerParams(vmem_limit_bytes=VMEM_LIMIT),
    )(*operands)


def shards(
    queries,
    keys,
    values,
    log_decay,
    doc_ids,
    residual,
    out_weight,
    norm_gain,
    expert_ids,
    route_weight,
    w_gate,
    w_up,
    w_down,
):
    n_seq, n_hx = lax.axis_size("seq"), lax.axis_size("hx")
    count = n_seq * n_hx
    inner = max(1, n_seq // 4)
    z_masks = bits(n_hx * inner, count)
    y_masks = bits(n_hx, n_hx * inner)
    x_masks = bits(2, n_hx)
    order_even = y_masks + x_masks
    order_odd = x_masks + y_masks if len(x_masks) == len(y_masks) else order_even
    net = list(zip(order_even, order_odd))
    core = (1, 1)
    hx_masks = [(m, m) for m in x_masks] + [core]
    hx_index = lax.axis_index("hx")
    device = lax.axis_index("seq") * n_hx + hx_index

    tok_count = queries.shape[0]
    own_count = tok_count // n_hx
    half_count = own_count // HALVES
    heads = log_decay.shape[1]
    chunk = heads * HS // n_seq

    decay_t, doc_row = log_decay.T, doc_ids.reshape(1, tok_count)
    shape = jax.ShapeDtypeStruct
    (payload,) = call(
        state_kernel,
        [shape((n_seq, chunk + EXTRA, HS), BF16)],
        hx_index.reshape(1), decay_t, doc_row, expert_ids.T, route_weight.T, keys, values,
        scalars=1, far=6,
    )
    arrived = lax.all_to_all(payload, "seq", split_axis=0, concat_axis=0, tiled=True)
    intra, query_weighted = call(
        intra_kernel,
        [shape((tok_count, heads * HS), F32), shape((tok_count, heads * HS), BF16)],
        decay_t, doc_row, queries, keys, values,
        far=5,
    )
    (incoming,) = call(prefix_kernel, [shape((n_seq, chunk, HS), BF16)], arrived)
    incoming = lax.all_to_all(incoming, "seq", split_axis=0, concat_axis=0, tiled=True)

    order = offsets([even for even, _ in hx_masks])

    def by_neighbour(x):
        blocks = [
            lax.dynamic_slice_in_dim(x, (hx_index ^ o) * own_count + i * half_count, half_count)
            for i in range(HALVES)
            for o in order
        ]
        return jnp.concatenate(blocks, axis=0)

    extra = arrived[:, chunk + 5 : chunk + 8, :].astype(F32)
    weights = jnp.sum(extra, axis=1).reshape(count, HALVES, half_count)
    units = {}
    for name, group in (("near", [0]), ("far", [z_masks[1]])):
        even = [o ^ g for g in group for o in offsets([z_masks[0]] + [m for m, _ in net])]
        odd = [o ^ g for g in group for o in offsets([z_masks[0]] + [m for _, m in net])]
        even, odd = even + [o ^ 1 for o in odd], odd + [o ^ 1 for o in even]
        units[name] = device ^ jnp.where(device & 1 == 1, jnp.array(odd), jnp.array(even))
    scale = {
        name + str(i): weights[rows, i].reshape(1, -1) for name, rows in units.items() for i in range(HALVES)
    }
    own_residual = lax.dynamic_slice_in_dim(residual, hx_index * own_count, own_count)
    wait = lax.optimization_barrier
    intra, query_weighted, scale, own_residual = wait(
        (by_neighbour(intra), by_neighbour(query_weighted), scale, own_residual)
    )

    (attn_in,) = call(
        attend_kernel,
        [shape((tok_count, heads * HS), BF16)],
        intra, query_weighted, incoming.reshape(heads, HS, HS),
    )
    projected = jnp.dot(attn_in, out_weight, preferred_element_type=F32).astype(BF16)

    def hx_send(i):
        rows = projected[i * n_hx * half_count : (i + 1) * n_hx * half_count]
        half = rows.shape[0] // 2
        return rows[:half], exchange(rows[half:], core, count)

    def hx_rest(rows, got):
        return reduce_rows(add(rows, got), hx_masks[:-1], count)

    def norm(i, rows, own_residual):
        hidden = own_residual[i * half_count : (i + 1) * half_count].astype(F32) + rows.astype(F32)
        normed = (
            hidden
            * lax.rsqrt(jnp.mean(hidden * hidden, axis=-1, keepdims=True) + 1e-06)
            * norm_gain
        ).astype(BF16)
        return hidden, normed

    def z_step(rows, mask):
        return exchange(rows, (mask, mask), count)

    def spread(unit):
        unit = gather_rows(unit, net[:-2], count)
        return [unit, exchange(unit, net[-2], count)]

    def alternate(a, b):
        blocks = [x.reshape(-1, 1, half_count, x.shape[1]) for x in (a, b)]
        return jnp.concatenate(blocks, axis=1).reshape(-1, a.shape[1])

    def joined(parts):
        return jnp.concatenate(parts, axis=0)

    def to_core(rows):
        return exchange(rows, core, count)

    def back(outs):
        mine, mine_last, other, other_last = outs
        return add(mine_last, to_core(other_last)), [mine, to_core(other)]

    def fold_sums(terms):
        half = terms[0].shape[0] // 2
        return total([t[:half] for t in terms]), total([t[half:] for t in terms]).astype(BF16)

    def fold(stays, sent, masks):
        terms = [stays, exchange(sent, masks[-1], count)]
        for mask in reversed(masks[:-1]):
            stays, sent = fold_sums(terms)
            terms = [stays, exchange(sent, mask, count)]
        return terms

    def deliver(own, across, place):
        width = own.shape[1] // n_hx

        def piece(rows, to):
            return lax.dynamic_slice_in_dim(rows, (place ^ to) * width, width, axis=1)

        group = offsets(x_masks + [1])
        sums = {to: [] for to in group}
        if across is not None:
            for to in group:
                sums[to].append(exchange(piece(across, to), (z_masks[0] ^ to,) * 2, count))
        sums[0].append(piece(own, 0))
        sums[1].append(to_core(piece(own, 1)))
        others = {to: piece(own, to) for to in group if to > 1}
        if across is not None:
            others, sums[1] = wait((others, sums[1]))
        for to, rows in others.items():
            sums[to].append(exchange(rows, (to, to), count))
        return {to: total(parts).astype(BF16) if len(parts) > 1 else parts[0] for to, parts in sums.items()}

    last = net[-1]
    rows_a, got_a = hx_send(0)
    rows_b, got_b = hx_send(1)
    a = hx_rest(rows_a, got_a)
    a, rows_b, got_b, weights_in, scale, own_residual = wait(
        (a, rows_b, got_b, (w_gate, w_up, w_down), scale, own_residual)
    )
    hidden_a, a = norm(0, a, own_residual)
    w_gate, w_up, w_down = weights_in
    weights_in, loaded = load(jnp.swapaxes(w_gate, 1, 2), jnp.swapaxes(w_up, 1, 2), w_down)
    a_z, a_own = z_step(a, z_masks[0]), spread(a)
    a, a_z, a_own, rows_b, got_b, loaded = wait((a, a_z, a_own, rows_b, got_b, loaded))
    a2 = z_step(joined([a, a_z]), z_masks[1])
    a_own = joined(a_own)
    a_own_last, a_z = exchange(a_own, last, count), spread(a_z)
    b = hx_rest(rows_b, got_b)
    a_own, a_own_last, a_z, a2, b, own_residual = wait((a_own, a_own_last, a_z, a2, b, own_residual))
    a_z = joined(a_z)
    a_z_last = exchange(a_z, last, count)
    a1 = alternate(a_own, a_z)
    a1_other = to_core(a1)
    a2 = spread(a2)
    hidden_b, b = norm(1, b, own_residual)
    b1 = jnp.concatenate([b, z_step(b, z_masks[0])], axis=0)
    a1, a_own_last, a_z_last, a1_other, a2, b1 = wait((a1, a_own_last, a_z_last, a1_other, a2, b1))
    a1_last = alternate(a_own_last, a_z_last)
    a2 = joined(a2)
    a2_last, a2_other = exchange(a2, last, count), to_core(a2)
    a1_out = expert([a1, a1_last, a1_other, to_core(a1_last)], *weights_in, loaded, scale["near0"])
    b2 = z_step(b1, z_masks[1])
    b1 = spread(b1)
    a2, a2_last, a2_other, b1, b2, a1_out = wait((a2, a2_last, a2_other, b1, b2, a1_out))
    b2 = [gather_rows(b2, net[:-2], count), z_step(b1[1], z_masks[1])]
    b1 = joined(b1)
    b1_last, b1_other = exchange(b1, last, count), to_core(b1)
    a2_out = expert([a2, a2_last, a2_other, to_core(a2_last)], *weights_in, loaded, scale["far0"])
    a1_send, a1_rest = back(a1_out)
    a2_send, a2_rest = back(a2_out)
    b1, b1_last, b1_other, b2, a1_send, a1_rest, a2_send, a2_rest = wait(
        (b1, b1_last, b1_other, b2, a1_send, a1_rest, a2_send, a2_rest)
    )
    b2_last = [exchange(b2[0], last, count), z_step(b1_last[b1_last.shape[0] // 2 :], z_masks[1])]
    b2 = joined(b2)
    b2_other = to_core(b2)
    a2_got = exchange(a2_send, last, count)
    b1_out = expert([b1, b1_last, b1_other, to_core(b1_last)], *weights_in, loaded, scale["near1"])
    b2, b2_last, b2_other, a2_got, b1_out, a1_send = wait((b2, b2_last, b2_other, a2_got, b1_out, a1_send))
    b2_last = joined(b2_last)
    steps = net[:-1]
    a1_got = exchange(a1_send, last, count)
    a2_stays, a2_sent = fold_sums(a2_rest + [a2_got])
    a2_across = z_step(a2_sent, z_masks[1])
    b2_out = expert([b2, b2_last, b2_other, to_core(b2_last)], *weights_in, loaded, scale["far1"])
    b1_send, b1_rest = back(b1_out)
    b2_send, b2_rest = back(b2_out)
    a2_stays, a2_across, a1_got, b2_send, b2_rest, b1_send, b1_rest = wait(
        (a2_stays, a2_across, a1_got, b2_send, b2_rest, b1_send, b1_rest)
    )
    for mask in reversed(steps[:-1]):
        a2_stays = total(fold(*fold_sums([a2_stays]), [mask]))
    a_z = z_step(a2_stays.astype(BF16), z_masks[1])
    half = a1_got.shape[0] // 2
    a1_sent = total([t[half:] for t in a1_rest + [a1_got]] + [a2_across]).astype(BF16)
    a1_sum = fold(total([t[:half] for t in a1_rest + [a1_got]]), a1_sent, steps)
    b2_got = exchange(b2_send, last, count)
    b2_parts = fold_sums(b2_rest + [b2_got])
    a_z, a1_sum, b2_parts, b1_send = wait((a_z, a1_sum, b2_parts, b1_send))
    half = b1_send.shape[0] // 2
    b1_got = exchange(b1_send[half:], last, count)
    b1_sent = total([t[half:] for t in b1_rest] + [b1_got]).astype(BF16)
    b1_stays = [b1_send[:half], total([t[:half] for t in b1_rest])]
    a_sum = a1_sum + [a_z]
    a_z = z_step(total([t[half_count:] for t in a_sum]).astype(BF16), z_masks[0])
    a_sum = total([t[:half_count] for t in a_sum])
    b2_sum = total(fold(*b2_parts, steps)).astype(BF16)
    a_z, a_sum, b2_sum, b1_sent, b1_stays, place = wait((a_z, a_sum, b2_sum, b1_sent, b1_stays, hx_index))
    b_z = z_step(b2_sum, z_masks[1])
    b1_got = exchange(b1_stays[0], last, count)
    a_out = total([hidden_a, a_sum, a_z]).astype(BF16)
    b1_got, a_out = wait((b1_got, a_out))
    b1_sum = fold(total([b1_stays[1], b1_got]), b1_sent, steps)
    a_out = deliver(a_out, None, place)
    b_z, b1_sum, a_out = wait((b_z, b1_sum, a_out))
    b_sum = b1_sum + [b_z]
    across = total([t[half_count:] for t in b_sum]).astype(BF16)
    b_out = deliver(total([hidden_b] + [t[:half_count] for t in b_sum]).astype(BF16), across, place)
    out = jnp.zeros((n_hx, HALVES * half_count, across.shape[1] // n_hx), BF16)
    for to in a_out:
        rows = jnp.concatenate([a_out[to], b_out[to]], axis=0)
        out = lax.dynamic_update_slice_in_dim(out, rows[None], place ^ to, axis=0)
    return out.reshape(tok_count, -1)


def solution(mesh):
    return jax.shard_map(
        shards,
        mesh=mesh,
        in_specs=(
            P("seq", "hx"),
            P("seq", "hx"),
            P("seq", "hx"),
            P("seq", "hx"),
            P("seq"),
            P("seq", None),
            P("hx", None),
            P(),
            P("seq", None),
            P("seq", None),
            P("hx", None, "seq"),
            P("hx", None, "seq"),
            P("hx", "seq", None),
        ),
        out_specs=P("seq", "hx"),
        check_vma=False,
    )
```

```python
import functools

import jax
import jax.numpy as jnp
from jax import lax
from jax.experimental import pallas as pl
from jax.experimental.pallas import tpu as pltpu
from jax.sharding import PartitionSpec as P

HS = 128
AXES = ("seq", "hx")
HALVES = 2
EXTRA = 16
VMEM_LIMIT = 16 * 1024 * 1024
F32, BF16 = jnp.float32, jnp.bfloat16


def bits(low, high):
    out = []
    bit = high // 2
    while bit >= low:
        out.append(bit)
        bit //= 2
    return out


def exchange(x, mask, count):
    even, odd = mask
    pairs = [(d, d ^ (odd if d & 1 else even)) for d in range(count)]
    return lax.ppermute(x, AXES, pairs)


def total(parts):
    return functools.reduce(lambda a, b: a + b, [p.astype(F32) for p in parts])


def add(a, b):
    return total([a, b]).astype(BF16)


def gather_rows(x, masks, count):
    for mask in masks:
        x = jnp.concatenate([x, exchange(x, mask, count)], axis=0)
    return x


def reduce_rows(x, masks, count):
    for mask in reversed(masks):
        half = x.shape[0] // 2
        x = add(x[:half], exchange(x[half:], mask, count))
    return x


def offsets(masks):
    out = [0]
    for mask in masks:
        out = out + [o ^ mask for o in out]
    return out


def split3(x):
    high = x.astype(BF16)
    rest = x - high.astype(F32)
    mid = rest.astype(BF16)
    low = (rest - mid.astype(F32)).astype(BF16)
    return [high, mid, low]


def whole():
    return pl.BlockSpec(memory_space=pltpu.VMEM)


def over_last(a, b):
    return lax.dot_general(
        a, b, (((1,), (1,)), ((), ())), precision=lax.Precision.HIGHEST, preferred_element_type=F32
    )


def by_column(decay_t, doc_row):
    tok = doc_row.shape[1]
    row = lax.broadcasted_iota(jnp.int32, (tok, tok), 0)
    col = lax.broadcasted_iota(jnp.int32, (tok, tok), 1)
    doc_rows = jnp.broadcast_to(doc_row.astype(F32), (8, tok))
    log_cum = over_last((row >= col).astype(F32), decay_t)
    return log_cum, over_last((row == col).astype(F32), doc_rows)[:, :1]


def fetch(sources, targets, sems):
    copies = [pltpu.make_async_copy(s, t, sems.at[i]) for i, (s, t) in enumerate(zip(sources, targets))]
    for copy in copies:
        copy.start()
    return copies


def state_kernel(me_ref, *refs):
    sources, out_ref, targets, sems = refs[:6], refs[6], refs[7:13], refs[13]
    decay_ref, doc_ref, ids_ref, route_ref, k_ref, v_ref = targets
    copies = fetch(sources, targets, sems)
    for copy in copies[:4]:
        copy.wait()
    heads, tok = decay_ref.shape
    chunks = out_ref.shape[0]
    chunk = out_ref.shape[1] - EXTRA
    doc_row = doc_ref[...].astype(F32)
    log_cum, doc_col = by_column(decay_ref[...], doc_row)
    total = log_cum[tok - 1 : tok, :]
    first, last = doc_row[:, :1], doc_row[:, tok - 1 :]
    end_weight = jnp.exp(total - log_cum) * (doc_col == last).astype(F32)
    through = jnp.exp(total)
    weight = jnp.sum(jnp.where(ids_ref[...] == me_ref[0], route_ref[...], 0.0), axis=0, keepdims=True)
    row = lax.broadcasted_iota(jnp.int32, (EXTRA, HS), 0)
    fixed = [jnp.broadcast_to(w.astype(F32), (EXTRA, HS)) for w in [first, last] + split3(weight)]
    per_head = chunks // heads
    for copy in copies[4:]:
        copy.wait()
    for h in range(heads):
        lanes = slice(h * HS, (h + 1) * HS)
        weighted = (k_ref[:, lanes].astype(F32) * end_weight[:, h : h + 1]).astype(BF16)
        state = lax.dot_general(
            weighted, v_ref[:, lanes], (((0,), (0,)), ((), ())), preferred_element_type=F32
        ).astype(BF16)
        parts = [
            jnp.broadcast_to(p.astype(F32), (EXTRA, HS)) for p in split3(through[:, h : h + 1])
        ] + fixed
        extra = jnp.zeros((EXTRA, HS), F32)
        for i, part in enumerate(parts):
            extra = jnp.where(row == i, part, extra)
        for j in range(per_head):
            at = h * per_head + j
            out_ref[at, :chunk, :] = state[j * chunk : (j + 1) * chunk, :]
            out_ref[at, chunk:, :] = extra.astype(BF16)


def prefix_kernel(in_ref, out_ref):
    shards_n = in_ref.shape[0]
    chunk = out_ref.shape[1]
    carry = jnp.zeros((chunk, HS), F32)
    before = None
    for s in range(shards_n):
        extra = in_ref[s, chunk:, :].astype(F32)
        decay = extra[0:1] + extra[1:2] + extra[2:3]
        first, last = extra[3:4], extra[4:5]
        if s:
            out_ref[s] = (carry * (before == first).astype(F32)).astype(BF16)
            decay = decay * (before == last).astype(F32)
        else:
            out_ref[s] = carry.astype(BF16)
        carry = decay * carry + in_ref[s, :chunk, :].astype(F32)
        before = last


def intra_kernel(*refs):
    sources, (out_ref, qw_ref), targets, sems = refs[:5], refs[5:7], refs[7:12], refs[12]
    decay_ref, doc_ref, q_ref, k_ref, v_ref = targets
    copies = fetch(sources, targets, sems)
    for copy in copies[:2]:
        copy.wait()
    heads, tok = decay_ref.shape
    doc_row = doc_ref[...].astype(F32)
    log_cum, doc_col = by_column(decay_ref[...], doc_row)
    row = lax.broadcasted_iota(jnp.int32, (tok, tok), 0)
    col = lax.broadcasted_iota(jnp.int32, (tok, tok), 1)
    log_cum_t = jnp.dot(
        decay_ref[...], (row <= col).astype(F32), precision=lax.Precision.HIGHEST, preferred_element_type=F32
    )
    allowed = (row >= col) & (doc_col == doc_row)
    carry = jnp.exp(log_cum) * (doc_col == doc_row[:, :1]).astype(F32)
    for copy in copies[2:]:
        copy.wait()
    for h in range(heads):
        lanes = slice(h * HS, (h + 1) * HS)
        scores = lax.dot_general(
            q_ref[:, lanes], k_ref[:, lanes], (((1,), (1,)), ((), ())), preferred_element_type=F32
        )
        exponent = jnp.where(allowed, log_cum[:, h : h + 1] - log_cum_t[h : h + 1, :], -jnp.inf)
        weighted = (scores * jnp.exp(exponent)).astype(BF16)
        out_ref[:, lanes] = jnp.dot(weighted, v_ref[:, lanes], preferred_element_type=F32)
        qw_ref[:, lanes] = (q_ref[:, lanes].astype(F32) * carry[:, h : h + 1]).astype(BF16)


def attend_kernel(intra_ref, qw_ref, state_ref, out_ref):
    heads = state_ref.shape[0]
    for h in range(heads):
        lanes = slice(h * HS, (h + 1) * HS)
        head_out = intra_ref[:, lanes] + jnp.dot(
            qw_ref[:, lanes], state_ref[h], preferred_element_type=F32
        )
        scale = lax.rsqrt(jnp.mean(head_out * head_out, axis=-1, keepdims=True) + 1e-05)
        out_ref[:, lanes] = (head_out * scale).astype(BF16)


def load_kernel(*refs):
    count = (len(refs) - 2) // 2
    sems = refs[-1]
    copies = [
        pltpu.make_async_copy(refs[i].at[0], refs[count + i], sems.at[i]) for i in range(count)
    ]
    for copy in copies:
        copy.start()
    for copy in copies:
        copy.wait()
    refs[2 * count][...] = jnp.zeros_like(refs[2 * count])


def load(*weights):
    shapes = [w.shape[1:] for w in weights]
    weights = [pltpu.with_memory_space_constraint(w, pltpu.HBM) for w in weights]
    *loaded, done = pl.pallas_call(
        load_kernel,
        in_specs=[pl.BlockSpec(memory_space=pltpu.HBM)] * len(weights),
        out_specs=[whole()] * (len(weights) + 1),
        out_shape=[pltpu.VMEM(s, BF16) for s in shapes] + [jax.ShapeDtypeStruct((8, 128), F32)],
        scratch_shapes=[pltpu.SemaphoreType.DMA((len(weights),))],
        compiler_params=pltpu.CompilerParams(vmem_limit_bytes=VMEM_LIMIT),
    )(*weights)
    return loaded, done


def expert_kernel(blocks, *refs):
    x_refs, (gate_ref, up_ref, down_ref, scale_ref) = refs[:blocks], refs[blocks : blocks + 4]
    out_refs, (x, act) = refs[blocks + 5 : -2], refs[-2:]
    rows, width = x_refs[0].shape
    for i, ref in enumerate(x_refs):
        x[i * rows : (i + 1) * rows, :] = ref[...]
    over_width = (((1,), (1,)), ((), ()))
    g = lax.dot_general(gate_ref[...], x[...], over_width, preferred_element_type=F32)
    u = lax.dot_general(up_ref[...], x[...], over_width, preferred_element_type=F32)
    act[...] = (g / (1.0 + jnp.exp(-g)) * u * scale_ref[...]).T.astype(BF16)
    block = min(1024, width)
    for start in range(0, width, block):
        lanes = slice(start, start + block)
        out = jnp.dot(act[...], down_ref[:, lanes], preferred_element_type=F32).astype(BF16)
        at = 0
        for ref in out_refs:
            ref[:, lanes] = out[at : at + ref.shape[0]]
            at += ref.shape[0]


def expert(xs, w_gate, w_up, w_down, loaded, scale):
    rows, width = xs[0].shape
    hidden = w_gate.shape[0]
    blocks = len(xs)
    out_rows = [rows] * blocks
    return pl.pallas_call(
        functools.partial(expert_kernel, blocks),
        in_specs=[whole()] * (blocks + 5),
        out_specs=[whole()] * len(out_rows),
        out_shape=[jax.ShapeDtypeStruct((r, width), BF16) for r in out_rows],
        scratch_shapes=[pltpu.VMEM((blocks * rows, width), BF16), pltpu.VMEM((blocks * rows, hidden), BF16)],
        compiler_params=pltpu.CompilerParams(vmem_limit_bytes=VMEM_LIMIT),
        cost_estimate=pl.CostEstimate(flops=1000, bytes_accessed=1000, transcendentals=0),
    )(*xs, w_gate, w_up, w_down, scale, loaded)


def call(kernel, out_shapes, *operands, scalars=0, far=0):
    fetched = operands[scalars : scalars + far]
    specs = [pl.BlockSpec(memory_space=pltpu.SMEM)] * scalars + [pl.BlockSpec(memory_space=pltpu.HBM)] * far
    operands = (
        operands[:scalars]
        + tuple(pltpu.with_memory_space_constraint(f, pltpu.HBM) for f in fetched)
        + operands[scalars + far :]
    )
    scratch = [pltpu.VMEM(f.shape, f.dtype) for f in fetched]
    return pl.pallas_call(
        kernel,
        in_specs=specs + [whole()] * (len(operands) - len(specs)),
        out_specs=[whole()] * len(out_shapes),
        out_shape=out_shapes,
        scratch_shapes=scratch + [pltpu.SemaphoreType.DMA((far,))] * (far > 0),
        compiler_params=pltpu.CompilerParams(vmem_limit_bytes=VMEM_LIMIT),
    )(*operands)


def shards(
    queries,
    keys,
    values,
    log_decay,
    doc_ids,
    residual,
    out_weight,
    norm_gain,
    expert_ids,
    route_weight,
    w_gate,
    w_up,
    w_down,
):
    n_seq, n_hx = lax.axis_size("seq"), lax.axis_size("hx")
    count = n_seq * n_hx
    inner = max(1, n_seq // 4)
    z_masks = bits(n_hx * inner, count)
    y_masks = bits(n_hx, n_hx * inner)
    x_masks = bits(2, n_hx)
    order_even = y_masks + x_masks
    order_odd = x_masks + y_masks if len(x_masks) == len(y_masks) else order_even
    net = list(zip(order_even, order_odd))
    core = (1, 1)
    hx_masks = [(m, m) for m in x_masks] + [core]
    hx_index = lax.axis_index("hx")
    device = lax.axis_index("seq") * n_hx + hx_index

    tok_count = queries.shape[0]
    own_count = tok_count // n_hx
    half_count = own_count // HALVES
    heads = log_decay.shape[1]
    chunk = heads * HS // n_seq

    decay_t, doc_row = log_decay.T, doc_ids.reshape(1, tok_count)
    shape = jax.ShapeDtypeStruct
    (payload,) = call(
        state_kernel,
        [shape((n_seq, chunk + EXTRA, HS), BF16)],
        hx_index.reshape(1), decay_t, doc_row, expert_ids.T, route_weight.T, keys, values,
        scalars=1, far=6,
    )
    arrived = lax.all_to_all(payload, "seq", split_axis=0, concat_axis=0, tiled=True)
    intra, query_weighted = call(
        intra_kernel,
        [shape((tok_count, heads * HS), F32), shape((tok_count, heads * HS), BF16)],
        decay_t, doc_row, queries, keys, values,
        far=5,
    )
    (incoming,) = call(prefix_kernel, [shape((n_seq, chunk, HS), BF16)], arrived)
    incoming = lax.all_to_all(incoming, "seq", split_axis=0, concat_axis=0, tiled=True)

    order = offsets([even for even, _ in hx_masks])

    def by_neighbour(x):
        blocks = [
            lax.dynamic_slice_in_dim(x, (hx_index ^ o) * own_count + i * half_count, half_count)
            for i in range(HALVES)
            for o in order
        ]
        return jnp.concatenate(blocks, axis=0)

    extra = arrived[:, chunk + 5 : chunk + 8, :].astype(F32)
    weights = jnp.sum(extra, axis=1).reshape(count, HALVES, half_count)
    units = {}
    for name, group in (("near", [0]), ("far", [z_masks[1]])):
        even = [o ^ g for g in group for o in offsets([z_masks[0]] + [m for m, _ in net])]
        odd = [o ^ g for g in group for o in offsets([z_masks[0]] + [m for _, m in net])]
        even, odd = even + [o ^ 1 for o in odd], odd + [o ^ 1 for o in even]
        units[name] = device ^ jnp.where(device & 1 == 1, jnp.array(odd), jnp.array(even))
    scale = {
        name + str(i): weights[rows, i].reshape(1, -1) for name, rows in units.items() for i in range(HALVES)
    }
    own_residual = lax.dynamic_slice_in_dim(residual, hx_index * own_count, own_count)
    wait = lax.optimization_barrier
    intra, query_weighted, scale, own_residual = wait(
        (by_neighbour(intra), by_neighbour(query_weighted), scale, own_residual)
    )

    (attn_in,) = call(
        attend_kernel,
        [shape((tok_count, heads * HS), BF16)],
        intra, query_weighted, incoming.reshape(heads, HS, HS),
    )
    projected = jnp.dot(attn_in, out_weight, preferred_element_type=F32).astype(BF16)

    def hx_send(i):
        rows = projected[i * n_hx * half_count : (i + 1) * n_hx * half_count]
        half = rows.shape[0] // 2
        return rows[:half], exchange(rows[half:], core, count)

    def hx_rest(rows, got):
        return reduce_rows(add(rows, got), hx_masks[:-1], count)

    def norm(i, rows, own_residual):
        hidden = own_residual[i * half_count : (i + 1) * half_count].astype(F32) + rows.astype(F32)
        normed = (
            hidden
            * lax.rsqrt(jnp.mean(hidden * hidden, axis=-1, keepdims=True) + 1e-06)
            * norm_gain
        ).astype(BF16)
        return hidden, normed

    def z_step(rows, mask):
        return exchange(rows, (mask, mask), count)

    def spread(unit):
        unit = gather_rows(unit, net[:-2], count)
        return [unit, exchange(unit, net[-2], count)]

    def alternate(a, b):
        blocks = [x.reshape(-1, 1, half_count, x.shape[1]) for x in (a, b)]
        return jnp.concatenate(blocks, axis=1).reshape(-1, a.shape[1])

    def joined(parts):
        return jnp.concatenate(parts, axis=0)

    def to_core(rows):
        return exchange(rows, core, count)

    def back(outs):
        mine, mine_last, other, other_last = outs
        return add(mine_last, to_core(other_last)), [mine, to_core(other)]

    def fold_sums(terms):
        half = terms[0].shape[0] // 2
        return total([t[:half] for t in terms]), total([t[half:] for t in terms]).astype(BF16)

    def fold(stays, sent, masks):
        terms = [stays, exchange(sent, masks[-1], count)]
        for mask in reversed(masks[:-1]):
            stays, sent = fold_sums(terms)
            terms = [stays, exchange(sent, mask, count)]
        return terms

    def deliver(own, across, place):
        width = own.shape[1] // n_hx

        def piece(rows, to):
            return lax.dynamic_slice_in_dim(rows, (place ^ to) * width, width, axis=1)

        group = offsets(x_masks + [1])
        sums = {to: [] for to in group}
        if across is not None:
            for to in group:
                sums[to].append(exchange(piece(across, to), (z_masks[0] ^ to,) * 2, count))
        sums[0].append(piece(own, 0))
        sums[1].append(to_core(piece(own, 1)))
        others = {to: piece(own, to) for to in group if to > 1}
        if across is not None:
            others, sums[1] = wait((others, sums[1]))
        for to, rows in others.items():
            sums[to].append(exchange(rows, (to, to), count))
        return {to: total(parts).astype(BF16) if len(parts) > 1 else parts[0] for to, parts in sums.items()}

    last = net[-1]
    rows_a, got_a = hx_send(0)
    rows_b, got_b = hx_send(1)
    a = hx_rest(rows_a, got_a)
    a, rows_b, got_b, weights_in, scale, own_residual = wait(
        (a, rows_b, got_b, (w_gate, w_up, w_down), scale, own_residual)
    )
    hidden_a, a = norm(0, a, own_residual)
    w_gate, w_up, w_down = weights_in
    weights_in, loaded = load(jnp.swapaxes(w_gate, 1, 2), jnp.swapaxes(w_up, 1, 2), w_down)
    a_z, a_own = z_step(a, z_masks[0]), spread(a)
    a, a_z, a_own, rows_b, got_b, loaded = wait((a, a_z, a_own, rows_b, got_b, loaded))
    a2 = z_step(joined([a, a_z]), z_masks[1])
    a_own = joined(a_own)
    a_own_last, a_z = exchange(a_own, last, count), spread(a_z)
    b = hx_rest(rows_b, got_b)
    a_own, a_own_last, a_z, a2, b, own_residual = wait((a_own, a_own_last, a_z, a2, b, own_residual))
    a_z = joined(a_z)
    a_z_last = exchange(a_z, last, count)
    a1 = alternate(a_own, a_z)
    a1_other = to_core(a1)
    a2 = spread(a2)
    hidden_b, b = norm(1, b, own_residual)
    b1 = jnp.concatenate([b, z_step(b, z_masks[0])], axis=0)
    a1, a_own_last, a_z_last, a1_other, a2, b1 = wait((a1, a_own_last, a_z_last, a1_other, a2, b1))
    a1_last = alternate(a_own_last, a_z_last)
    a2 = joined(a2)
    a2_last, a2_other = exchange(a2, last, count), to_core(a2)
    a1_out = expert([a1, a1_last, a1_other, to_core(a1_last)], *weights_in, loaded, scale["near0"])
    b2 = z_step(b1, z_masks[1])
    b1 = spread(b1)
    a2, a2_last, a2_other, b1, b2, a1_out = wait((a2, a2_last, a2_other, b1, b2, a1_out))
    b2 = [gather_rows(b2, net[:-2], count), z_step(b1[1], z_masks[1])]
    b1 = joined(b1)
    b1_last, b1_other = exchange(b1, last, count), to_core(b1)
    a2_out = expert([a2, a2_last, a2_other, to_core(a2_last)], *weights_in, loaded, scale["far0"])
    a1_send, a1_rest = back(a1_out)
    a2_send, a2_rest = back(a2_out)
    b1, b1_last, b1_other, b2, a1_send, a1_rest, a2_send, a2_rest = wait(
        (b1, b1_last, b1_other, b2, a1_send, a1_rest, a2_send, a2_rest)
    )
    b2_last = [exchange(b2[0], last, count), z_step(b1_last[b1_last.shape[0] // 2 :], z_masks[1])]
    b2 = joined(b2)
    b2_other = to_core(b2)
    a2_got = exchange(a2_send, last, count)
    b1_out = expert([b1, b1_last, b1_other, to_core(b1_last)], *weights_in, loaded, scale["near1"])
    b2, b2_last, b2_other, a2_got, b1_out, a1_send = wait((b2, b2_last, b2_other, a2_got, b1_out, a1_send))
    b2_last = joined(b2_last)
    steps = net[:-1]
    a1_got = exchange(a1_send, last, count)
    a2_stays, a2_sent = fold_sums(a2_rest + [a2_got])
    a2_across = z_step(a2_sent, z_masks[1])
    b2_out = expert([b2, b2_last, b2_other, to_core(b2_last)], *weights_in, loaded, scale["far1"])
    b1_send, b1_rest = back(b1_out)
    b2_send, b2_rest = back(b2_out)
    a2_stays, a2_across, a1_got, b2_send, b2_rest, b1_send, b1_rest = wait(
        (a2_stays, a2_across, a1_got, b2_send, b2_rest, b1_send, b1_rest)
    )
    for mask in reversed(steps[:-1]):
        a2_stays = total(fold(*fold_sums([a2_stays]), [mask]))
    a_z = z_step(a2_stays.astype(BF16), z_masks[1])
    half = a1_got.shape[0] // 2
    a1_sent = total([t[half:] for t in a1_rest + [a1_got]] + [a2_across]).astype(BF16)
    a1_sum = fold(total([t[:half] for t in a1_rest + [a1_got]]), a1_sent, steps)
    b2_got = exchange(b2_send, last, count)
    b2_parts = fold_sums(b2_rest + [b2_got])
    a_z, a1_sum, b2_parts, b1_send = wait((a_z, a1_sum, b2_parts, b1_send))
    half = b1_send.shape[0] // 2
    b1_got = exchange(b1_send[half:], last, count)
    b1_sent = total([t[half:] for t in b1_rest] + [b1_got]).astype(BF16)
    b1_stays = [b1_send[:half], total([t[:half] for t in b1_rest])]
    a_sum = a1_sum + [a_z]
    a_z = z_step(total([t[half_count:] for t in a_sum]).astype(BF16), z_masks[0])
    a_sum = total([t[:half_count] for t in a_sum])
    b2_sum = total(fold(*b2_parts, steps)).astype(BF16)
    a_z, a_sum, b2_sum, b1_sent, b1_stays, place = wait((a_z, a_sum, b2_sum, b1_sent, b1_stays, hx_index))
    b_z = z_step(b2_sum, z_masks[1])
    b1_got = exchange(b1_stays[0], last, count)
    a_out = total([hidden_a, a_sum, a_z]).astype(BF16)
    b1_sum = fold(total([b1_stays[1], b1_got]), b1_sent, steps)
    b_z, b1_sum, a_out = wait((b_z, b1_sum, a_out))
    b_sum = b1_sum + [b_z]
    across = total([t[half_count:] for t in b_sum]).astype(BF16)
    b_out = deliver(total([hidden_b] + [t[:half_count] for t in b_sum]).astype(BF16), across, place)
    a_out = deliver(a_out, None, place)
    out = jnp.zeros((n_hx, HALVES * half_count, across.shape[1] // n_hx), BF16)
    for to in a_out:
        rows = jnp.concatenate([a_out[to], b_out[to]], axis=0)
        out = lax.dynamic_update_slice_in_dim(out, rows[None], place ^ to, axis=0)
    return out.reshape(tok_count, -1)


def solution(mesh):
    return jax.shard_map(
        shards,
        mesh=mesh,
        in_specs=(
            P("seq", "hx"),
            P("seq", "hx"),
            P("seq", "hx"),
            P("seq", "hx"),
            P("seq"),
            P("seq", None),
            P("hx", None),
            P(),
            P("seq", None),
            P("seq", None),
            P("hx", None, "seq"),
            P("hx", None, "seq"),
            P("hx", "seq", None),
        ),
        out_specs=P("seq", "hx"),
        check_vma=False,
    )
```
